128 devices in a mesh: dp: 32 (over x, z, core), enc: 4 (over y).
Axes of the slice: x: 4, y: 4, z: 4, core: 2. Of those that a mesh axis runs over, the one named last changes fastest.
Arguments:
- text_in: bfloat16 [256, 128, 768], P(('dp', 'enc')), may hold values from -6 to 6
- cotangent: bfloat16 [256, 228, 768], P(('dp', 'enc')), may hold values from -6 to 6
- region_feats: bfloat16 [16384, 2048], P(('dp', 'enc')), may hold values from -6 to 6
- boxes: float32 [4, 16384], P(None, ('dp', 'enc')), may hold values from 0 to 1
- region_dest: int32 [16384, 1], P(('dp', 'enc')), may hold values from 0 to 7; in each aligned block of 128 rows (0 to 127, 128 to 255, ...) at most 25 rows name the same one
- weights_mat: float32 [15728640], P('dp')
- moment1_mat: float32 [15728640], P('dp')
- moment2_mat: float32 [15728640], P('dp'), as said below
- weights_small: float32 [23808], replicated
- moment1_small: float32 [23808], replicated
- moment2_small: float32 [23808], replicated, as said below
Outputs:
- hidden_out: bfloat16 [256, 228, 768], P(('dp', 'enc'))
- text_grad: float32 [256, 128, 768], P(('dp', 'enc'))
- feat_grad: float32 [16384, 2048], P(('dp', 'enc'))
- grad_norm: float32 [], replicated
- grad_mat: float32 [15728640], P('dp')
- grad_small: float32 [23808], replicated
- new_moment1_mat: float32 [15728640], P('dp')
- new_moment2_mat: float32 [15728640], P('dp')
- new_weights_mat: float32 [15728640], P('dp')
- new_weights_low: bfloat16 [15728640], P('dp')
- new_moment1_small: float32 [23808], replicated
- new_moment2_small: float32 [23808], replicated
- new_weights_small: float32 [23808], replicated
The draws below stay inside these ranges and needn't reach their ends.
Inputs may be any that keep to these rules, and one draw needn't show every extreme that they name: `region_dest`: on one device, no sequence is named by more than 25 of its region rows; on some devices one is named by exactly 25. `moment2_mat`: Positive. `moment2_small`: Positive.
All inputs are finite; a program needn't handle non-finite values.
Results may differ from the reference program's by a relative error of at most 0.025.
Values may be sent and summed in bfloat16 or wider, within the bound.
A program may use at most 256 MiB of HBM per device.

```python
import math
import jax
import jax.numpy as jnp
import numpy as np
from jax import lax

D = 768
HEADS = 12
HEAD_DIM = 64
FF = 3072
FEAT = 2048
LAYERS = 2
CAP_TOK = 128
CAPP = 25
STEP = 10
SEQ_DEV = 2
RSLOTS = 100
LEN = 228
REG_DEV = 128
SEQS = 256
REG_ROWS = 16384
P_MAT = 15728640
P_SMALL = 23808
N_ENC = 4
DEVICES = 128


def matrix_scales():
    index_pos = jnp.arange(P_MAT, dtype=jnp.int32)
    region_part = FEAT * D
    layer_size = 4 * D * D + 2 * D * FF
    within_layer = jnp.mod(index_pos - region_part, layer_size)
    scale_vec = jnp.where(within_layer < 3 * D * D, D ** (-0.5), 4.0 * D ** (-0.5))
    scale_vec = jnp.where(within_layer >= 4 * D * D, D ** (-0.5), scale_vec)
    scale_vec = jnp.where(within_layer >= 4 * D * D + D * FF, FF ** (-0.5), scale_vec)
    scale_vec = jnp.where(index_pos < region_part, FEAT ** (-0.5), scale_vec)
    return scale_vec.astype(jnp.float32)


def gradient_scale():
    return (P_MAT + P_SMALL) ** (-0.5)


def gain_mask():
    index_pos = jnp.arange(P_SMALL, dtype=jnp.int32)
    mask_vec = index_pos < D
    for layer_idx in range(LAYERS):
        base_pos = 7 * D + layer_idx * (8 * D + FF)
        mask_vec = mask_vec | (index_pos >= base_pos + 3 * D) & (index_pos < base_pos + 4 * D)
        mask_vec = mask_vec | (index_pos >= base_pos + 6 * D + FF) & (index_pos < base_pos + 7 * D + FF)
    return mask_vec


def draw_weights_mat(key, part):
    key = jax.random.fold_in(key, 11)
    return jax.random.normal(key, (P_MAT,), jnp.float32) * matrix_scales()


def draw_moment1_mat(key, part):
    key = jax.random.fold_in(key, 12)
    return jax.random.normal(key, (P_MAT,), jnp.float32) * gradient_scale()


def draw_moment2_mat(key, part):
    key = jax.random.fold_in(key, 13)
    factor_vals = jnp.exp(jax.random.uniform(key, (P_MAT,), jnp.float32, 0.0, math.log(4.0)))
    return factor_vals * gradient_scale() ** 2


def draw_weights_small(key, part):
    key = jax.random.fold_in(key, 14)
    gain_key, other_key = jax.random.split(key)
    gain_vals = jax.random.uniform(gain_key, (P_SMALL,), jnp.float32, 0.6, 1.4)
    other_vals = 0.3 * jax.random.normal(other_key, (P_SMALL,), jnp.float32)
    return jnp.where(gain_mask(), gain_vals, other_vals)


def draw_moment1_small(key, part):
    key = jax.random.fold_in(key, 15)
    return jax.random.normal(key, (P_SMALL,), jnp.float32) * (2.0 * gradient_scale())


def draw_moment2_small(key, part):
    key = jax.random.fold_in(key, 16)
    factor_vals = jnp.exp(jax.random.uniform(key, (P_SMALL,), jnp.float32, 0.0, math.log(4.0)))
    return factor_vals * (4.0 * gradient_scale() ** 2)


def level_of(key, shape, shards, low, largest):
    def one(position, shards_of):
        steps = jax.random.uniform(jax.random.fold_in(jax.random.fold_in(key, 6), position), (shards_of,), jnp.float32, low / len(shards), largest / len(shards))
        return jnp.repeat(jnp.exp(steps), shape[position] // shards_of).reshape((-1,) + (1,) * (len(shape) - position - 1))

    gain = one(*shards[0])
    for cut in shards[1:]:
        gain = gain * one(*cut)
    return gain


def deal_out(stream_key, own, number, rows, amount, top, most, lean):
    sequence = jax.random.permutation(stream_key, amount)
    heavy_load, common = shares(amount, rows * top, most, lean, True), shares(amount, rows * top, most, lean, False)
    places = jnp.arange(amount)

    def named(tallies, offset_by):
        used = int((tallies > 0).sum())
        fixed = max(1, used // 4)
        shifted = fixed + (places - fixed + offset_by * (used - fixed)) % max(1, amount - fixed)
        return jnp.zeros((amount,), jnp.int32).at[sequence[jnp.where(places < fixed, places, shifted)]].set(jnp.asarray(tallies, jnp.int32))

    tallies = jnp.where(number % 4 == 0, named(heavy_load, number // 4), named(common, number - number // 4 - 1))
    mixed = jax.random.permutation(jax.random.fold_in(own, 3), amount)
    donor, receiver = mixed[0:amount // 2 * 2:2], mixed[1:amount // 2 * 2:2]
    margin = jnp.minimum(tallies[donor] - 1, most - tallies[receiver]) // 2
    margin = jnp.where((donor == sequence[0]) | (receiver == sequence[0]) | (tallies[receiver] == 0), 0, jnp.maximum(margin, 0))
    shifted = jax.random.randint(jax.random.fold_in(own, 4), (amount // 2,), 0, 1 << 20) % (margin + 1)
    tallies = tallies.at[donor].add(-shifted).at[receiver].add(shifted)
    labels = jnp.searchsorted(jnp.cumsum(tallies), jnp.arange(rows * top), side="right").astype(jnp.int32)
    table = labels.reshape(top, rows).T
    table = table[jax.random.permutation(jax.random.fold_in(own, 1), rows)]
    offset_by = jax.random.randint(jax.random.fold_in(own, 2), (rows, 1), 0, top)
    return jnp.take_along_axis(table, (jnp.arange(top)[None, :] + offset_by) % top, axis=1)


def shares(count, total, bound, lean, full):
    loads = [(1 << 20) // math.isqrt(standing ** lean) + 1 for standing in range(1, count + 1)]
    largest = bound if full else min(bound, max(-(-total // count), total * loads[0] // sum(loads)))
    least = 1 if total - largest >= count - 1 else 0
    counts, rest = [largest] + [least] * (count - 1), total - largest - least * (count - 1)
    while rest > 0:
        free = [i for i in range(1, count) if counts[i] < largest] or [i for i in range(1, count) if counts[i] < bound]
        whole, left = sum([loads[i] for i in free]), rest
        for i in free:
            addition = min(bound - counts[i], max(1, left * loads[i] // whole), rest)
            counts[i] = counts[i] + addition
            rest = rest - addition
    return np.array(counts)


def scatter_about(key, extent, width, limit, shards=(), kind=jnp.bfloat16):
    gain = level_of(key, extent, shards, -0.22, 0.18) if shards else 1.0
    result = jax.random.normal(key, extent, jnp.float32) * width * gain
    return jnp.minimum(jnp.maximum(result, -limit), limit).astype(kind)


def setup_inputs(seed: int = 0) -> dict:
    key_list = jax.random.split(jax.random.key(seed), 12)
    text_in = scatter_about(key_list[0], (SEQS, CAP_TOK, D), 1.0, 6.0, ((0, 128),))
    cotangent = scatter_about(key_list[1], (SEQS, LEN, D), 1.0, 6.0, ((0, 128),))
    region_feats = scatter_about(key_list[2], (REG_ROWS, FEAT), 1.0, 6.0, ((0, 128),))
    boxes = jnp.clip(1.0 * jax.random.uniform(key_list[3], (4, REG_ROWS), jnp.float32) ** level_of(key_list[3], (4, REG_ROWS), ((1, 128),), -0.2, 0.2), 0.0, 1.0)
    region_dest_keys = jax.random.split(jax.random.fold_in(key_list[4], 1), REG_ROWS // REG_DEV)
    region_dest_turns = jax.random.permutation(jax.random.fold_in(key_list[4], 3), REG_ROWS // REG_DEV)
    region_dest = jax.vmap(lambda own, number: deal_out(jax.random.fold_in(key_list[4], 2), own, number, REG_DEV, N_ENC * SEQ_DEV, 1, CAPP, 1))(region_dest_keys, region_dest_turns).reshape((REG_ROWS, 1))
    weights_mat = draw_weights_mat(jax.random.fold_in(key_list[11], 71), 0)
    moment1_mat = draw_moment1_mat(jax.random.fold_in(key_list[11], 71), 0)
    moment2_mat = draw_moment2_mat(jax.random.fold_in(key_list[11], 71), 0)
    weights_small = draw_weights_small(jax.random.fold_in(key_list[11], 71), 0)
    moment1_small = draw_moment1_small(jax.random.fold_in(key_list[11], 71), 0)
    moment2_small = draw_moment2_small(jax.random.fold_in(key_list[11], 71), 0)
    return dict(text_in=text_in, cotangent=cotangent, region_feats=region_feats, boxes=boxes, region_dest=region_dest, weights_mat=weights_mat, moment1_mat=moment1_mat, moment2_mat=moment2_mat, weights_small=weights_small, moment1_small=moment1_small, moment2_small=moment2_small)


@jax.custom_vjp
def low(v):
    return lax.optimization_barrier(v.astype(jnp.bfloat16)).astype(jnp.float32)

@jax.custom_vjp
def reduced_pullback(v):
    return v

def low_keep(v):
    return (low(v), None)

def low_pass(kept, grad):
    return (grad,)

def back_keep(v):
    return (v, None)

def back_low(kept, grad):
    return (low(grad),)
low.defvjp(low_keep, low_pass)
reduced_pullback.defvjp(back_keep, back_low)
norm_eps = 1e-05
beta_one = 0.5
beta_two = 0.5
mat_rate = 0.06
small_rate = 0.4
decay_rate = 0.01
adam_eps = 1e-08
clip_norm = 1.0
masked_score = -1e+30
highest_exactness = lax.Precision.HIGHEST

def layer_norm(values, gain_vec, bias_vec):
    centre_val = values - lax.optimization_barrier(jnp.mean(values, -1, keepdims=True))
    spread_val = lax.optimization_barrier(jnp.mean(centre_val * centre_val, -1, keepdims=True))
    return centre_val * lax.rsqrt(spread_val + norm_eps) * gain_vec + bias_vec

def split_matrices(flat_vec):
    region_proj = flat_vec[:FEAT * D].reshape(FEAT, D)
    layer_list = []
    offset_pos = FEAT * D
    for layer_idx in range(LAYERS):
        query_key_value_weight = flat_vec[offset_pos:offset_pos + 3 * D * D].reshape(D, 3 * D)
        offset_pos = offset_pos + 3 * D * D
        output_weight = flat_vec[offset_pos:offset_pos + D * D].reshape(D, D)
        offset_pos = offset_pos + D * D
        up_weight = flat_vec[offset_pos:offset_pos + D * FF].reshape(D, FF)
        offset_pos = offset_pos + D * FF
        down_weight = flat_vec[offset_pos:offset_pos + FF * D].reshape(FF, D)
        offset_pos = offset_pos + FF * D
        layer_list.append((query_key_value_weight, output_weight, up_weight, down_weight))
    return (region_proj, layer_list)

def split_small(small_vec):
    emb_gain = small_vec[0:D]
    emb_bias = small_vec[D:2 * D]
    region_bias = small_vec[2 * D:3 * D]
    box_proj = small_vec[3 * D:7 * D].reshape(4, D)
    layer_small = []
    for layer_idx in range(LAYERS):
        base_pos = 7 * D + layer_idx * (8 * D + FF)
        pieces_list = []
        for start_pos, width_len in ((0, D), (D, D), (2 * D, D), (3 * D, D), (4 * D, D), (5 * D, FF), (5 * D + FF, D), (6 * D + FF, D), (7 * D + FF, D)):
            pieces_list.append(small_vec[base_pos + start_pos:base_pos + start_pos + width_len])
        layer_small.append(tuple(pieces_list))
    return (emb_gain, emb_bias, region_bias, box_proj, layer_small)

def encoder_layer(hidden, key_valid, weights, smalls):
    query_key_value_weight, output_weight, up_weight, down_weight = weights
    query_bias, value_bias, output_projection_bias, first_gain, first_bias, up_projection_bias, down_projection_bias, second_gain, second_bias = smalls
    seq_count, seq_len, width_dim = hidden.shape
    input_reduced = low(hidden)
    query_key_value_bias = jnp.concatenate([query_bias, jnp.zeros_like(query_bias), value_bias])
    query_key_value_wide = jnp.einsum('mux,xq->muq', input_reduced, query_key_value_weight, precision=highest_exactness) + query_key_value_bias
    qkv_low = low(reduced_pullback(query_key_value_wide)).reshape(seq_count, seq_len, 3, HEADS, HEAD_DIM)
    queries = qkv_low[:, :, 0]
    key_rows = qkv_low[:, :, 1]
    value_rows = qkv_low[:, :, 2]
    scale_val = 1.0 / math.sqrt(HEAD_DIM)
    scores = reduced_pullback(jnp.einsum('sqhd,skhd->shqk', queries, key_rows, precision=highest_exactness) * scale_val)
    scores = jnp.where(key_valid[:, None, None, :], scores, masked_score)
    top_score = lax.optimization_barrier(jnp.max(scores, -1, keepdims=True))
    expo_vals = jnp.exp(scores - top_score)
    prob_vals = expo_vals / lax.optimization_barrier(jnp.sum(expo_vals, -1, keepdims=True))
    prob_low = low(prob_vals)
    attended = jnp.einsum('shqk,skhd->sqhd', prob_low, value_rows, precision=highest_exactness).reshape(seq_count, seq_len, width_dim)
    attended_reduced = low(reduced_pullback(attended))
    branch_result = reduced_pullback(jnp.einsum('mux,xq->muq', attended_reduced, output_weight, precision=highest_exactness) + output_projection_bias)
    first_norm = layer_norm(hidden + branch_result, first_gain, first_bias)
    first_reduced = low(first_norm)
    up_projected = reduced_pullback(jnp.einsum('woa,av->wov', first_reduced, up_weight, precision=highest_exactness) + up_projection_bias)
    activated_reduced = low(jax.nn.gelu(up_projected))
    down_projected = reduced_pullback(jnp.einsum('tgk,ky->tgy', activated_reduced, down_weight, precision=highest_exactness) + down_projection_bias)
    return layer_norm(first_norm + down_projected, second_gain, second_bias)

def adam_update(params, first_mom, second_mom, gradient, step_rate):
    new_first = beta_one * first_mom + (1.0 - beta_one) * gradient
    new_second = beta_two * second_mom + (1.0 - beta_two) * gradient * gradient
    first_hat = new_first / (1.0 - beta_one ** STEP)
    second_hat = new_second / (1.0 - beta_two ** STEP)
    new_params = params - step_rate * (first_hat / (jnp.sqrt(second_hat) + adam_eps) + decay_rate * params)
    return (new_first, new_second, new_params)

def reference(text_in, cotangent, region_feats, boxes, region_dest, weights_mat, moment1_mat, moment2_mat, weights_small, moment1_small, moment2_small):
    group_seqs = N_ENC * SEQ_DEV
    dest_rows = region_dest[:, 0].reshape(DEVICES, REG_DEV)
    dest_hot = (dest_rows[:, :, None] == jnp.arange(group_seqs, dtype=jnp.int32)[None, None, :]).astype(jnp.int32)
    earlier = jnp.cumsum(dest_hot, axis=1) - dest_hot
    rank_row = lax.optimization_barrier(jnp.sum(earlier * dest_hot, axis=2))
    device_pos = jnp.arange(DEVICES, dtype=jnp.int32)[:, None]
    seq_global = device_pos // N_ENC * group_seqs + dest_rows
    slot_pos = device_pos % N_ENC * CAPP + rank_row
    target_rows = (seq_global * RSLOTS + slot_pos).reshape(-1).astype(jnp.int32)
    slot_valid = jnp.zeros((SEQS * RSLOTS,), jnp.float32).at[target_rows].set(1.0).reshape(SEQS, RSLOTS)
    row_valid = jnp.concatenate([jnp.ones((SEQS, CAP_TOK), jnp.float32), slot_valid], axis=1)
    block_seqs = math.gcd(SEQS, 16)
    block_count = SEQS // block_seqs
    box_rows = boxes.T

    def forward(text_vals, feat_vals, mat_vals, small_vals):
        region_proj, layer_list = split_matrices(low(mat_vals))
        emb_gain, emb_bias, region_bias, box_proj, layer_small = split_small(small_vals)
        region_emb = jnp.dot(feat_vals, region_proj, precision=highest_exactness) + region_bias + jnp.dot(box_rows, box_proj, precision=highest_exactness)
        region_low = low(reduced_pullback(region_emb))
        slotted = jnp.zeros((SEQS * RSLOTS, D), jnp.float32).at[target_rows].set(region_low).reshape(SEQS, RSLOTS, D)

        def block_fn(block_args):
            text_block, slot_block, valid_block = block_args
            hidden = layer_norm(jnp.concatenate([text_block, slot_block], axis=1), emb_gain, emb_bias)
            key_valid = valid_block > 0.5
            for layer_idx in range(LAYERS):
                hidden = encoder_layer(hidden, key_valid, layer_list[layer_idx], layer_small[layer_idx])
            return hidden * valid_block[:, :, None]
        out_blocks = lax.map(jax.checkpoint(block_fn), (text_vals.reshape(block_count, block_seqs, CAP_TOK, D), slotted.reshape(block_count, block_seqs, RSLOTS, D), row_valid.reshape(block_count, block_seqs, LEN)))
        return out_blocks.reshape(SEQS, LEN, D)
    out_vals, pullback = jax.vjp(forward, text_in.astype(jnp.float32), region_feats.astype(jnp.float32), weights_mat, weights_small)
    text_grad, feat_grad, grad_mat, grad_small = pullback(cotangent.astype(jnp.float32))
    hidden_out = out_vals.astype(jnp.bfloat16)
    grad_norm = jnp.sqrt(jnp.sum(grad_mat * grad_mat) + jnp.sum(grad_small * grad_small))
    clip_factor = clip_norm / jnp.maximum(grad_norm, clip_norm)
    new_m_mat, new_v_mat, new_w_mat = adam_update(weights_mat, moment1_mat, moment2_mat, grad_mat * clip_factor, mat_rate)
    new_m_small, new_v_small, new_w_small = adam_update(weights_small, moment1_small, moment2_small, grad_small * clip_factor, small_rate)
    return (hidden_out, text_grad, feat_grad, grad_norm, grad_mat, grad_small, new_m_mat, new_v_mat, new_w_mat, new_w_mat.astype(jnp.bfloat16), new_m_small, new_v_small, new_w_small)
```

```python
import math

import jax
import jax.numpy as jnp
from jax import lax
from jax.experimental import pallas as pl
from jax.experimental.pallas import tpu as pltpu
from jax.sharding import PartitionSpec as P

MESH = pl.DeviceIdType.MESH

D = 768
HEADS = 12
HEAD_DIM = 64
FF = 3072
FEAT = 2048
LAYERS = 2
CAP_TOK = 128
CAPP = 25
STEP = 10


norm_eps = 1e-05
beta_one = 0.5
beta_two = 0.5
mat_rate = 0.06
small_rate = 0.4
decay_rate = 0.01
adam_eps = 1e-08
clip_norm = 1.0
masked_score = -1e30
highest_exactness = lax.Precision.HIGHEST


def adam_update(params, first_mom, second_mom, gradient, step_rate):
    new_first = beta_one * first_mom + (1.0 - beta_one) * gradient
    new_second = beta_two * second_mom + (1.0 - beta_two) * gradient * gradient
    first_hat = new_first / (1.0 - beta_one**STEP)
    second_hat = new_second / (1.0 - beta_two**STEP)
    new_params = params - step_rate * (
        first_hat / (jnp.sqrt(second_hat) + adam_eps) + decay_rate * params
    )
    return (new_first, new_second, new_params)


ROWS = 512
SEQ_ROWS = 256
LEN = 228
GRAN = 128
CHUNK = 256
GRAN_QKV = (16, 88)
GRAN_OUT = (34, 106)
GRAN_UP = (40, 112)
GRAN_DOWN = (64, 136)
GRANS = 160
LAST = (((1,), (1,)), ((), ()))
FIRST = (((0,), (0,)), ((), ()))
gelu_root = math.sqrt(2.0 / math.pi)
gelu_cube = 0.044715


def is_up(gran):
    return ((gran >= GRAN_UP[0]) & (gran < GRAN_DOWN[0])) | (
        (gran >= GRAN_UP[1]) & (gran < GRAN_DOWN[1])
    )


def dot_wide(left, right, dims=None):
    if dims is None:
        return jnp.dot(left, right, preferred_element_type=jnp.float32)
    return lax.dot_general(left, right, dims, preferred_element_type=jnp.float32)


AXIS_ORDER = ((0, 1, 2), (1, 2, 0), (2, 0, 1))
HALF = 80
PIECE = 160
THIRD = 256


def place():
    dp_pos = lax.axis_index("dp")
    y_pos = lax.axis_index("enc")
    return (dp_pos // 8, (dp_pos // 2) % 4, y_pos, dp_pos % 2)


def device_at(x_pos, z_pos, y_pos, core):
    return (x_pos * 8 + z_pos * 2 + core, y_pos)


def moved(here, axis, step):
    there = list(here)
    if axis == 3:
        there[3] = 1 - here[3]
    else:
        there[axis] = (here[axis] + step) % 4
    return device_at(*there)


def greet(here):
    barrier = pltpu.get_barrier_semaphore()
    for axis, steps in ((0, (1, 2, 3)), (1, (1, 2, 3)), (2, (1, 2, 3)), (3, (1,))):
        for step in steps:
            pl.semaphore_signal(
                barrier, inc=1, device_id=moved(here, axis, step), device_id_type=MESH
            )
    pl.semaphore_wait(barrier, 10)


GATHER_ORDER = ((2, 1, 0), (0, 2, 1), (1, 0, 2))
MESH_DIMS = (0, 1, 3)


def dispatch(dest_row, target):
    earlier = lax.broadcasted_iota(jnp.int32, (128, 128), 0) < lax.broadcasted_iota(
        jnp.int32, (128, 128), 1
    )
    dest_col = jnp.broadcast_to(dest_row, (128, 128)).T
    same = earlier & (dest_col == dest_row)
    rank = jnp.sum(jnp.where(same, 1.0, 0.0), axis=0, keepdims=True).astype(jnp.int32)
    spot = rank + 32 * (dest_row & 1)
    spots = lax.broadcasted_iota(jnp.int32, (64, 128), 0)
    chosen = (spots == spot) & ((dest_row >> 1) == target)
    return jnp.where(chosen, 1.0, 0.0)


def region_loads(full_ref, region, sems):
    return [
        pltpu.make_async_copy(
            full_ref.at[third, 0, pl.ds(0, 2)],
            region.at[:, :, :, :, pl.ds(THIRD * third, THIRD)],
            sems.at[third],
        )
        for third in range(3)
    ]


def gather_kernel(
    flat_in_ref,
    feat_in_ref,
    box_in_ref,
    dest_in_ref,
    small_in_ref,
    full_ref,
    slot_out_ref,
    valid_out_ref,
    flat_ref,
    feat_ref,
    box_ref,
    dest_row_ref,
    small_ref,
    slot_ref,
    valid_ref,
    operand_sems,
    own,
    region,
    rows_out,
    valid_out,
    places,
    own_sem,
    region_sem,
    one_send,
    one_recv,
    two_send,
    two_recv,
    last_one_send,
    last_one_recv,
    last_two_send,
    last_two_recv,
    core_send,
    core_recv,
    slot_send,
    slot_recv,
):
    here = place()
    operands = [
        pltpu.make_async_copy(source, target, operand_sems.at[number])
        for number, (source, target) in enumerate(
            (
                (flat_in_ref, flat_ref),
                (dest_in_ref, dest_row_ref),
                (feat_in_ref, feat_ref),
                (box_in_ref, box_ref),
                (small_in_ref, small_ref),
            )
        )
    ]
    for copy in operands:
        copy.start()
    greet(here)
    operands[0].wait()
    first = lax.axis_index("dp") * 5
    for gran in range(5):
        up = is_up(first + gran)

        def fill(gran, dense):
            for block in range(4):
                row = GRAN * gran + 32 * block
                for col in range(6):
                    if dense:
                        rows = pl.ds(6 * GRAN * gran + 6 * 32 * block + col, 32, stride=6)
                    else:
                        rows = pl.ds(6 * GRAN * gran + 6 * block + col, 32, stride=24)
                    own[
                        col // 2, row // PIECE, pl.ds(row % PIECE, 32), pl.ds(128 * (col % 2), 128)
                    ] = flat_ref[rows, :].astype(jnp.bfloat16)

        @pl.when(up)
        def _(gran=gran):
            fill(gran, False)

        @pl.when(jnp.logical_not(up))
        def _(gran=gran):
            fill(gran, True)

    fills = [
        pltpu.make_async_copy(
            own.at[0], full_ref.at[0, here[0], here[1], here[3]], own_sem.at[0]
        )
    ]
    for part in (1, 2):
        fills.append(
            pltpu.make_async_copy(
                own.at[part, here[2]],
                full_ref.at[part, here[0], here[1], here[3], here[2]],
                own_sem.at[part],
            )
        )
    for copy in fills:
        copy.start()

    first_half, second_half, both = pl.ds(0, HALF), pl.ds(HALF, HALF), pl.ds(0, PIECE)
    halves = (first_half, second_half)
    sent = []

    def spot(part, level, target, rows, core, sub=None):
        index = [None, None, core, None]
        for step, axis in enumerate(GATHER_ORDER[part]):
            if step < level:
                value = slice(None)
            elif step == level:
                value = target
            else:
                value = here[axis]
            index[MESH_DIMS[axis]] = value
        if sub is not None:
            index[MESH_DIMS[GATHER_ORDER[part][1]]] = at_step(part, 1, sub)
        return full_ref.at[(part,) + tuple(index) + (rows, slice(None))]

    def at_step(part, level, step):
        return (here[GATHER_ORDER[part][level]] + step) % 4

    def copy_to(where, device, send_sem, recv_sem, source=None):
        return pltpu.make_async_remote_copy(
            src_ref=where if source is None else source,
            dst_ref=where,
            send_sem=send_sem,
            recv_sem=recv_sem,
            device_id=device,
            device_id_type=MESH,
        )

    def send(where, device, send_sem, recv_sem, source=None):
        copy = copy_to(where, device, send_sem, recv_sem, source)
        copy.start()
        sent.append(copy)

    def neighbour(part, level, way):
        return moved(here, GATHER_ORDER[part][level], (1, 3)[way])

    def begin(part, level, source=None):
        block = spot(part, level, at_step(part, level, 0), both, here[3])
        for way in (0, 1):
            send(
                block,
                neighbour(part, level, way),
                one_send.at[part, level, way],
                one_recv.at[part, level, way],
                source,
            )

    def relay(part, level, way):
        came = at_step(part, level, (3, 1)[way])
        copy_to(
            spot(part, level, came, both, here[3]),
            neighbour(part, level, way),
            one_send.at[part, level, way],
            one_recv.at[part, level, way],
        ).wait_recv()
        send(
            spot(part, level, came, halves[way], here[3]),
            neighbour(part, level, way),
            two_send.at[part, level, way],
            two_recv.at[part, level, way],
        )

    def finish(part, level):
        for way in (0, 1):
            copy_to(
                spot(part, level, at_step(part, level, 2), halves[way], here[3]),
                neighbour(part, level, way),
                two_send.at[part, level, way],
                two_recv.at[part, level, way],
            ).wait_recv()

    sibling = moved(here, 3, 1)

    def begin_last(part, sub, source=None):
        block = spot(part, 2, at_step(part, 2, 0), both, here[3], sub)
        for way in (0, 1):
            send(
                block,
                neighbour(part, 2, way),
                last_one_send.at[part, sub, way],
                last_one_recv.at[part, sub, way],
                source,
            )
        send(block, sibling, core_send.at[part, 16 + sub], core_recv.at[part, 16 + sub], source)

    def relay_last(part, sub):
        for way in (0, 1):
            came = at_step(part, 2, (3, 1)[way])
            block = spot(part, 2, came, both, here[3], sub)
            copy_to(
                block,
                neighbour(part, 2, way),
                last_one_send.at[part, sub, way],
                last_one_recv.at[part, sub, way],
            ).wait_recv()
            send(
                spot(part, 2, came, halves[way], here[3], sub),
                neighbour(part, 2, way),
                last_two_send.at[part, sub, way],
                last_two_recv.at[part, sub, way],
            )
            send(
                block,
                sibling,
                core_send.at[part, 4 * way + sub],
                core_recv.at[part, 4 * way + sub],
            )

    def finish_last(part, sub):
        for way in (0, 1):
            block = spot(part, 2, at_step(part, 2, 2), halves[way], here[3], sub)
            copy_to(
                block,
                neighbour(part, 2, way),
                last_two_send.at[part, sub, way],
                last_two_recv.at[part, sub, way],
            ).wait_recv()
            send(
                block,
                sibling,
                core_send.at[part, 8 + 4 * way + sub],
                core_recv.at[part, 8 + 4 * way + sub],
            )

    def await_sibling(part):
        other = 1 - here[3]

        def wait(where, number):
            copy_to(where, sibling, core_send.at[part, number], core_recv.at[part, number]).wait_recv()

        for sub in range(4):
            wait(spot(part, 2, at_step(part, 2, 0), both, other, sub), 16 + sub)
            for way in (0, 1):
                came = at_step(part, 2, (3, 1)[way])
                wait(spot(part, 2, came, both, other, sub), 4 * way + sub)
                across = spot(part, 2, at_step(part, 2, 2), halves[way], other, sub)
                wait(across, 8 + 4 * way + sub)

    begin(1, 0, own.at[1, here[2]])
    begin(2, 0, own.at[2, here[2]])
    begin(0, 1, own.at[0])
    begin_last(0, 0, own.at[0])

    def slot_copy(kind, step, source, target):
        return pltpu.make_async_remote_copy(
            src_ref=source.at[step],
            dst_ref=target.at[:, here[2]],
            send_sem=slot_send.at[kind, step],
            recv_sem=slot_recv.at[kind, step],
            device_id=moved(here, 2, step),
            device_id_type=MESH,
        )

    for copy in operands[1:]:
        copy.wait()
    for step in (1, 2, 3, 0):
        chosen = dispatch(dest_row_ref[...], (here[2] + step) % 4)
        places[step] = chosen.astype(jnp.bfloat16)
        filled = jnp.broadcast_to(jnp.sum(chosen, axis=1, keepdims=True), (64, 128))
        if step == 0:
            valid_ref[:, here[2]] = filled.reshape(2, 32, 128)
        else:
            valid_out[step] = filled.reshape(2, 32, 128)
            slot_copy(1, step, valid_out, valid_ref).start()
    for copy in fills:
        copy.wait()
    for part in (1, 2):
        relay(part, 0, 0)
        relay(part, 0, 1)
    for part in (1, 2):
        finish(part, 0)
        begin(part, 1)
        begin_last(part, 0)
    for part in range(3):
        for way in (0, 1):
            relay(part, 1, way)
            begin_last(part, (3, 1)[way])
    for part in range(3):
        relay_last(part, 0)
    for part in range(3):
        finish(part, 1)
        begin_last(part, 2)
    for sub in (3, 1, 2):
        for part in range(3):
            relay_last(part, sub)
        before = {3: 0, 1: 3, 2: 1}[sub]
        for part in range(3):
            finish_last(part, before)
    for part in range(3):
        finish_last(part, 2)
    for part in range(3):
        await_sibling(part)

    loads = region_loads(full_ref, region, region_sem)
    for copy in loads:
        copy.start()
    emb = small_ref[pl.ds(2, 1), :] + lax.dot_general(
        box_ref[...],
        small_ref[pl.ds(3, 4), :],
        FIRST,
        precision=highest_exactness,
        preferred_element_type=jnp.float32,
    )
    for copy in loads:
        copy.wait()
    matrix = region[...].reshape(16 * PIECE, D)[:FEAT]
    emb = emb + dot_wide(feat_ref[...], matrix)
    emb = emb.astype(jnp.bfloat16)
    for step in (1, 2, 3, 0):
        placed = dot_wide(places[step], emb).astype(jnp.bfloat16).reshape(2, 32, D)
        if step == 0:
            slot_ref[:, here[2]] = placed
        else:
            rows_out[step] = placed
            slot_copy(0, step, rows_out, slot_ref).start()
    slot_copies = [slot_copy(0, step, rows_out, slot_ref) for step in (1, 2, 3)]
    slot_copies += [slot_copy(1, step, valid_out, valid_ref) for step in (1, 2, 3)]
    for copy in slot_copies:
        copy.wait_recv()
    results = [
        pltpu.make_async_copy(slot_ref, slot_out_ref, operand_sems.at[5]),
        pltpu.make_async_copy(valid_ref, valid_out_ref, operand_sems.at[6]),
    ]
    for copy in results:
        copy.start()
    for copy in results:
        copy.wait()
    for copy in slot_copies:
        copy.wait_send()
    for copy in sent:
        copy.wait_send()


def gather_matrices(flat_vec, region_feats, boxes, region_dest, small_rows):
    low, wide = jnp.bfloat16, jnp.float32
    dma = pltpu.SemaphoreType.DMA
    return pl.pallas_call(
        gather_kernel,
        out_shape=(
            jax.ShapeDtypeStruct((3, 4, 4, 2, 4, PIECE, THIRD), low),
            jax.ShapeDtypeStruct((2, 4, 32, D), low),
            jax.ShapeDtypeStruct((2, 4, 32, 128), wide),
        ),
        in_specs=[pl.BlockSpec(memory_space=pl.ANY)] * 5,
        out_specs=(pl.BlockSpec(memory_space=pl.ANY),) * 3,
        scratch_shapes=[
            pltpu.VMEM((3840, 128), wide),
            pltpu.VMEM((128, FEAT), low),
            pltpu.VMEM((4, 128), wide),
            pltpu.VMEM((1, 128), jnp.int32),
            pltpu.VMEM((32, D), wide),
            pltpu.VMEM((2, 4, 32, D), low),
            pltpu.VMEM((2, 4, 32, 128), wide),
            dma((7,)),
            pltpu.VMEM((3, 4, PIECE, THIRD), low),
            pltpu.VMEM((2, 2, 4, PIECE, D), low),
            pltpu.VMEM((4, 2, 32, D), low),
            pltpu.VMEM((4, 2, 32, 128), wide),
            pltpu.VMEM((4, 64, 128), low),
            dma((3,)),
            dma((3,)),
            dma((3, 2, 2)),
            dma((3, 2, 2)),
            dma((3, 2, 2)),
            dma((3, 2, 2)),
            dma((3, 4, 2)),
            dma((3, 4, 2)),
            dma((3, 4, 2)),
            dma((3, 4, 2)),
            dma((3, 20)),
            dma((3, 20)),
            dma((2, 4)),
            dma((2, 4)),
        ],
        compiler_params=pltpu.CompilerParams(
            collective_id=1, has_side_effects=True, vmem_limit_bytes=62 * 1024 * 1024
        ),
    )(
        flat_vec.reshape(3840, 128),
        region_feats,
        boxes,
        region_dest.reshape(1, -1),
        small_rows,
    )


def normal(values):
    centre = values - jnp.mean(values, -1, keepdims=True)
    spread = lax.rsqrt(jnp.mean(centre * centre, -1, keepdims=True) + norm_eps)
    return centre * spread, spread


def layers_kernel(
    text_in_ref,
    slot_in_ref,
    valid_ref,
    cot_ref,
    small_ref,
    weight_ref,
    hidden_ref,
    text_ref,
    slot_ref,
    small_grad_ref,
    grad_ref,
    keep_act,
    keep_slope,
    keep_probs,
    keep_qkv,
    embed,
    row_mask,
    key_mask,
    spreads,
    x_wide,
    f_wide,
    x_low,
    qkv,
    att,
    mid,
    f_low,
    second,
    act,
    slope,
    probs,
    d_low,
    turned,
    w_qkv,
    w_out,
    w_up,
    w_down,
    raw,
    stage_f,
    stage_q,
    stage_r,
    load_sems,
    keep_sems,
    p_sems,
    q_sems,
    r_sems,
):
    low, wide = jnp.bfloat16, jnp.float32
    step_rows = 128

    def small_row(row):
        return small_ref[pl.ds(row, 1), :]

    def small_part(row, col):
        return small_ref[pl.ds(row, 1), pl.ds(pl.multiple_of(col * CHUNK, CHUNK), CHUNK)]

    def cols(col):
        return pl.ds(pl.multiple_of(col * CHUNK, CHUNK), CHUNK)

    def panel(third):
        return pl.ds(THIRD * third, THIRD)

    def load(which, layer):
        first, count, target, number = {
            "qkv": (GRAN_QKV[layer], 18, raw, 0),
            "out": (GRAN_OUT[layer], 6, w_out, 1),
            "down": (GRAN_DOWN[layer], 24, w_down, 2),
            "up": (GRAN_UP[layer], 24, w_up, 3),
        }[which]
        copies = []
        for third in range(3):
            if which != "up":
                copies.append(
                    pltpu.make_async_copy(
                        weight_ref.at[third, pl.ds(first, count)],
                        target.at[:, :, :, panel(third)],
                        load_sems.at[number, third],
                    )
                )
                continue
            for block in range(4):
                copies.append(
                    pltpu.make_async_copy(
                        weight_ref.at[third, pl.ds(first, count), block],
                        target.at[block, :, :, panel(third)],
                        load_sems.at[number + block, third],
                    )
                )
        return copies

    def begin(which, layer):
        for copy in load(which, layer):
            copy.start()

    def ready(which, layer):
        for copy in load(which, layer):
            copy.wait()

    keeps = {
        "act": (act, keep_act, 0),
        "slope": (slope, keep_slope, 1),
        "probs": (probs, keep_probs, 2),
        "qkv": (w_qkv, keep_qkv, 3),
    }

    def put_away(name):
        here, there, sem = keeps[name]
        return pltpu.make_async_copy(here, there, keep_sems.at[sem])

    def take_back(name):
        here, there, sem = keeps[name]
        return pltpu.make_async_copy(there, here, keep_sems.at[4 + sem])

    def norm_loop(source, layer, number, gain_row, bias_row, store):
        gain, bias = small_row(gain_row), small_row(bias_row)

        def one(step, carry):
            rows = pl.ds(pl.multiple_of(step * step_rows, step_rows), step_rows)
            if layer is None:
                scaled, spread = normal(source[rows, :].astype(wide))
            else:
                scaled, spread = normal(source[layer, rows, :])
                source[layer, rows, :] = scaled
                spreads[number, rows, :] = jnp.broadcast_to(spread, (step_rows, 128))
            store(rows, scaled * gain + bias)
            return carry

        lax.fori_loop(0, ROWS // step_rows, one, 0, unroll=True)

    def norm_back_loop(source, layer, number, gain_row, dy_of, store):
        gain = small_row(gain_row)

        def fold(values):
            return jnp.sum(values.reshape(step_rows // 8, 8, D), axis=0)

        def one(step, carry):
            rows = pl.ds(pl.multiple_of(step * step_rows, step_rows), step_rows)
            if layer is None:
                scaled, spread = normal(source[rows, :].astype(wide))
            else:
                scaled, spread = source[layer, rows, :], spreads[number, rows, :][:, :1]
            grad = dy_of(rows)
            up = grad * gain
            result = spread * (
                up
                - jnp.mean(up, -1, keepdims=True)
                - scaled * jnp.mean(up * scaled, -1, keepdims=True)
            )
            store(rows, result)
            rounded = result.astype(low).astype(wide)
            return (
                carry[0] + fold(grad * scaled),
                carry[1] + fold(grad),
                carry[2] + fold(rounded),
            )

        zero = jnp.zeros((8, D), wide)
        sums = lax.fori_loop(0, ROWS // step_rows, one, (zero, zero, zero), unroll=True)
        return [jnp.sum(value, axis=0, keepdims=True) for value in sums]

    lane = lax.broadcasted_iota(jnp.int32, (SEQ_ROWS, 128), 1)
    halves = (lane < 64, lane >= 64)

    def only(value, half):
        return jnp.where(halves[half], value, jnp.zeros_like(value))

    def stacked(value):
        return jnp.concatenate([only(value, 0), only(value, 1)], axis=0)

    def beside(value):
        return jnp.concatenate([value[:SEQ_ROWS], value[SEQ_ROWS:]], axis=1)

    for name in ("qkv", "out", "up", "down"):
        begin(name, 0)

    def slot_spots(shape, slot_axis):
        padded = lax.broadcasted_iota(jnp.int32, shape, 1 - slot_axis)
        slots = lax.broadcasted_iota(jnp.int32, shape, slot_axis)
        place_of = (padded >> 5) * CAPP + (padded & 31)
        chosen = (slots == place_of) & ((padded & 31) < CAPP)
        return jnp.where(chosen, 1.0, 0.0).astype(low)

    for seq in range(2):
        text_rows = pl.ds(seq * SEQ_ROWS, CAP_TOK)
        slot_rows = pl.ds(seq * SEQ_ROWS + CAP_TOK, CAP_TOK)
        embed[text_rows, :] = text_in_ref[seq]
        embed[slot_rows, :] = slot_in_ref[seq]
        row_mask[text_rows, :] = jnp.ones((CAP_TOK, 128), wide)
        row_mask[slot_rows, :] = valid_ref[seq]
        key_mask[seq, :, pl.ds(0, CAP_TOK)] = jnp.ones((8, CAP_TOK), wide)
        key_mask[seq, :, pl.ds(CAP_TOK, CAP_TOK)] = valid_ref[seq].T[:8]

    def first_store(rows, value):
        x_wide[rows, :] = value
        x_low[0, rows, :] = value.astype(low)

    norm_loop(embed, None, None, 0, 1, first_store)

    for layer in range(LAYERS):
        base = 7 + 12 * layer
        ready("qkv", layer)
        if layer:
            put_away("qkv").wait()
        for part in range(3):
            for col in range(6):
                stage_f[col] = raw[pl.ds(6 * part, 6), :, :, pl.ds(128 * col, 128)].reshape(
                    D, 128
                ).astype(wide)
            for block in range(3):
                for col in range(6):
                    w_qkv[pl.ds(CHUNK * part, CHUNK), pl.ds(D * block + 128 * col, 128)] = stage_f[
                        col, pl.ds(block, CHUNK, stride=3), :
                    ].astype(low)
        if layer == 0:
            begin("qkv", 1)
            put_away("qkv").start()

        def project(count, carry, layer=layer, base=base):
            block, col = count // 3, count % 3
            value = dot_wide(x_low[layer], w_qkv[:, cols(count)])
            row = jnp.where(block == 2, base + 1, base)
            bias = jnp.where(block == 1, 0.0, small_part(row, col))
            qkv[layer, block, :, cols(col)] = (value + bias).astype(low)
            return carry

        lax.fori_loop(0, 9, project, 0, unroll=9)
        if layer:
            put_away("probs").wait()

        def attend(pair, carry, layer=layer):
            lanes = pl.ds(pl.multiple_of(pair * 128, 128), 128)
            for seq in range(2):
                rows = pl.ds(seq * SEQ_ROWS, SEQ_ROWS)
                scores = dot_wide(
                    stacked(qkv[layer, 0, rows, lanes]), qkv[layer, 1, rows, lanes], LAST
                )
                scores = jnp.where(key_mask[seq, pl.ds(0, 1), :] > 0.5, scores, masked_score)
                grown = jnp.exp2(
                    (scores - jnp.max(scores, -1, keepdims=True)) * (0.125 * math.log2(math.e))
                )
                prob = (grown * (1.0 / jnp.sum(grown, -1, keepdims=True))).astype(low)
                probs[seq, pair] = prob
                total = dot_wide(beside(prob), stacked(qkv[layer, 2, rows, lanes]))
                att[layer, rows, lanes] = total.astype(low)
            return carry

        lax.fori_loop(0, 6, attend, 0, unroll=6)
        ready("out", layer)

        def project_out(col, carry, layer=layer, base=base):
            value = dot_wide(att[layer], w_out[:, :, :, cols(col)].reshape(D, CHUNK))
            mid[layer, :, cols(col)] = x_wide[:, cols(col)] + value + small_part(base + 2, col)
            return carry

        lax.fori_loop(0, 3, project_out, 0, unroll=3)
        if layer == 0:
            begin("out", 1)

        def mid_store(rows, value, layer=layer):
            f_wide[rows, :] = value
            f_low[layer, rows, :] = value.astype(low)

        norm_loop(mid, layer, 2 * layer, base + 3, base + 4, mid_store)
        ready("up", layer)
        if layer:
            put_away("act").wait()
            put_away("slope").wait()

        def widen(count, carry, layer=layer, base=base):
            block, col = count // 3, count % 3
            value = dot_wide(f_low[layer], w_up[block, :, :, cols(col)].reshape(D, CHUNK))
            value = value + small_part(base + 5 + block, col)
            square = value * value
            bent = jnp.tanh(value * (gelu_root + (gelu_root * gelu_cube) * square))
            half = 0.5 + 0.5 * bent
            result = value * half
            act[block, :, cols(col)] = result.astype(low)
            slope[block, :, cols(col)] = (
                half
                + result * (1.0 - half) * (2.0 * gelu_root + (6.0 * gelu_root * gelu_cube) * square)
            ).astype(low)
            return carry

        lax.fori_loop(0, 12, widen, 0, unroll=6)
        if layer == 0:
            begin("up", 1)
        ready("down", layer)

        def narrow(col, carry, layer=layer, base=base):
            value = f_wide[:, cols(col)] + small_part(base + 9, col)
            for block in range(4):
                value = value + dot_wide(
                    act[block], w_down[pl.ds(6 * block, 6), :, :, cols(col)].reshape(D, CHUNK)
                )
            second[layer, :, cols(col)] = value
            return carry

        lax.fori_loop(0, 3, narrow, 0, unroll=3)
        if layer == 0:
            begin("down", 1)
            for name in ("act", "slope", "probs"):
                put_away(name).start()

        def out_store(rows, value, layer=layer):
            if layer + 1 < LAYERS:
                x_wide[rows, :] = value
                x_low[layer + 1, rows, :] = value.astype(low)
            else:
                f_wide[rows, :] = value * row_mask[rows, :][:, :1]

        norm_loop(second, layer, 2 * layer + 1, base + 10, base + 11, out_store)

    take = slot_spots((LEN - CAP_TOK, CAP_TOK), 0)
    spread_out = slot_spots((CAP_TOK, LEN - CAP_TOK), 1)
    for seq in range(2):
        text_rows = pl.ds(seq * SEQ_ROWS, CAP_TOK)
        slot_rows = pl.ds(seq * SEQ_ROWS + CAP_TOK, CAP_TOK)
        hidden_ref[seq, pl.ds(0, CAP_TOK), :] = f_wide[text_rows, :].astype(low)
        hidden_ref[seq, pl.ds(CAP_TOK, LEN - CAP_TOK), :] = dot_wide(
            take, f_wide[slot_rows, :].astype(low)
        ).astype(low)
        x_wide[text_rows, :] = cot_ref[seq, pl.ds(0, CAP_TOK), :].astype(wide)
        x_wide[slot_rows, :] = (
            dot_wide(spread_out, cot_ref[seq, pl.ds(CAP_TOK, LEN - CAP_TOK), :])
            * row_mask[slot_rows, :][:, :1]
        )

    small_grad_ref[...] = jnp.zeros_like(small_grad_ref)
    counts, slots = {"p": 0, "q": 0}, {"p": 9, "q": 6}

    def panels_out(stage, index, target, sems):
        return [
            pltpu.make_async_copy(
                stage.at[index + (panel(third),)], target(third), sems.at[third]
            )
            for third in range(3)
        ]

    def stage_copies(kind, slot, target):
        if kind == "p":
            return panels_out(
                raw, (pl.ds(2 * slot, 2), slice(None), slice(None)), target, p_sems.at[slot]
            )
        return panels_out(stage_q, (slot, slice(None), slice(None)), target, q_sems.at[slot])

    def send(kind, count, value, target):
        slot = count % slots[kind]
        copies = stage_copies(kind, slot, target)

        for copy in copies:
            copy.wait()
        if kind == "p":
            raw[pl.ds(2 * slot, 2)] = value.astype(low).reshape(2, 4, 32, D)
        else:
            stage_q[slot] = value.astype(low).reshape(8, 32, D)
        for copy in copies:
            copy.start()

    def all_stages():
        copies = []
        for slot in range(slots["p"]):
            copies += stage_copies(
                "p", slot, lambda third: grad_ref.at[third, pl.ds(GRAN_DOWN[1] + 2 * slot, 2)]
            )
        for slot in range(slots["q"]):
            copies += stage_copies(
                "q",
                slot,
                lambda third: grad_ref.at[third, pl.ds(GRAN_UP[1] + 8 * (slot % 3), 8), slot // 3],
            )
        return copies + panels_out(
            stage_r,
            (slice(None), slice(None), slice(None)),
            lambda third: grad_ref.at[third, pl.ds(GRAN_QKV[1], 6)],
            r_sems,
        )

    for stage in (stage_q, stage_r):
        stage[...] = jnp.zeros_like(stage)
    for copy in all_stages():
        copy.start()

    for layer in reversed(range(LAYERS)):
        base = 7 + 12 * layer
        top = layer == LAYERS - 1

        def d_out(rows):
            return x_wide[rows, :]

        def second_back(rows, value):
            f_wide[rows, :] = value
            d_low[rows, :] = value.astype(low)

        sums = norm_back_loop(second, layer, 2 * layer + 1, base + 10, d_out, second_back)
        for row, value in zip((10, 11, 9), sums):
            small_grad_ref[pl.ds(base + row, 1), :] = value
        if not top:
            ready("down", 0)
            take_back("act").wait()
            take_back("slope").wait()
        p_first = counts["p"]

        def down_back(count, carry, layer=layer, base=base, p_first=p_first):
            block, col = count // 3, count % 3
            grad = dot_wide(act[block, :, cols(col)], d_low[...], FIRST)
            send(
                "p",
                p_first + count,
                grad,
                lambda third: grad_ref.at[third, pl.ds(GRAN_DOWN[layer] + 2 * count, 2)],
            )
            value = dot_wide(d_low[...], w_down[pl.ds(2 * count, 2)].reshape(CHUNK, D), LAST)
            rounded = (value * slope[block, :, cols(col)].astype(wide)).astype(low)
            slope[block, :, cols(col)] = rounded
            small_grad_ref[pl.ds(base + 5 + block, 1), cols(col)] = jnp.sum(
                rounded.astype(wide), axis=0, keepdims=True
            )
            return carry

        lax.fori_loop(0, 12, down_back, 0, unroll=6)
        counts["p"] += 12
        if top:
            begin("down", 0)
            take_back("act").start()
        else:
            ready("up", 0)
        turned[...] = f_low[layer].T
        q_first = counts["q"]

        def up_back(count, carry, layer=layer, q_first=q_first):
            block, part = count // 3, count % 3
            left = turned[pl.ds(pl.multiple_of(part * CHUNK, CHUNK), CHUNK), :]
            grad = dot_wide(left, slope[block])
            send(
                "q",
                q_first + count,
                grad,
                lambda third: grad_ref.at[third, pl.ds(GRAN_UP[layer] + 8 * part, 8), block],
            )
            return carry

        lax.fori_loop(0, 12, up_back, 0, unroll=6)
        counts["q"] += 12

        def first_back(part, carry):
            value = f_wide[:, cols(part)]
            for block in range(4):
                value = value + dot_wide(
                    slope[block], w_up[block, pl.ds(8 * part, 8)].reshape(CHUNK, D), LAST
                )
            f_wide[:, cols(part)] = value
            return carry

        lax.fori_loop(0, 3, first_back, 0, unroll=3)
        if top:
            begin("up", 0)
            take_back("slope").start()

        def mid_back(rows, value):
            x_wide[rows, :] = value
            d_low[rows, :] = value.astype(low)

        sums = norm_back_loop(
            mid, layer, 2 * layer, base + 3, lambda rows: f_wide[rows, :], mid_back
        )
        for row, value in zip((3, 4, 2), sums):
            small_grad_ref[pl.ds(base + row, 1), :] = value
        turned[...] = att[layer].T
        p_first = counts["p"]
        if not top:
            ready("out", 0)

        def out_back(part, carry, layer=layer, p_first=p_first):
            left = turned[pl.ds(pl.multiple_of(part * CHUNK, CHUNK), CHUNK), :]
            grad = dot_wide(left, d_low[...])
            send(
                "p",
                p_first + part,
                grad,
                lambda third: grad_ref.at[third, pl.ds(GRAN_OUT[layer] + 2 * part, 2)],
            )
            value = dot_wide(d_low[...], w_out[pl.ds(2 * part, 2)].reshape(CHUNK, D), LAST)
            att[layer, :, cols(part)] = value.astype(low)
            return carry

        lax.fori_loop(0, 3, out_back, 0, unroll=3)
        counts["p"] += 3
        if top:
            begin("out", 0)
        else:
            take_back("probs").wait()

        def attend_back(pair, carry, layer=layer):
            lanes = pl.ds(pl.multiple_of(pair * 128, 128), 128)
            for seq in range(2):
                rows = pl.ds(seq * SEQ_ROWS, SEQ_ROWS)
                query = stacked(qkv[layer, 0, rows, lanes])
                key_rows = stacked(qkv[layer, 1, rows, lanes])
                value_rows = qkv[layer, 2, rows, lanes]
                grad = stacked(att[layer, rows, lanes])
                prob = probs[seq, pair]
                d_value = dot_wide(prob, grad, FIRST)
                d_prob = dot_wide(grad, value_rows, LAST)
                prob = prob.astype(wide)
                product = d_prob * prob
                d_score = (product - prob * jnp.sum(product, -1, keepdims=True)).astype(low)
                d_query = dot_wide(beside(d_score), key_rows)
                d_key = dot_wide(d_score, query, FIRST)
                qkv[layer, 0, rows, lanes] = (d_query * 0.125).astype(low)
                qkv[layer, 1, rows, lanes] = (d_key * 0.125).astype(low)
                qkv[layer, 2, rows, lanes] = d_value.astype(low)
            return carry

        lax.fori_loop(0, 6, attend_back, 0, unroll=3)
        if top:
            take_back("probs").start()
        for block, row in ((0, 0), (2, 1)):

            def column_sum(step, carry, block=block, layer=layer):
                rows = pl.ds(pl.multiple_of(step * 64, 64), 64)
                value = qkv[layer, block, rows, :].astype(wide)
                return carry + jnp.sum(value.reshape(8, 8, D), axis=0)

            value = lax.fori_loop(0, ROWS // 64, column_sum, jnp.zeros((8, D), wide))
            small_grad_ref[pl.ds(base + row, 1), :] = jnp.sum(value, axis=0, keepdims=True)
        turned[...] = x_low[layer].T
        if not top:
            take_back("qkv").wait()

        def qkv_back(part, carry, layer=layer):
            left = turned[pl.ds(pl.multiple_of(part * CHUNK, CHUNK), CHUNK), :]
            for block in range(3):
                grad = dot_wide(left, qkv[layer, block])
                for col in range(6):
                    stage_f[col, pl.ds(block, CHUNK, stride=3), :] = grad[
                        :, 128 * col : 128 * col + 128
                    ]
            copies = panels_out(
                stage_r,
                (slice(None), slice(None), slice(None)),
                lambda third: grad_ref.at[third, pl.ds(GRAN_QKV[layer] + 6 * part, 6)],
                r_sems,
            )

            for copy in copies:
                copy.wait()
            for col in range(6):
                stage_r[:, :, :, pl.ds(128 * col, 128)] = (
                    stage_f[col].astype(low).reshape(6, 4, 32, 128)
                )
            for copy in copies:
                copy.start()
            value = x_wide[:, cols(part)]
            for block in range(3):
                value = value + dot_wide(
                    qkv[layer, block],
                    w_qkv[pl.ds(pl.multiple_of(part * CHUNK, CHUNK), CHUNK), pl.ds(D * block, D)],
                    LAST,
                )
            x_wide[:, cols(part)] = value
            return carry

        lax.fori_loop(0, 3, qkv_back, 0)
        if top:
            take_back("qkv").start()

    def embed_back(rows, value):
        x_wide[rows, :] = value

    sums = norm_back_loop(embed, None, None, 0, lambda rows: x_wide[rows, :], embed_back)
    small_grad_ref[pl.ds(0, 1), :] = sums[0]
    small_grad_ref[pl.ds(1, 1), :] = sums[1]
    for seq in range(2):
        text_ref[seq] = x_wide[pl.ds(seq * SEQ_ROWS, CAP_TOK), :]
        slot_ref[seq] = x_wide[pl.ds(seq * SEQ_ROWS + CAP_TOK, CAP_TOK), :].astype(low)
    for copy in all_stages():
        copy.wait()


def both_layers(text_in, slots, valid, cotangent, small_rows, weight_rows):
    low, wide = jnp.bfloat16, jnp.float32
    dma = pltpu.SemaphoreType.DMA
    whole = pl.BlockSpec(memory_space=pltpu.VMEM)
    remote = pl.BlockSpec(memory_space=pl.ANY)
    made = pl.pallas_call(
        layers_kernel,
        out_shape=(
            jax.ShapeDtypeStruct((2, LEN, D), low),
            jax.ShapeDtypeStruct((2, CAP_TOK, D), wide),
            jax.ShapeDtypeStruct((2, CAP_TOK, D), low),
            jax.ShapeDtypeStruct((32, D), wide),
            jax.ShapeDtypeStruct((3, GRANS, 4, 32, THIRD), low),
            jax.ShapeDtypeStruct((4, ROWS, D), low),
            jax.ShapeDtypeStruct((4, ROWS, D), low),
            jax.ShapeDtypeStruct((2, 6, 2 * SEQ_ROWS, SEQ_ROWS), low),
            jax.ShapeDtypeStruct((D, 3 * D), low),
        ),
        in_specs=[whole] * 5 + [remote],
        out_specs=(whole,) * 4 + (remote,) * 5,
        scratch_shapes=[
            pltpu.VMEM((ROWS, D), low),
            pltpu.VMEM((ROWS, 128), wide),
            pltpu.VMEM((2, 8, SEQ_ROWS), wide),
            pltpu.VMEM((2 * LAYERS, ROWS, 128), wide),
            pltpu.VMEM((ROWS, D), wide),
            pltpu.VMEM((ROWS, D), wide),
            pltpu.VMEM((LAYERS, ROWS, D), low),
            pltpu.VMEM((LAYERS, 3, ROWS, D), low),
            pltpu.VMEM((LAYERS, ROWS, D), low),
            pltpu.VMEM((LAYERS, ROWS, D), wide),
            pltpu.VMEM((LAYERS, ROWS, D), low),
            pltpu.VMEM((LAYERS, ROWS, D), wide),
            pltpu.VMEM((4, ROWS, D), low),
            pltpu.VMEM((4, ROWS, D), low),
            pltpu.VMEM((2, 6, 2 * SEQ_ROWS, SEQ_ROWS), low),
            pltpu.VMEM((ROWS, D), low),
            pltpu.VMEM((D, ROWS), low),
            pltpu.VMEM((D, 3 * D), low),
            pltpu.VMEM((6, 4, 32, D), low),
            pltpu.VMEM((4, 24, 32, D), low),
            pltpu.VMEM((24, 4, 32, D), low),
            pltpu.VMEM((18, 4, 32, D), low),
            pltpu.VMEM((6, D, 128), wide),
            pltpu.VMEM((6, 8, 32, D), low),
            pltpu.VMEM((6, 4, 32, D), low),
            dma((7, 3)),
            dma((8,)),
            dma((9, 3)),
            dma((6, 3)),
            dma((3,)),
        ],
        compiler_params=pltpu.CompilerParams(vmem_limit_bytes=62 * 1024 * 1024),
    )(
        text_in,
        slots.reshape(2, CAP_TOK, D),
        valid.reshape(2, CAP_TOK, 128),
        cotangent,
        small_rows,
        weight_rows.reshape(3, GRANS, 4, 32, THIRD),
    )
    return made[:5]


def in_plane(here, number, step):
    if number == 0:
        pos = (2 * here[2] + here[3] + step) % 8
        return device_at(here[0], here[1], pos // 2, pos % 2)
    pos = (4 * here[0] + here[1] + step) % 16
    return device_at(pos // 4, pos % 4, here[2], here[3])


def greet_planes(here):
    barrier = pltpu.get_barrier_semaphore()
    for number, count in ((0, 8), (1, 16)):
        for step in range(1, count):
            pl.semaphore_signal(
                barrier, inc=1, device_id=in_plane(here, number, step), device_id_type=MESH
            )
    pl.semaphore_wait(barrier, 22)


class Total:
    def __init__(self, here, slots, send_sems, recv_sems):
        self.here, self.slots, self.sems = here, slots, (send_sems, recv_sems)
        self.copies = {}

    def send(self, level, value=None):
        axis = (2, 1, 0, 3)[level]
        slots, own = self.slots[level], self.here[axis]
        if value is not None:
            slots[own] = value
        for step in range(1, 2 if axis == 3 else 4):
            copy = pltpu.make_async_remote_copy(
                src_ref=slots.at[own],
                dst_ref=slots.at[own],
                send_sem=self.sems[0].at[level, step],
                recv_sem=self.sems[1].at[level, step],
                device_id=moved(self.here, axis, step),
                device_id_type=MESH,
            )
            copy.start()
            self.copies[level, step] = copy

    def take(self, level):
        count = 2 if level == 3 else 4
        for step in range(1, count):
            self.copies[level, step].wait_recv()
        value = self.slots[level][0]
        for pos in range(1, count):
            value = value + self.slots[level][pos]
        return value

    def end(self):
        for copy in self.copies.values():
            copy.wait_send()


def reduce_kernel(
    grad_in_ref,
    small_ref,
    slot_ref,
    feat_ref,
    box_ref,
    dest_row_ref,
    full_ref,
    grad_ref,
    shard_ref,
    total_ref,
    square_ref,
    feat_grad_ref,
    acc,
    sibling,
    chain_one,
    fin_one,
    chain_two,
    fin_two,
    fin_three,
    shares,
    back,
    region,
    region_grad,
    flat,
    small_a,
    small_b,
    small_c,
    small_d,
    tile_a,
    tile_b,
    load_sems,
    core_send,
    core_recv,
    chain_send,
    chain_recv,
    fin_send,
    fin_recv,
    last_send,
    last_recv,
    share_send,
    share_recv,
    small_send,
    small_recv,
    tile_send,
    tile_recv,
    back_send,
    back_recv,
    region_sem,
    put_sems,
):
    low, wide = jnp.bfloat16, jnp.float32
    here = place()
    greet_planes(here)
    core = here[3]

    chains, fins = (chain_one, chain_two), (fin_one, fin_two)
    first_half, second_half, both = pl.ds(0, HALF), pl.ds(HALF, HALF), pl.ds(0, PIECE)
    halves = (first_half, second_half)

    def at_step(part, level, step):
        return (here[AXIS_ORDER[part][level]] + step) % 4

    def fixed(part, level, step, sub=None):
        index = [None] * 3
        for before in range(level):
            index[AXIS_ORDER[part][before]] = here[AXIS_ORDER[part][before]]
        index[AXIS_ORDER[part][level]] = at_step(part, level, step)
        if sub is not None:
            index[AXIS_ORDER[part][level + 1]] = at_step(part, level + 1, sub)
        return index

    def block(buffer, part, level, step, rows, sub=None):
        index = [slice(None) if value is None else value for value in fixed(part, level, step, sub)]
        return buffer.at[(part,) + tuple(index) + (rows, slice(None))]

    def grad_block(part, step, sub, which):
        index = [slice(None) if value is None else value for value in fixed(part, 0, step, sub)]
        index.insert(2, which)
        return grad_ref.at[(part,) + tuple(index) + (slice(None), slice(None))]

    order = (2, 1, 3, 0)
    loads, core_copies = {}, {}
    for sub in order:
        for step in order:
            for part in range(3):
                core_copies[part, step, sub] = pltpu.make_async_remote_copy(
                    src_ref=grad_block(part, step, sub, 1 - core),
                    dst_ref=block(sibling, part, 0, step, both, sub),
                    send_sem=core_send.at[part, step, sub],
                    recv_sem=core_recv.at[part, step, sub],
                    device_id=moved(here, 3, 1),
                    device_id_type=MESH,
                )
                loads[part, step, sub] = pltpu.make_async_copy(
                    grad_block(part, step, sub, core),
                    block(acc, part, 0, step, both, sub),
                    load_sems.at[part, step, sub],
                )

    def with_region(part, step, sub):
        if part == 0:
            return (at_step(0, 0, step) == 0) & (at_step(0, 1, sub) < 2)
        if part == 1:
            return at_step(1, 0, step) < 2
        return at_step(2, 1, sub) == 0

    def issue(sub, region_blocks=None):
        for step in order:
            for part in range(3):

                def go(part=part, step=step):
                    core_copies[part, step, sub].start()
                    loads[part, step, sub].start()

                if region_blocks is None:
                    go()
                else:
                    pl.when(with_region(part, step, sub) == region_blocks)(go)

    back_copies = []
    for step in (1, 2, 3):
        copy = pltpu.make_async_remote_copy(
            src_ref=slot_ref.at[:, (here[2] + step) % 4],
            dst_ref=back.at[here[2]],
            send_sem=back_send.at[step],
            recv_sem=back_recv.at[step],
            device_id=moved(here, 2, step),
            device_id_type=MESH,
        )
        copy.start()
        back_copies.append(copy)
    issue(2, False)
    issue(1, False)
    loaded = region_loads(full_ref, region, region_sem)
    for copy in loaded:
        copy.start()
    back[here[2]] = slot_ref[:, here[2]]
    dest_row = dest_row_ref[...]
    dest_col = jnp.broadcast_to(dest_row, (128, 128)).T
    earlier = lax.broadcasted_iota(jnp.int32, (128, 128), 1) < lax.broadcasted_iota(
        jnp.int32, (128, 128), 0
    )
    rank = jnp.sum(
        jnp.where(earlier & (dest_col == dest_row), 1.0, 0.0), axis=1, keepdims=True
    ).astype(jnp.int32)
    spots = lax.broadcasted_iota(jnp.int32, (128, 256), 1)
    chosen = jnp.where(spots == rank + 32 * dest_col[:, :1], 1.0, 0.0).astype(low)
    for copy in back_copies:
        copy.wait_recv()
    d_region = dot_wide(chosen, back[...].reshape(256, D)).astype(low)
    for part in range(8):
        value = dot_wide(feat_ref[:, pl.ds(CHUNK * part, CHUNK)], d_region, FIRST).astype(low)
        for piece in range(8):
            row = CHUNK * part + 32 * piece
            region_grad[row // PIECE, pl.ds(row % PIECE, 32), :] = value[32 * piece : 32 * piece + 32]
    puts = []
    for third in range(3):
        lanes = pl.ds(THIRD * third, THIRD)
        for shard in range(3):
            puts.append(
                pltpu.make_async_copy(
                    region_grad.at[pl.ds(4 * shard, 4), :, lanes],
                    grad_ref.at[third, 0, shard // 2, shard % 2],
                    put_sems.at[shard, third],
                )
            )
        puts.append(
            pltpu.make_async_copy(
                region_grad.at[12, pl.ds(0, GRAN), lanes],
                grad_ref.at[third, 0, 1, 1, 0, pl.ds(0, GRAN)],
                put_sems.at[3, third],
            )
        )
    for copy in puts:
        copy.start()
    d_wide = d_region.astype(wide)
    small_a[here[2]] = small_ref[...]
    small_a[here[2], pl.ds(2, 1), :] = jnp.sum(d_wide, axis=0, keepdims=True)
    small_a[here[2], pl.ds(3, 4), :] = jnp.dot(
        box_ref[...], d_wide, precision=highest_exactness, preferred_element_type=wide
    )
    for copy in puts:
        copy.wait()

    issue(2, True)
    small = Total(here, (small_a, small_b, small_c, small_d), small_send, small_recv)
    small.send(0)
    issue(1, True)

    def add_blocks(part, level, step, rows, terms, sub=None):
        index = fixed(part, level, step, sub)
        free = [axis for axis in range(3) if index[axis] is None]

        def one(count, carry):
            spot = list(index)
            if free:
                spot[free[0]] = count
            inner = (count,) if free else ()
            where = (part,) + tuple(spot) + (rows, slice(None))
            if len(terms) == 1:
                acc[where] = acc[where] + terms[0](tuple(spot), inner, rows)
                return carry
            value = acc[where].astype(wide)
            for term in terms:
                value = value + term(tuple(spot), inner, rows).astype(wide)
            acc[where] = value.astype(low)
            return carry

        if free:
            lax.fori_loop(0, 4, one, 0)
        else:
            one(0, 0)

    chain_copies, fin_copies, last_copies = {}, {}, {}

    def slot_of(level, part, way, sub):
        return (part, way) if sub is None else (part, way, sub)

    def send_chain(part, level, sub=None):
        for way in (0, 1):
            number = 0 if sub is None else sub
            copy = pltpu.make_async_remote_copy(
                src_ref=block(acc, part, level, 2, halves[way], sub),
                dst_ref=chains[level].at[slot_of(level, part, way, sub)],
                send_sem=chain_send.at[level, part, way, number],
                recv_sem=chain_recv.at[level, part, way, number],
                device_id=moved(here, AXIS_ORDER[part][level], (1, 3)[way]),
                device_id_type=MESH,
            )
            copy.start()
            chain_copies[part, level, way, sub] = copy

    def send_fin(part, level, way, half, sub=None):
        number = 0 if sub is None else sub
        count = 1 if sub is not None else 2 - level
        index = slot_of(level, part, way, sub) + (slice(None),) * count + (halves[half], slice(None))
        copy = pltpu.make_async_remote_copy(
            src_ref=block(acc, part, level, (1, 3)[way], halves[half], sub),
            dst_ref=fins[level].at[index],
            send_sem=fin_send.at[level, part, way, half, number],
            recv_sem=fin_recv.at[level, part, way, half, number],
            device_id=moved(here, AXIS_ORDER[part][level], (1, 3)[way]),
            device_id_type=MESH,
        )
        copy.start()
        fin_copies[part, level, way, half, sub] = copy

    def sibling_term(part):
        return lambda spot, inner, rows: sibling[(part,) + spot + (rows, slice(None))]

    def relay(part, level, sub=None):
        for way in (0, 1):
            chain_copies[part, level, way, sub].wait_recv()
            slot = slot_of(level, part, way, sub)
            terms = [lambda spot, inner, rows, slot=slot: chains[level][slot + inner]]
            if level == 0:
                terms.append(sibling_term(part))
            add_blocks(part, level, (1, 3)[way], halves[way], terms, sub)
            send_fin(part, level, way, way, sub)

    def finish(part, level, sub=None):
        for way in (0, 1):
            for half in (0, 1):
                fin_copies[part, level, way, half, sub].wait_recv()
        slots = [slot_of(level, part, way, sub) for way in (0, 1)]
        terms = [lambda spot, inner, rows, slot=slot: fins[level][slot + inner] for slot in slots]
        if level == 0:
            terms.append(sibling_term(part))
        add_blocks(part, level, 0, both, terms, sub)

    def gather_pair(part, step, sub, rows=None):
        loads[part, step, sub].wait()
        core_copies[part, step, sub].wait_recv()
        if rows is not None:
            add_blocks(part, 0, step, rows, [sibling_term(part)], sub)

    def second_phase(part, sub):
        finish(part, 0, sub)
        if sub == 2:
            send_chain(part, 1)
        elif sub == 1:
            send_fin(part, 1, 0, 1)
        elif sub == 3:
            send_fin(part, 1, 1, 0)

    for count, sub in enumerate(order):
        for part in range(3):
            gather_pair(part, 2, sub, both)
            send_chain(part, 0, sub)
        for step, way in ((1, 0), (3, 1)):
            for part in range(3):
                gather_pair(part, step, sub, halves[1 - way])
                send_fin(part, 0, way, 1 - way, sub)
        if count < 2:
            issue(order[count + 2])
        for part in range(3):
            gather_pair(part, 0, sub)
        for part in range(3):
            relay(part, 0, sub)
        if count:
            for part in range(3):
                second_phase(part, order[count - 1])
        if count < 3:
            small.send(count + 1, small.take(count))
        if count == 2:
            for copy in loaded:
                copy.wait()
            matrix = region[...].reshape(16 * PIECE, D)[:FEAT]
            feat_grad_ref[...] = dot_wide(d_region, matrix, LAST)
    total_ref[...] = small.take(3)
    for part in range(3):
        relay(part, 1)
    for part in range(3):
        second_phase(part, 0)
    for part in range(3):
        finish(part, 1)
        for step in (2, 1, 3):
            copy = pltpu.make_async_remote_copy(
                src_ref=block(acc, part, 2, step, both),
                dst_ref=fin_three.at[part, step],
                send_sem=last_send.at[part, step],
                recv_sem=last_recv.at[part, step],
                device_id=moved(here, AXIS_ORDER[part][2], step),
                device_id_type=MESH,
            )
            copy.start()
            last_copies[part, step] = copy
    for part in range(3):
        for step in (1, 3, 2):
            last_copies[part, step].wait_recv()
        add_blocks(
            part,
            2,
            0,
            both,
            [
                lambda spot, inner, rows, step=step: fin_three[part, step, rows, :]
                for step in (1, 2, 3)
            ],
        )

    square = jnp.zeros((8, 128), wide)
    for part in range(3):
        own = acc[part, here[0], here[1], here[2]]
        shares[here[2], part] = own
        value = own.astype(wide)
        value = value * value
        value = value.reshape(PIECE // 8, 8, THIRD)
        square = square + jnp.sum(value[:, :, :128] + value[:, :, 128:], axis=0)
    share_copies = []
    for step in (1, 2, 3):
        copy = pltpu.make_async_remote_copy(
            src_ref=shares.at[here[2]],
            dst_ref=shares.at[here[2]],
            send_sem=share_send.at[step],
            recv_sem=share_recv.at[step],
            device_id=moved(here, 2, step),
            device_id_type=MESH,
        )
        copy.start()
        share_copies.append(copy)
    tile_copies = [[], []]

    def tile_out(number, value):
        slots, own = ((tile_a, 2 * here[2] + core), (tile_b, 4 * here[0] + here[1]))[number]
        slots[own] = value
        for step in range(1, (8, 16)[number]):
            copy = pltpu.make_async_remote_copy(
                src_ref=slots.at[own],
                dst_ref=slots.at[own],
                send_sem=tile_send.at[number, step],
                recv_sem=tile_recv.at[number, step],
                device_id=in_plane(here, number, step),
                device_id_type=MESH,
            )
            copy.start()
            tile_copies[number].append(copy)

    def tile_in(number):
        for copy in tile_copies[number]:
            copy.wait_recv()
        slots = (tile_a, tile_b)[number]
        value = slots[0]
        for pos in range(1, (8, 16)[number]):
            value = value + slots[pos]
        return value

    tile_out(0, square)
    for copy in share_copies:
        copy.wait_recv()
    first = lax.axis_index("dp") * 5

    def spread_out(grans):
        for gran in grans:
            up = is_up(first + gran)

            def put(gran, dense):
                for piece in range(4):
                    quarter, spot = (4 * gran + piece) // 5, (4 * gran + piece) % 5
                    for part in range(3):
                        value = shares[quarter, part, pl.ds(32 * spot, 32), :].astype(wide)
                        for half in range(2):
                            col = 2 * part + half
                            if dense:
                                rows = pl.ds(6 * GRAN * gran + 6 * 32 * piece + col, 32, stride=6)
                            else:
                                rows = pl.ds(6 * GRAN * gran + 6 * piece + col, 32, stride=24)
                            flat[rows, :] = value[:, 128 * half : 128 * half + 128]

            @pl.when(up)
            def _(gran=gran):
                put(gran, False)

            @pl.when(jnp.logical_not(up))
            def _(gran=gran):
                put(gran, True)

    spread_out((0, 1))
    tile_out(1, tile_in(0))
    spread_out((2, 3, 4))
    shard_ref[...] = flat[...].astype(low)
    total = jnp.sum(tile_in(1), axis=0, keepdims=True)
    smalls = total_ref[...]
    smalls = jnp.sum(smalls * smalls, axis=0, keepdims=True)
    for col in range(6):
        total = total + smalls[:, 128 * col : 128 * col + 128]
    square_ref[0, 0] = jnp.sum(total)
    for copy in share_copies + back_copies:
        copy.wait_send()
    small.end()
    for copy in tile_copies[0] + tile_copies[1]:
        copy.wait_send()
    for copies in (core_copies, chain_copies, fin_copies, last_copies):
        for copy in copies.values():
            copy.wait_send()


def reduce_gradients(grad_rows, small_rows, slot_grads, region_feats, boxes, region_dest, full_low):
    low, wide = jnp.bfloat16, jnp.float32
    dma = pltpu.SemaphoreType.DMA
    whole = pl.BlockSpec(memory_space=pltpu.VMEM)
    remote = pl.BlockSpec(memory_space=pl.ANY)
    rows_shape = (3, 4, 4, 2, 4, PIECE, THIRD)
    made = pl.pallas_call(
        reduce_kernel,
        out_shape=(
            jax.ShapeDtypeStruct(rows_shape, low),
            jax.ShapeDtypeStruct((3840, 128), low),
            jax.ShapeDtypeStruct((32, D), wide),
            jax.ShapeDtypeStruct((1, 1), wide),
            jax.ShapeDtypeStruct((128, FEAT), wide),
        ),
        in_specs=[remote] + [whole] * 5 + [remote],
        out_specs=(remote, whole, whole, pl.BlockSpec(memory_space=pltpu.SMEM), whole),
        input_output_aliases={0: 0},
        scratch_shapes=[
            pltpu.VMEM((3, 4, 4, 4, PIECE, THIRD), low),
            pltpu.VMEM((3, 4, 4, 4, PIECE, THIRD), low),
            pltpu.VMEM((3, 2, 4, 4, HALF, THIRD), low),
            pltpu.VMEM((3, 2, 4, 4, PIECE, THIRD), low),
            pltpu.VMEM((3, 2, 4, HALF, THIRD), low),
            pltpu.VMEM((3, 2, 4, PIECE, THIRD), low),
            pltpu.VMEM((3, 4, PIECE, THIRD), low),
            pltpu.VMEM((4, 3, PIECE, THIRD), low),
            pltpu.VMEM((4, 2, 32, D), low),
            pltpu.VMEM((2, 2, 4, PIECE, D), low),
            pltpu.VMEM((13, PIECE, D), low),
            pltpu.VMEM((3840, 128), wide),
            pltpu.VMEM((4, 32, D), wide),
            pltpu.VMEM((4, 32, D), wide),
            pltpu.VMEM((4, 32, D), wide),
            pltpu.VMEM((2, 32, D), wide),
            pltpu.VMEM((8, 8, 128), wide),
            pltpu.VMEM((16, 8, 128), wide),
            dma((3, 4, 4)),
            dma((3, 4, 4)),
            dma((3, 4, 4)),
            dma((2, 3, 2, 4)),
            dma((2, 3, 2, 4)),
            dma((2, 3, 2, 2, 4)),
            dma((2, 3, 2, 2, 4)),
            dma((3, 4)),
            dma((3, 4)),
            dma((4,)),
            dma((4,)),
            dma((4, 4)),
            dma((4, 4)),
            dma((2, 16)),
            dma((2, 16)),
            dma((4,)),
            dma((4,)),
            dma((3,)),
            dma((4, 3)),
        ],
        compiler_params=pltpu.CompilerParams(
            collective_id=0, has_side_effects=True, vmem_limit_bytes=62 * 1024 * 1024
        ),
    )(
        grad_rows.reshape(rows_shape),
        small_rows,
        slot_grads.reshape(2, 4, 32, D),
        region_feats,
        boxes,
        region_dest.reshape(1, -1),
        full_low,
    )
    return made[1:]


def local(
    text_in,
    cotangent,
    region_feats,
    boxes,
    region_dest,
    weights_mat,
    moment1_mat,
    moment2_mat,
    weights_small,
    moment1_small,
    moment2_small,
):
    small_in = jnp.concatenate([weights_small, jnp.zeros((D,), jnp.float32)]).reshape(32, D)
    full_low, slots, slot_valid = gather_matrices(
        weights_mat, region_feats, boxes, region_dest, small_in
    )
    hidden_out, text_grad, grad_slots, small_part, mat_part = both_layers(
        text_in, slots, slot_valid, cotangent, small_in, full_low
    )
    shard_rows, small_sum, squares, feat_grad = reduce_gradients(
        mat_part, small_part, grad_slots, region_feats, boxes, region_dest, full_low
    )
    small_count = weights_small.shape[0]
    shard_grad = shard_rows.reshape(-1).astype(jnp.float32)
    small_total = small_sum.reshape(-1)[:small_count]
    grad_norm = jnp.sqrt(squares[0, 0])
    clip_factor = clip_norm / jnp.maximum(grad_norm, clip_norm)
    new_m_mat, new_v_mat, new_w_mat = adam_update(
        weights_mat, moment1_mat, moment2_mat, shard_grad * clip_factor, mat_rate
    )
    new_m_small, new_v_small, new_w_small = adam_update(
        weights_small, moment1_small, moment2_small, small_total * clip_factor, small_rate
    )
    return (
        hidden_out,
        text_grad,
        feat_grad,
        grad_norm,
        shard_grad,
        small_total,
        new_m_mat,
        new_v_mat,
        new_w_mat,
        new_w_mat.astype(jnp.bfloat16),
        new_m_small,
        new_v_small,
        new_w_small,
    )


def solution(mesh):
    return jax.shard_map(
        local,
        mesh=mesh,
        in_specs=(
            P(("dp", "enc"), None, None),
            P(("dp", "enc"), None, None),
            P(("dp", "enc"), None),
            P(None, ("dp", "enc")),
            P(("dp", "enc"), None),
            P("dp"),
            P("dp"),
            P("dp"),
            P(),
            P(),
            P(),
        ),
        out_specs=(
            P(("dp", "enc"), None, None),
            P(("dp", "enc"), None, None),
            P(("dp", "enc"), None),
            P(),
            P("dp"),
            P(),
            P("dp"),
            P("dp"),
            P("dp"),
            P("dp"),
            P(),
            P(),
            P(),
        ),
        check_vma=False,
    )
```

```python
import math

import jax
import jax.numpy as jnp
from jax import lax
from jax.experimental import pallas as pl
from jax.experimental.pallas import tpu as pltpu
from jax.sharding import PartitionSpec as P

MESH = pl.DeviceIdType.MESH

D = 768
HEADS = 12
HEAD_DIM = 64
FF = 3072
FEAT = 2048
LAYERS = 2
CAP_TOK = 128
CAPP = 25
STEP = 10


norm_eps = 1e-05
beta_one = 0.5
beta_two = 0.5
mat_rate = 0.06
small_rate = 0.4
decay_rate = 0.01
adam_eps = 1e-08
clip_norm = 1.0
masked_score = -1e30
highest_exactness = lax.Precision.HIGHEST


def adam_update(params, first_mom, second_mom, gradient, step_rate):
    new_first = beta_one * first_mom + (1.0 - beta_one) * gradient
    new_second = beta_two * second_mom + (1.0 - beta_two) * gradient * gradient
    first_hat = new_first / (1.0 - beta_one**STEP)
    second_hat = new_second / (1.0 - beta_two**STEP)
    new_params = params - step_rate * (
        first_hat / (jnp.sqrt(second_hat) + adam_eps) + decay_rate * params
    )
    return (new_first, new_second, new_params)


ROWS = 512
SEQ_ROWS = 256
LEN = 228
GRAN = 128
CHUNK = 256
GRAN_QKV = (16, 88)
GRAN_OUT = (34, 106)
GRAN_UP = (40, 112)
GRAN_DOWN = (64, 136)
GRANS = 160
LAST = (((1,), (1,)), ((), ()))
FIRST = (((0,), (0,)), ((), ()))
gelu_root = math.sqrt(2.0 / math.pi)
gelu_cube = 0.044715


def is_up(gran):
    return ((gran >= GRAN_UP[0]) & (gran < GRAN_DOWN[0])) | (
        (gran >= GRAN_UP[1]) & (gran < GRAN_DOWN[1])
    )


def dot_wide(left, right, dims=None):
    if dims is None:
        return jnp.dot(left, right, preferred_element_type=jnp.float32)
    return lax.dot_general(left, right, dims, preferred_element_type=jnp.float32)


AXIS_ORDER = ((0, 1, 2), (1, 2, 0), (2, 0, 1))
HALF = 80
PIECE = 160
THIRD = 256


def place():
    dp_pos = lax.axis_index("dp")
    y_pos = lax.axis_index("enc")
    return (dp_pos // 8, (dp_pos // 2) % 4, y_pos, dp_pos % 2)


def device_at(x_pos, z_pos, y_pos, core):
    return (x_pos * 8 + z_pos * 2 + core, y_pos)


def moved(here, axis, step):
    there = list(here)
    if axis == 3:
        there[3] = 1 - here[3]
    else:
        there[axis] = (here[axis] + step) % 4
    return device_at(*there)


def greet(here):
    barrier = pltpu.get_barrier_semaphore()
    for axis, steps in ((0, (1, 2, 3)), (1, (1, 2, 3)), (2, (1, 2, 3)), (3, (1,))):
        for step in steps:
            pl.semaphore_signal(
                barrier, inc=1, device_id=moved(here, axis, step), device_id_type=MESH
            )
    pl.semaphore_wait(barrier, 10)


GATHER_ORDER = ((2, 1, 0), (0, 2, 1), (1, 0, 2))
MESH_DIMS = (0, 1, 3)


def dispatch(dest_row, target):
    earlier = lax.broadcasted_iota(jnp.int32, (128, 128), 0) < lax.broadcasted_iota(
        jnp.int32, (128, 128), 1
    )
    dest_col = jnp.broadcast_to(dest_row, (128, 128)).T
    same = earlier & (dest_col == dest_row)
    rank = jnp.sum(jnp.where(same, 1.0, 0.0), axis=0, keepdims=True).astype(jnp.int32)
    spot = rank + 32 * (dest_row & 1)
    spots = lax.broadcasted_iota(jnp.int32, (64, 128), 0)
    chosen = (spots == spot) & ((dest_row >> 1) == target)
    return jnp.where(chosen, 1.0, 0.0)


def region_loads(full_ref, region, sems):
    return [
        pltpu.make_async_copy(
            full_ref.at[third, 0, pl.ds(0, 2)],
            region.at[:, :, :, :, pl.ds(THIRD * third, THIRD)],
            sems.at[third],
        )
        for third in range(3)
    ]


def gather_kernel(
    flat_in_ref,
    feat_in_ref,
    box_in_ref,
    dest_in_ref,
    small_in_ref,
    full_ref,
    slot_out_ref,
    valid_out_ref,
    flat_ref,
    feat_ref,
    box_ref,
    dest_row_ref,
    small_flat,
    slot_ref,
    valid_ref,
    operand_sems,
    own,
    region,
    rows_out,
    valid_out,
    places,
    own_sem,
    region_sem,
    one_send,
    one_recv,
    two_send,
    two_recv,
    last_one_send,
    last_one_recv,
    last_two_send,
    last_two_recv,
    core_send,
    core_recv,
    slot_send,
    slot_recv,
):
    here = place()
    operands = [
        pltpu.make_async_copy(source, target, operand_sems.at[number])
        for number, (source, target) in enumerate(
            (
                (flat_in_ref, flat_ref),
                (dest_in_ref, dest_row_ref),
                (feat_in_ref, feat_ref),
                (box_in_ref, box_ref),
                (small_in_ref, small_flat),
            )
        )
    ]
    for copy in operands:
        copy.start()
    greet(here)
    operands[0].wait()
    first = lax.axis_index("dp") * 5
    for gran in range(5):
        up = is_up(first + gran)

        def fill(gran, dense):
            for block in range(4):
                row = GRAN * gran + 32 * block
                for col in range(6):
                    if dense:
                        rows = pl.ds(6 * GRAN * gran + 6 * 32 * block + col, 32, stride=6)
                    else:
                        rows = pl.ds(6 * GRAN * gran + 6 * block + col, 32, stride=24)
                    own[
                        col // 2, row // PIECE, pl.ds(row % PIECE, 32), pl.ds(128 * (col % 2), 128)
                    ] = flat_ref[rows, :].astype(jnp.bfloat16)

        @pl.when(up)
        def _(gran=gran):
            fill(gran, False)

        @pl.when(jnp.logical_not(up))
        def _(gran=gran):
            fill(gran, True)

    fills = [
        pltpu.make_async_copy(
            own.at[0], full_ref.at[0, here[0], here[1], here[3]], own_sem.at[0]
        )
    ]
    for part in (1, 2):
        fills.append(
            pltpu.make_async_copy(
                own.at[part, here[2]],
                full_ref.at[part, here[0], here[1], here[3], here[2]],
                own_sem.at[part],
            )
        )
    for copy in fills:
        copy.start()

    first_half, second_half, both = pl.ds(0, HALF), pl.ds(HALF, HALF), pl.ds(0, PIECE)
    halves = (first_half, second_half)
    sent = []

    def spot(part, level, target, rows, core, sub=None):
        index = [None, None, core, None]
        for step, axis in enumerate(GATHER_ORDER[part]):
            if step < level:
                value = slice(None)
            elif step == level:
                value = target
            else:
                value = here[axis]
            index[MESH_DIMS[axis]] = value
        if sub is not None:
            index[MESH_DIMS[GATHER_ORDER[part][1]]] = at_step(part, 1, sub)
        return full_ref.at[(part,) + tuple(index) + (rows, slice(None))]

    def at_step(part, level, step):
        return (here[GATHER_ORDER[part][level]] + step) % 4

    def copy_to(where, device, send_sem, recv_sem, source=None):
        return pltpu.make_async_remote_copy(
            src_ref=where if source is None else source,
            dst_ref=where,
            send_sem=send_sem,
            recv_sem=recv_sem,
            device_id=device,
            device_id_type=MESH,
        )

    def send(where, device, send_sem, recv_sem, source=None):
        copy = copy_to(where, device, send_sem, recv_sem, source)
        copy.start()
        sent.append(copy)

    def neighbour(part, level, way):
        return moved(here, GATHER_ORDER[part][level], (1, 3)[way])

    def begin(part, level, source=None):
        block = spot(part, level, at_step(part, level, 0), both, here[3])
        for way in (0, 1):
            send(
                block,
                neighbour(part, level, way),
                one_send.at[part, level, way],
                one_recv.at[part, level, way],
                source,
            )

    def relay(part, level, way):
        came = at_step(part, level, (3, 1)[way])
        copy_to(
            spot(part, level, came, both, here[3]),
            neighbour(part, level, way),
            one_send.at[part, level, way],
            one_recv.at[part, level, way],
        ).wait_recv()
        send(
            spot(part, level, came, halves[way], here[3]),
            neighbour(part, level, way),
            two_send.at[part, level, way],
            two_recv.at[part, level, way],
        )

    def finish(part, level):
        for way in (0, 1):
            copy_to(
                spot(part, level, at_step(part, level, 2), halves[way], here[3]),
                neighbour(part, level, way),
                two_send.at[part, level, way],
                two_recv.at[part, level, way],
            ).wait_recv()

    sibling = moved(here, 3, 1)

    def begin_last(part, sub, source=None):
        block = spot(part, 2, at_step(part, 2, 0), both, here[3], sub)
        for way in (0, 1):
            send(
                block,
                neighbour(part, 2, way),
                last_one_send.at[part, sub, way],
                last_one_recv.at[part, sub, way],
                source,
            )
        send(block, sibling, core_send.at[part, 16 + sub], core_recv.at[part, 16 + sub], source)

    def relay_last(part, sub):
        for way in (0, 1):
            came = at_step(part, 2, (3, 1)[way])
            block = spot(part, 2, came, both, here[3], sub)
            copy_to(
                block,
                neighbour(part, 2, way),
                last_one_send.at[part, sub, way],
                last_one_recv.at[part, sub, way],
            ).wait_recv()
            send(
                spot(part, 2, came, halves[way], here[3], sub),
                neighbour(part, 2, way),
                last_two_send.at[part, sub, way],
                last_two_recv.at[part, sub, way],
            )
            send(
                block,
                sibling,
                core_send.at[part, 4 * way + sub],
                core_recv.at[part, 4 * way + sub],
            )

    def finish_last(part, sub):
        for way in (0, 1):
            block = spot(part, 2, at_step(part, 2, 2), halves[way], here[3], sub)
            copy_to(
                block,
                neighbour(part, 2, way),
                last_two_send.at[part, sub, way],
                last_two_recv.at[part, sub, way],
            ).wait_recv()
            send(
                block,
                sibling,
                core_send.at[part, 8 + 4 * way + sub],
                core_recv.at[part, 8 + 4 * way + sub],
            )

    def await_sibling(part):
        other = 1 - here[3]

        def wait(where, number):
            copy_to(where, sibling, core_send.at[part, number], core_recv.at[part, number]).wait_recv()

        for sub in range(4):
            wait(spot(part, 2, at_step(part, 2, 0), both, other, sub), 16 + sub)
            for way in (0, 1):
                came = at_step(part, 2, (3, 1)[way])
                wait(spot(part, 2, came, both, other, sub), 4 * way + sub)
                across = spot(part, 2, at_step(part, 2, 2), halves[way], other, sub)
                wait(across, 8 + 4 * way + sub)

    begin(1, 0, own.at[1, here[2]])
    begin(2, 0, own.at[2, here[2]])
    begin(0, 1, own.at[0])
    begin_last(0, 0, own.at[0])

    def slot_copy(kind, step, source, target):
        return pltpu.make_async_remote_copy(
            src_ref=source.at[step],
            dst_ref=target.at[:, here[2]],
            send_sem=slot_send.at[kind, step],
            recv_sem=slot_recv.at[kind, step],
            device_id=moved(here, 2, step),
            device_id_type=MESH,
        )

    for copy in operands[1:]:
        copy.wait()
    for step in (1, 2, 3, 0):
        chosen = dispatch(dest_row_ref[...], (here[2] + step) % 4)
        places[step] = chosen.astype(jnp.bfloat16)
        filled = jnp.broadcast_to(jnp.sum(chosen, axis=1, keepdims=True), (64, 128))
        if step == 0:
            valid_ref[:, here[2]] = filled.reshape(2, 32, 128)
        else:
            valid_out[step] = filled.reshape(2, 32, 128)
            slot_copy(1, step, valid_out, valid_ref).start()
    for copy in fills:
        copy.wait()
    for part in (1, 2):
        relay(part, 0, 0)
        relay(part, 0, 1)
    for part in (1, 2):
        finish(part, 0)
        begin(part, 1)
        begin_last(part, 0)
    for part in range(3):
        for way in (0, 1):
            relay(part, 1, way)
            begin_last(part, (3, 1)[way])
    for part in range(3):
        relay_last(part, 0)
    for part in range(3):
        finish(part, 1)
        begin_last(part, 2)
    for sub in (3, 1, 2):
        for part in range(3):
            relay_last(part, sub)
        before = {3: 0, 1: 3, 2: 1}[sub]
        for part in range(3):
            finish_last(part, before)
    for part in range(3):
        finish_last(part, 2)
    for part in range(3):
        await_sibling(part)

    loads = region_loads(full_ref, region, region_sem)
    for copy in loads:
        copy.start()
    region_small = jnp.concatenate(
        [small_flat[pl.ds(12 + col, 5, stride=6), :] for col in range(6)], axis=1
    )
    emb = region_small[:1] + lax.dot_general(
        box_ref[...],
        region_small[1:],
        FIRST,
        precision=highest_exactness,
        preferred_element_type=jnp.float32,
    )
    for copy in loads:
        copy.wait()
    matrix = region[...].reshape(16 * PIECE, D)[:FEAT]
    emb = emb + dot_wide(feat_ref[...], matrix)
    emb = emb.astype(jnp.bfloat16)
    for step in (2, 1, 3, 0):
        placed = dot_wide(places[step], emb).astype(jnp.bfloat16).reshape(2, 32, D)
        if step == 0:
            slot_ref[:, here[2]] = placed
        else:
            rows_out[step] = placed
            slot_copy(0, step, rows_out, slot_ref).start()
    slot_copies = [slot_copy(0, step, rows_out, slot_ref) for step in (1, 2, 3)]
    slot_copies += [slot_copy(1, step, valid_out, valid_ref) for step in (1, 2, 3)]
    for copy in slot_copies:
        copy.wait_recv()
    results = [
        pltpu.make_async_copy(slot_ref, slot_out_ref, operand_sems.at[5]),
        pltpu.make_async_copy(valid_ref, valid_out_ref, operand_sems.at[6]),
    ]
    for copy in results:
        copy.start()
    for copy in results:
        copy.wait()
    for copy in slot_copies:
        copy.wait_send()
    for copy in sent:
        copy.wait_send()


def gather_matrices(flat_vec, region_feats, boxes, region_dest, small_rows):
    low, wide = jnp.bfloat16, jnp.float32
    dma = pltpu.SemaphoreType.DMA
    return pl.pallas_call(
        gather_kernel,
        out_shape=(
            jax.ShapeDtypeStruct((3, 4, 4, 2, 4, PIECE, THIRD), low),
            jax.ShapeDtypeStruct((2, 4, 32, D), low),
            jax.ShapeDtypeStruct((2, 4, 32, 128), wide),
        ),
        in_specs=[pl.BlockSpec(memory_space=pl.ANY)] * 5,
        out_specs=(pl.BlockSpec(memory_space=pl.ANY),) * 3,
        scratch_shapes=[
            pltpu.VMEM((3840, 128), wide),
            pltpu.VMEM((128, FEAT), low),
            pltpu.VMEM((4, 128), wide),
            pltpu.VMEM((1, 128), jnp.int32),
            pltpu.VMEM((186, 128), wide),
            pltpu.VMEM((2, 4, 32, D), low),
            pltpu.VMEM((2, 4, 32, 128), wide),
            dma((7,)),
            pltpu.VMEM((3, 4, PIECE, THIRD), low),
            pltpu.VMEM((2, 2, 4, PIECE, D), low),
            pltpu.VMEM((4, 2, 32, D), low),
            pltpu.VMEM((4, 2, 32, 128), wide),
            pltpu.VMEM((4, 64, 128), low),
            dma((3,)),
            dma((3,)),
            dma((3, 2, 2)),
            dma((3, 2, 2)),
            dma((3, 2, 2)),
            dma((3, 2, 2)),
            dma((3, 4, 2)),
            dma((3, 4, 2)),
            dma((3, 4, 2)),
            dma((3, 4, 2)),
            dma((3, 20)),
            dma((3, 20)),
            dma((2, 4)),
            dma((2, 4)),
        ],
        compiler_params=pltpu.CompilerParams(
            collective_id=1, has_side_effects=True, vmem_limit_bytes=62 * 1024 * 1024
        ),
    )(
        flat_vec.reshape(3840, 128),
        region_feats,
        boxes,
        region_dest.reshape(1, -1),
        small_rows,
    )


def normal(values):
    centre = values - jnp.mean(values, -1, keepdims=True)
    spread = lax.rsqrt(jnp.mean(centre * centre, -1, keepdims=True) + norm_eps)
    return centre * spread, spread


def layers_kernel(
    text_in_ref,
    slot_in_ref,
    valid_ref,
    cot_ref,
    small_flat,
    feat_ref,
    box_ref,
    dest_row_ref,
    weight_ref,
    hidden_ref,
    text_ref,
    region_ref,
    small_grad_ref,
    grad_ref,
    keep_act,
    keep_slope,
    keep_probs,
    keep_qkv,
    embed,
    row_mask,
    key_mask,
    spreads,
    x_wide,
    f_wide,
    x_low,
    qkv,
    att,
    mid,
    f_low,
    second,
    act,
    slope,
    probs,
    d_low,
    turned,
    w_qkv,
    w_out,
    w_up,
    w_down,
    raw,
    stage_f,
    stage_q,
    stage_r,
    load_sems,
    keep_sems,
    p_sems,
    q_sems,
    r_sems,
    slots_out,
    back,
    back_send,
    back_recv,
    text_sems,
    small_ref,
):
    low, wide = jnp.bfloat16, jnp.float32
    step_rows = 128
    here = place()
    barrier = pltpu.get_barrier_semaphore()
    for step in (1, 2, 3):
        pl.semaphore_signal(
            barrier, inc=1, device_id=moved(here, 2, step), device_id_type=MESH
        )

    for col in range(6):
        small_ref[pl.ds(0, 31), pl.ds(128 * col, 128)] = small_flat[pl.ds(col, 31, stride=6), :]

    def small_row(row):
        return small_ref[pl.ds(row, 1), :]

    def small_part(row, col):
        return small_ref[pl.ds(row, 1), pl.ds(pl.multiple_of(col * CHUNK, CHUNK), CHUNK)]

    def cols(col):
        return pl.ds(pl.multiple_of(col * CHUNK, CHUNK), CHUNK)

    def panel(third):
        return pl.ds(THIRD * third, THIRD)

    def load(which, layer):
        first, count, target, number = {
            "qkv": (GRAN_QKV[layer], 18, raw, 0),
            "out": (GRAN_OUT[layer], 6, w_out, 1),
            "down": (GRAN_DOWN[layer], 24, w_down, 2),
            "up": (GRAN_UP[layer], 24, w_up, 3),
        }[which]
        copies = []
        for third in range(3):
            if which != "up":
                copies.append(
                    pltpu.make_async_copy(
                        weight_ref.at[third, pl.ds(first, count)],
                        target.at[:, :, :, panel(third)],
                        load_sems.at[number, third],
                    )
                )
                continue
            for block in range(4):
                copies.append(
                    pltpu.make_async_copy(
                        weight_ref.at[third, pl.ds(first, count), block],
                        target.at[block, :, :, panel(third)],
                        load_sems.at[number + block, third],
                    )
                )
        return copies

    def begin(which, layer):
        for copy in load(which, layer):
            copy.start()

    def ready(which, layer):
        for copy in load(which, layer):
            copy.wait()

    keeps = {
        "act": (act, keep_act, 0),
        "slope": (slope, keep_slope, 1),
        "probs": (probs, keep_probs, 2),
        "qkv": (w_qkv, keep_qkv, 3),
    }

    def put_away(name):
        here, there, sem = keeps[name]
        return pltpu.make_async_copy(here, there, keep_sems.at[sem])

    def take_back(name):
        here, there, sem = keeps[name]
        return pltpu.make_async_copy(there, here, keep_sems.at[4 + sem])

    def norm_loop(source, layer, number, gain_row, bias_row, store):
        gain, bias = small_row(gain_row), small_row(bias_row)

        def one(step, carry):
            rows = pl.ds(pl.multiple_of(step * step_rows, step_rows), step_rows)
            if layer is None:
                scaled, spread = normal(source[rows, :].astype(wide))
            else:
                scaled, spread = normal(source[layer, rows, :])
                source[layer, rows, :] = scaled
                spreads[number, rows, :] = jnp.broadcast_to(spread, (step_rows, 128))
            store(rows, scaled * gain + bias)
            return carry

        lax.fori_loop(0, ROWS // step_rows, one, 0, unroll=True)

    def norm_back_loop(source, layer, number, gain_row, dy_of, store):
        gain = small_row(gain_row)

        def fold(values):
            return jnp.sum(values.reshape(step_rows // 8, 8, D), axis=0)

        def one(step, carry):
            rows = pl.ds(pl.multiple_of(step * step_rows, step_rows), step_rows)
            if layer is None:
                scaled, spread = normal(source[rows, :].astype(wide))
            else:
                scaled, spread = source[layer, rows, :], spreads[number, rows, :][:, :1]
            grad = dy_of(rows)
            up = grad * gain
            result = spread * (
                up
                - jnp.mean(up, -1, keepdims=True)
                - scaled * jnp.mean(up * scaled, -1, keepdims=True)
            )
            store(rows, result)
            rounded = result.astype(low).astype(wide)
            return (
                carry[0] + fold(grad * scaled),
                carry[1] + fold(grad),
                carry[2] + fold(rounded),
            )

        zero = jnp.zeros((8, D), wide)
        sums = lax.fori_loop(0, ROWS // step_rows, one, (zero, zero, zero), unroll=True)
        return [jnp.sum(value, axis=0, keepdims=True) for value in sums]

    lane = lax.broadcasted_iota(jnp.int32, (SEQ_ROWS, 128), 1)
    halves = (lane < 64, lane >= 64)

    def only(value, half):
        return jnp.where(halves[half], value, jnp.zeros_like(value))

    def stacked(value):
        return jnp.concatenate([only(value, 0), only(value, 1)], axis=0)

    def beside(value):
        return jnp.concatenate([value[:SEQ_ROWS], value[SEQ_ROWS:]], axis=1)

    for name in ("qkv", "out", "up", "down"):
        begin(name, 0)

    def slot_spots(shape, slot_axis):
        padded = lax.broadcasted_iota(jnp.int32, shape, 1 - slot_axis)
        slots = lax.broadcasted_iota(jnp.int32, shape, slot_axis)
        place_of = (padded >> 5) * CAPP + (padded & 31)
        chosen = (slots == place_of) & ((padded & 31) < CAPP)
        return jnp.where(chosen, 1.0, 0.0).astype(low)

    for seq in range(2):
        text_rows = pl.ds(seq * SEQ_ROWS, CAP_TOK)
        slot_rows = pl.ds(seq * SEQ_ROWS + CAP_TOK, CAP_TOK)
        embed[text_rows, :] = text_in_ref[seq]
        embed[slot_rows, :] = slot_in_ref[seq]
        row_mask[text_rows, :] = jnp.ones((CAP_TOK, 128), wide)
        row_mask[slot_rows, :] = valid_ref[seq]
        key_mask[seq, :, pl.ds(0, CAP_TOK)] = jnp.ones((8, CAP_TOK), wide)
        key_mask[seq, :, pl.ds(CAP_TOK, CAP_TOK)] = valid_ref[seq].T[:8]

    def first_store(rows, value):
        x_wide[rows, :] = value
        x_low[0, rows, :] = value.astype(low)

    norm_loop(embed, None, None, 0, 1, first_store)

    for layer in range(LAYERS):
        base = 7 + 12 * layer
        ready("qkv", layer)
        if layer:
            put_away("qkv").wait()
        for part in range(3):
            for col in range(6):
                stage_f[col] = raw[pl.ds(6 * part, 6), :, :, pl.ds(128 * col, 128)].reshape(
                    D, 128
                ).astype(wide)
            for block in range(3):
                for col in range(6):
                    w_qkv[pl.ds(CHUNK * part, CHUNK), pl.ds(D * block + 128 * col, 128)] = stage_f[
                        col, pl.ds(block, CHUNK, stride=3), :
                    ].astype(low)
        if layer == 0:
            begin("qkv", 1)
            put_away("qkv").start()

        def project(count, carry, layer=layer, base=base):
            block, col = count // 3, count % 3
            value = dot_wide(x_low[layer], w_qkv[:, cols(count)])
            row = jnp.where(block == 2, base + 1, base)
            bias = jnp.where(block == 1, 0.0, small_part(row, col))
            qkv[layer, block, :, cols(col)] = (value + bias).astype(low)
            return carry

        lax.fori_loop(0, 9, project, 0, unroll=9)
        if layer:
            put_away("probs").wait()

        def attend(pair, carry, layer=layer):
            lanes = pl.ds(pl.multiple_of(pair * 128, 128), 128)
            for seq in range(2):
                rows = pl.ds(seq * SEQ_ROWS, SEQ_ROWS)
                scores = dot_wide(
                    stacked(qkv[layer, 0, rows, lanes]), qkv[layer, 1, rows, lanes], LAST
                )
                scores = jnp.where(key_mask[seq, pl.ds(0, 1), :] > 0.5, scores, masked_score)
                grown = jnp.exp2(
                    (scores - jnp.max(scores, -1, keepdims=True)) * (0.125 * math.log2(math.e))
                )
                prob = (grown * (1.0 / jnp.sum(grown, -1, keepdims=True))).astype(low)
                probs[seq, pair] = prob
                total = dot_wide(beside(prob), stacked(qkv[layer, 2, rows, lanes]))
                att[layer, rows, lanes] = total.astype(low)
            return carry

        lax.fori_loop(0, 6, attend, 0, unroll=6)
        ready("out", layer)

        def project_out(col, carry, layer=layer, base=base):
            value = dot_wide(att[layer], w_out[:, :, :, cols(col)].reshape(D, CHUNK))
            mid[layer, :, cols(col)] = x_wide[:, cols(col)] + value + small_part(base + 2, col)
            return carry

        lax.fori_loop(0, 3, project_out, 0, unroll=3)
        if layer == 0:
            begin("out", 1)

        def mid_store(rows, value, layer=layer):
            f_wide[rows, :] = value
            f_low[layer, rows, :] = value.astype(low)

        norm_loop(mid, layer, 2 * layer, base + 3, base + 4, mid_store)
        ready("up", layer)
        if layer:
            put_away("act").wait()
            put_away("slope").wait()

        def widen(count, carry, layer=layer, base=base):
            block, col = count // 3, count % 3
            value = dot_wide(f_low[layer], w_up[block, :, :, cols(col)].reshape(D, CHUNK))
            value = value + small_part(base + 5 + block, col)
            square = value * value
            bent = jnp.tanh(value * (gelu_root + (gelu_root * gelu_cube) * square))
            half = 0.5 + 0.5 * bent
            result = value * half
            act[block, :, cols(col)] = result.astype(low)
            slope[block, :, cols(col)] = (
                half
                + result * (1.0 - half) * (2.0 * gelu_root + (6.0 * gelu_root * gelu_cube) * square)
            ).astype(low)
            return carry

        lax.fori_loop(0, 12, widen, 0, unroll=6)
        if layer == 0:
            begin("up", 1)
        ready("down", layer)

        def narrow(col, carry, layer=layer, base=base):
            value = f_wide[:, cols(col)] + small_part(base + 9, col)
            for block in range(4):
                value = value + dot_wide(
                    act[block], w_down[pl.ds(6 * block, 6), :, :, cols(col)].reshape(D, CHUNK)
                )
            second[layer, :, cols(col)] = value
            return carry

        lax.fori_loop(0, 3, narrow, 0, unroll=3)
        if layer == 0:
            begin("down", 1)
            for name in ("act", "slope", "probs"):
                put_away(name).start()

        def out_store(rows, value, layer=layer):
            if layer + 1 < LAYERS:
                x_wide[rows, :] = value
                x_low[layer + 1, rows, :] = value.astype(low)
            else:
                f_wide[rows, :] = value * row_mask[rows, :][:, :1]

        norm_loop(second, layer, 2 * layer + 1, base + 10, base + 11, out_store)

    take = slot_spots((LEN - CAP_TOK, CAP_TOK), 0)
    spread_out = slot_spots((CAP_TOK, LEN - CAP_TOK), 1)
    for seq in range(2):
        text_rows = pl.ds(seq * SEQ_ROWS, CAP_TOK)
        slot_rows = pl.ds(seq * SEQ_ROWS + CAP_TOK, CAP_TOK)
        hidden_ref[seq, pl.ds(0, CAP_TOK), :] = f_wide[text_rows, :].astype(low)
        hidden_ref[seq, pl.ds(CAP_TOK, LEN - CAP_TOK), :] = dot_wide(
            take, f_wide[slot_rows, :].astype(low)
        ).astype(low)
        x_wide[text_rows, :] = cot_ref[seq, pl.ds(0, CAP_TOK), :].astype(wide)
        x_wide[slot_rows, :] = (
            dot_wide(spread_out, cot_ref[seq, pl.ds(CAP_TOK, LEN - CAP_TOK), :])
            * row_mask[slot_rows, :][:, :1]
        )

    small_grad_ref[...] = jnp.zeros_like(small_grad_ref)
    counts, slots = {"p": 0, "q": 0}, {"p": 9, "q": 4}

    def panels_out(stage, index, target, sems):
        return [
            pltpu.make_async_copy(
                stage.at[index + (panel(third),)], target(third), sems.at[third]
            )
            for third in range(3)
        ]

    def stage_copies(kind, slot, target):
        if kind == "p":
            return panels_out(
                raw, (pl.ds(2 * slot, 2), slice(None), slice(None)), target, p_sems.at[slot]
            )
        return panels_out(stage_q, (slot, slice(None), slice(None)), target, q_sems.at[slot])

    def send(kind, count, value, target):
        slot = count % slots[kind]
        copies = stage_copies(kind, slot, target)

        for copy in copies:
            copy.wait()
        if kind == "p":
            raw[pl.ds(2 * slot, 2)] = value.astype(low).reshape(2, 4, 32, D)
        else:
            stage_q[slot] = value.astype(low).reshape(8, 32, D)
        for copy in copies:
            copy.start()

    back_copies, text_copies = [], []

    def send_slots():
        def embed_back(rows, value):
            x_wide[rows, :] = value

        sums = norm_back_loop(embed, None, None, 0, lambda rows: x_wide[rows, :], embed_back)
        small_grad_ref[pl.ds(0, 1), :] = sums[0]
        small_grad_ref[pl.ds(1, 1), :] = sums[1]
        for seq in range(2):
            text_copies.append(
                pltpu.make_async_copy(
                    x_wide.at[pl.ds(seq * SEQ_ROWS, CAP_TOK)], text_ref.at[seq], text_sems.at[seq]
                )
            )
            text_copies[seq].start()
            slots_out[seq] = (
                x_wide[pl.ds(seq * SEQ_ROWS + CAP_TOK, CAP_TOK), :].astype(low).reshape(4, 32, D)
            )
        pl.semaphore_wait(barrier, 3)
        for step in (2, 1, 3):
            copy = pltpu.make_async_remote_copy(
                src_ref=slots_out.at[:, (here[2] + step) % 4],
                dst_ref=back.at[here[2]],
                send_sem=back_send.at[step],
                recv_sem=back_recv.at[step],
                device_id=moved(here, 2, step),
                device_id_type=MESH,
            )
            copy.start()
            back_copies.append(copy)
        back[here[2]] = slots_out[:, here[2]]

    def all_stages():
        copies = []
        for slot in range(slots["p"]):
            copies += stage_copies(
                "p", slot, lambda third: grad_ref.at[third, pl.ds(GRAN_DOWN[1] + 2 * slot, 2)]
            )
        for slot in range(slots["q"]):
            copies += stage_copies(
                "q",
                slot,
                lambda third: grad_ref.at[third, pl.ds(GRAN_UP[1] + 8 * (slot % 3), 8), slot // 3],
            )
        return copies + panels_out(
            stage_r,
            (slice(None), slice(None), slice(None)),
            lambda third: grad_ref.at[third, pl.ds(GRAN_QKV[1], 6)],
            r_sems,
        )

    for stage in (stage_q, stage_r):
        stage[...] = jnp.zeros_like(stage)
    for copy in all_stages():
        copy.start()

    for layer in reversed(range(LAYERS)):
        base = 7 + 12 * layer
        top = layer == LAYERS - 1

        def d_out(rows):
            return x_wide[rows, :]

        def second_back(rows, value):
            f_wide[rows, :] = value
            d_low[rows, :] = value.astype(low)

        sums = norm_back_loop(second, layer, 2 * layer + 1, base + 10, d_out, second_back)
        for row, value in zip((10, 11, 9), sums):
            small_grad_ref[pl.ds(base + row, 1), :] = value
        if not top:
            ready("down", 0)
            take_back("act").wait()
            take_back("slope").wait()
        p_first = counts["p"]

        def down_back(count, carry, layer=layer, base=base, p_first=p_first):
            block, col = count // 3, count % 3
            grad = dot_wide(act[block, :, cols(col)], d_low[...], FIRST)
            send(
                "p",
                p_first + count,
                grad,
                lambda third: grad_ref.at[third, pl.ds(GRAN_DOWN[layer] + 2 * count, 2)],
            )
            value = dot_wide(d_low[...], w_down[pl.ds(2 * count, 2)].reshape(CHUNK, D), LAST)
            rounded = (value * slope[block, :, cols(col)].astype(wide)).astype(low)
            slope[block, :, cols(col)] = rounded
            small_grad_ref[pl.ds(base + 5 + block, 1), cols(col)] = jnp.sum(
                rounded.astype(wide), axis=0, keepdims=True
            )
            return carry

        lax.fori_loop(0, 12, down_back, 0, unroll=6)
        counts["p"] += 12
        if top:
            begin("down", 0)
            take_back("act").start()
        else:
            ready("up", 0)
        turned[...] = f_low[layer].T
        q_first = counts["q"]

        def up_back(count, carry, layer=layer, q_first=q_first):
            block, part = count // 3, count % 3
            left = turned[pl.ds(pl.multiple_of(part * CHUNK, CHUNK), CHUNK), :]
            grad = dot_wide(left, slope[block])
            send(
                "q",
                q_first + count,
                grad,
                lambda third: grad_ref.at[third, pl.ds(GRAN_UP[layer] + 8 * part, 8), block],
            )
            return carry

        lax.fori_loop(0, 12, up_back, 0, unroll=6)
        counts["q"] += 12

        def first_back(part, carry):
            value = f_wide[:, cols(part)]
            for block in range(4):
                value = value + dot_wide(
                    slope[block], w_up[block, pl.ds(8 * part, 8)].reshape(CHUNK, D), LAST
                )
            f_wide[:, cols(part)] = value
            return carry

        lax.fori_loop(0, 3, first_back, 0, unroll=3)
        if top:
            begin("up", 0)
            take_back("slope").start()

        def mid_back(rows, value):
            x_wide[rows, :] = value
            d_low[rows, :] = value.astype(low)

        sums = norm_back_loop(
            mid, layer, 2 * layer, base + 3, lambda rows: f_wide[rows, :], mid_back
        )
        for row, value in zip((3, 4, 2), sums):
            small_grad_ref[pl.ds(base + row, 1), :] = value
        turned[...] = att[layer].T
        p_first = counts["p"]
        if not top:
            ready("out", 0)

        def out_back(part, carry, layer=layer, p_first=p_first):
            left = turned[pl.ds(pl.multiple_of(part * CHUNK, CHUNK), CHUNK), :]
            grad = dot_wide(left, d_low[...])
            send(
                "p",
                p_first + part,
                grad,
                lambda third: grad_ref.at[third, pl.ds(GRAN_OUT[layer] + 2 * part, 2)],
            )
            value = dot_wide(d_low[...], w_out[pl.ds(2 * part, 2)].reshape(CHUNK, D), LAST)
            att[layer, :, cols(part)] = value.astype(low)
            return carry

        lax.fori_loop(0, 3, out_back, 0, unroll=3)
        counts["p"] += 3
        if top:
            begin("out", 0)
        else:
            take_back("probs").wait()

        def attend_back(pair, carry, layer=layer):
            lanes = pl.ds(pl.multiple_of(pair * 128, 128), 128)
            for seq in range(2):
                rows = pl.ds(seq * SEQ_ROWS, SEQ_ROWS)
                query = stacked(qkv[layer, 0, rows, lanes])
                key_rows = stacked(qkv[layer, 1, rows, lanes])
                value_rows = qkv[layer, 2, rows, lanes]
                grad = stacked(att[layer, rows, lanes])
                prob = probs[seq, pair]
                d_value = dot_wide(prob, grad, FIRST)
                d_prob = dot_wide(grad, value_rows, LAST)
                prob = prob.astype(wide)
                product = d_prob * prob
                d_score = (product - prob * jnp.sum(product, -1, keepdims=True)).astype(low)
                d_query = dot_wide(beside(d_score), key_rows)
                d_key = dot_wide(d_score, query, FIRST)
                qkv[layer, 0, rows, lanes] = (d_query * 0.125).astype(low)
                qkv[layer, 1, rows, lanes] = (d_key * 0.125).astype(low)
                qkv[layer, 2, rows, lanes] = d_value.astype(low)
            return carry

        lax.fori_loop(0, 6, attend_back, 0, unroll=3)
        if top:
            take_back("probs").start()
        if not top:
            take_back("qkv").wait()

        def in_back(part, carry, layer=layer):
            value = x_wide[:, cols(part)]
            for block in range(3):
                value = value + dot_wide(
                    qkv[layer, block],
                    w_qkv[pl.ds(pl.multiple_of(part * CHUNK, CHUNK), CHUNK), pl.ds(D * block, D)],
                    LAST,
                )
            x_wide[:, cols(part)] = value
            return carry

        lax.fori_loop(0, 3, in_back, 0, unroll=3)
        if top:
            take_back("qkv").start()
        else:
            send_slots()
        for block, row in ((0, 0), (2, 1)):

            def column_sum(step, carry, block=block, layer=layer):
                rows = pl.ds(pl.multiple_of(step * 64, 64), 64)
                value = qkv[layer, block, rows, :].astype(wide)
                return carry + jnp.sum(value.reshape(8, 8, D), axis=0)

            value = lax.fori_loop(0, ROWS // 64, column_sum, jnp.zeros((8, D), wide))
            small_grad_ref[pl.ds(base + row, 1), :] = jnp.sum(value, axis=0, keepdims=True)
        turned[...] = x_low[layer].T

        def qkv_back(part, carry, layer=layer):
            left = turned[pl.ds(pl.multiple_of(part * CHUNK, CHUNK), CHUNK), :]
            for block in range(3):
                grad = dot_wide(left, qkv[layer, block])
                for col in range(6):
                    stage_f[col, pl.ds(block, CHUNK, stride=3), :] = grad[
                        :, 128 * col : 128 * col + 128
                    ]
            copies = panels_out(
                stage_r,
                (slice(None), slice(None), slice(None)),
                lambda third: grad_ref.at[third, pl.ds(GRAN_QKV[layer] + 6 * part, 6)],
                r_sems,
            )
            for copy in copies:
                copy.wait()
            for col in range(6):
                stage_r[:, :, :, pl.ds(128 * col, 128)] = (
                    stage_f[col].astype(low).reshape(6, 4, 32, 128)
                )
            for copy in copies:
                copy.start()
            return carry

        lax.fori_loop(0, 3, qkv_back, 0)

    dest_row = dest_row_ref[...]
    dest_col = jnp.broadcast_to(dest_row, (128, 128)).T
    earlier = lax.broadcasted_iota(jnp.int32, (128, 128), 1) < lax.broadcasted_iota(
        jnp.int32, (128, 128), 0
    )
    rank = jnp.sum(
        jnp.where(earlier & (dest_col == dest_row), 1.0, 0.0), axis=1, keepdims=True
    ).astype(jnp.int32)
    spots = lax.broadcasted_iota(jnp.int32, (128, 256), 1)
    chosen = jnp.where(spots == rank + 32 * dest_col[:, :1], 1.0, 0.0).astype(low)
    for copy in back_copies:
        copy.wait_recv()
    d_region = dot_wide(chosen, back[...].reshape(256, D)).astype(low)
    region_ref[...] = d_region
    for part in range(8):
        grad = dot_wide(feat_ref[:, pl.ds(CHUNK * part, CHUNK)], d_region, FIRST)
        send(
            "p",
            counts["p"] + part,
            grad,
            lambda third, part=part: grad_ref.at[third, pl.ds(2 * part, 2)],
        )
    d_wide = d_region.astype(wide)
    small_grad_ref[pl.ds(2, 1), :] = jnp.sum(d_wide, axis=0, keepdims=True)
    small_grad_ref[pl.ds(3, 4), :] = jnp.dot(
        box_ref[...], d_wide, precision=highest_exactness, preferred_element_type=wide
    )
    for copy in back_copies:
        copy.wait_send()
    for copy in text_copies:
        copy.wait()
    for copy in all_stages():
        copy.wait()


def both_layers(
    text_in, slots, valid, cotangent, small_rows, region_feats, boxes, region_dest, weight_rows
):
    low, wide = jnp.bfloat16, jnp.float32
    dma = pltpu.SemaphoreType.DMA
    whole = pl.BlockSpec(memory_space=pltpu.VMEM)
    remote = pl.BlockSpec(memory_space=pl.ANY)
    made = pl.pallas_call(
        layers_kernel,
        out_shape=(
            jax.ShapeDtypeStruct((2, LEN, D), low),
            jax.ShapeDtypeStruct((2, CAP_TOK, D), wide),
            jax.ShapeDtypeStruct((128, D), low),
            jax.ShapeDtypeStruct((32, D), wide),
            jax.ShapeDtypeStruct((3, GRANS, 4, 32, THIRD), low),
            jax.ShapeDtypeStruct((4, ROWS, D), low),
            jax.ShapeDtypeStruct((4, ROWS, D), low),
            jax.ShapeDtypeStruct((2, 6, 2 * SEQ_ROWS, SEQ_ROWS), low),
            jax.ShapeDtypeStruct((D, 3 * D), low),
        ),
        in_specs=[whole] * 8 + [remote],
        out_specs=(whole, remote, whole, whole) + (remote,) * 5,
        scratch_shapes=[
            pltpu.VMEM((ROWS, D), low),
            pltpu.VMEM((ROWS, 128), wide),
            pltpu.VMEM((2, 8, SEQ_ROWS), wide),
            pltpu.VMEM((2 * LAYERS, ROWS, 128), wide),
            pltpu.VMEM((ROWS, D), wide),
            pltpu.VMEM((ROWS, D), wide),
            pltpu.VMEM((LAYERS, ROWS, D), low),
            pltpu.VMEM((LAYERS, 3, ROWS, D), low),
            pltpu.VMEM((LAYERS, ROWS, D), low),
            pltpu.VMEM((LAYERS, ROWS, D), wide),
            pltpu.VMEM((LAYERS, ROWS, D), low),
            pltpu.VMEM((LAYERS, ROWS, D), wide),
            pltpu.VMEM((4, ROWS, D), low),
            pltpu.VMEM((4, ROWS, D), low),
            pltpu.VMEM((2, 6, 2 * SEQ_ROWS, SEQ_ROWS), low),
            pltpu.VMEM((ROWS, D), low),
            pltpu.VMEM((D, ROWS), low),
            pltpu.VMEM((D, 3 * D), low),
            pltpu.VMEM((6, 4, 32, D), low),
            pltpu.VMEM((4, 24, 32, D), low),
            pltpu.VMEM((24, 4, 32, D), low),
            pltpu.VMEM((18, 4, 32, D), low),
            pltpu.VMEM((6, D, 128), wide),
            pltpu.VMEM((4, 8, 32, D), low),
            pltpu.VMEM((6, 4, 32, D), low),
            dma((7, 3)),
            dma((8,)),
            dma((9, 3)),
            dma((4, 3)),
            dma((3,)),
            pltpu.VMEM((2, 4, 32, D), low),
            pltpu.VMEM((4, 2, 32, D), low),
            dma((4,)),
            dma((4,)),
            dma((2,)),
            pltpu.VMEM((32, D), wide),
        ],
        compiler_params=pltpu.CompilerParams(
            collective_id=2, has_side_effects=True, vmem_limit_bytes=62 * 1024 * 1024
        ),
    )(
        text_in,
        slots.reshape(2, CAP_TOK, D),
        valid.reshape(2, CAP_TOK, 128),
        cotangent,
        small_rows,
        region_feats,
        boxes,
        region_dest.reshape(1, -1),
        weight_rows.reshape(3, GRANS, 4, 32, THIRD),
    )
    return made[:5]


def in_plane(here, number, step):
    if number == 0:
        pos = (2 * here[2] + here[3] + step) % 8
        return device_at(here[0], here[1], pos // 2, pos % 2)
    pos = (4 * here[0] + here[1] + step) % 16
    return device_at(pos // 4, pos % 4, here[2], here[3])


def greet_planes(here):
    barrier = pltpu.get_barrier_semaphore()
    for number, count in ((0, 8), (1, 16)):
        for step in range(1, count):
            pl.semaphore_signal(
                barrier, inc=1, device_id=in_plane(here, number, step), device_id_type=MESH
            )
    pl.semaphore_wait(barrier, 22)


class Total:
    def __init__(self, here, slots, send_sems, recv_sems):
        self.here, self.slots, self.sems = here, slots, (send_sems, recv_sems)
        self.copies = {}

    def send(self, level, value=None):
        axis = (2, 1, 0, 3)[level]
        slots, own = self.slots[level], self.here[axis]
        if value is not None:
            slots[own] = value.astype(slots.dtype)
        for step in range(1, 2 if axis == 3 else 4):
            copy = pltpu.make_async_remote_copy(
                src_ref=slots.at[own],
                dst_ref=slots.at[own],
                send_sem=self.sems[0].at[level, step],
                recv_sem=self.sems[1].at[level, step],
                device_id=moved(self.here, axis, step),
                device_id_type=MESH,
            )
            copy.start()
            self.copies[level, step] = copy

    def take(self, level):
        count = 2 if level == 3 else 4
        for step in range(1, count):
            self.copies[level, step].wait_recv()
        value = self.slots[level][0].astype(jnp.float32)
        for pos in range(1, count):
            value = value + self.slots[level][pos].astype(jnp.float32)
        return value

    def end(self):
        for copy in self.copies.values():
            copy.wait_send()


def reduce_kernel(
    grad_ref,
    small_ref,
    region_ref,
    full_ref,
    shard_ref,
    total_ref,
    square_ref,
    feat_grad_ref,
    acc,
    sibling,
    chain_one,
    fin_one,
    chain_two,
    fin_two,
    fin_three,
    shares,
    region,
    flat,
    small_a,
    small_b,
    small_c,
    small_d,
    tile_a,
    tile_b,
    load_sems,
    core_send,
    core_recv,
    chain_send,
    chain_recv,
    fin_send,
    fin_recv,
    last_send,
    last_recv,
    share_send,
    share_recv,
    small_send,
    small_recv,
    tile_send,
    tile_recv,
    region_sem,
):
    low, wide = jnp.bfloat16, jnp.float32
    here = place()
    greet_planes(here)
    core = here[3]

    chains, fins = (chain_one, chain_two), (fin_one, fin_two)
    first_half, second_half, both = pl.ds(0, HALF), pl.ds(HALF, HALF), pl.ds(0, PIECE)
    halves = (first_half, second_half)

    def at_step(part, level, step):
        return (here[AXIS_ORDER[part][level]] + step) % 4

    def fixed(part, level, step, sub=None):
        index = [None] * 3
        for before in range(level):
            index[AXIS_ORDER[part][before]] = here[AXIS_ORDER[part][before]]
        index[AXIS_ORDER[part][level]] = at_step(part, level, step)
        if sub is not None:
            index[AXIS_ORDER[part][level + 1]] = at_step(part, level + 1, sub)
        return index

    def block(buffer, part, level, step, rows, sub=None):
        index = [slice(None) if value is None else value for value in fixed(part, level, step, sub)]
        return buffer.at[(part,) + tuple(index) + (rows, slice(None))]

    def grad_block(part, step, sub, which):
        index = [slice(None) if value is None else value for value in fixed(part, 0, step, sub)]
        index.insert(2, which)
        return grad_ref.at[(part,) + tuple(index) + (slice(None), slice(None))]

    order = (2, 1, 3, 0)
    loads, core_copies = {}, {}
    for sub in order:
        for step in order:
            for part in range(3):
                core_copies[part, step, sub] = pltpu.make_async_remote_copy(
                    src_ref=grad_block(part, step, sub, 1 - core),
                    dst_ref=block(sibling, part, 0, step, both, sub),
                    send_sem=core_send.at[part, step, sub],
                    recv_sem=core_recv.at[part, step, sub],
                    device_id=moved(here, 3, 1),
                    device_id_type=MESH,
                )
                loads[part, step, sub] = pltpu.make_async_copy(
                    grad_block(part, step, sub, core),
                    block(acc, part, 0, step, both, sub),
                    load_sems.at[part, step, sub],
                )

    def issue(sub):
        for step in order:
            for part in range(3):
                core_copies[part, step, sub].start()
                loads[part, step, sub].start()

    small = Total(here, (small_a, small_b, small_c, small_d), small_send, small_recv)
    small.send(0, small_ref[...])
    issue(2)

    def add_blocks(part, level, step, rows, terms, sub=None):
        index = fixed(part, level, step, sub)
        free = [axis for axis in range(3) if index[axis] is None]

        def one(count, carry):
            spot = list(index)
            if free:
                spot[free[0]] = count
            inner = (count,) if free else ()
            where = (part,) + tuple(spot) + (rows, slice(None))
            if len(terms) == 1:
                acc[where] = acc[where] + terms[0](tuple(spot), inner, rows)
                return carry
            value = acc[where].astype(wide)
            for term in terms:
                value = value + term(tuple(spot), inner, rows).astype(wide)
            acc[where] = value.astype(low)
            return carry

        if free:
            lax.fori_loop(0, 4, one, 0)
        else:
            one(0, 0)

    chain_copies, fin_copies, last_copies = {}, {}, {}

    def slot_of(level, part, way, sub):
        return (part, way) if sub is None else (part, way, sub)

    def send_chain(part, level, sub=None):
        for way in (0, 1):
            number = 0 if sub is None else sub
            copy = pltpu.make_async_remote_copy(
                src_ref=block(acc, part, level, 2, halves[way], sub),
                dst_ref=chains[level].at[slot_of(level, part, way, sub)],
                send_sem=chain_send.at[level, part, way, number],
                recv_sem=chain_recv.at[level, part, way, number],
                device_id=moved(here, AXIS_ORDER[part][level], (1, 3)[way]),
                device_id_type=MESH,
            )
            copy.start()
            chain_copies[part, level, way, sub] = copy

    def send_fin(part, level, way, half, sub=None):
        number = 0 if sub is None else sub
        count = 1 if sub is not None else 2 - level
        index = slot_of(level, part, way, sub) + (slice(None),) * count + (halves[half], slice(None))
        copy = pltpu.make_async_remote_copy(
            src_ref=block(acc, part, level, (1, 3)[way], halves[half], sub),
            dst_ref=fins[level].at[index],
            send_sem=fin_send.at[level, part, way, half, number],
            recv_sem=fin_recv.at[level, part, way, half, number],
            device_id=moved(here, AXIS_ORDER[part][level], (1, 3)[way]),
            device_id_type=MESH,
        )
        copy.start()
        fin_copies[part, level, way, half, sub] = copy

    def sibling_term(part):
        return lambda spot, inner, rows: sibling[(part,) + spot + (rows, slice(None))]

    def relay(part, level, sub=None):
        for way in (0, 1):
            chain_copies[part, level, way, sub].wait_recv()
            slot = slot_of(level, part, way, sub)
            terms = [lambda spot, inner, rows, slot=slot: chains[level][slot + inner]]
            if level == 0:
                terms.append(sibling_term(part))
            add_blocks(part, level, (1, 3)[way], halves[way], terms, sub)
            send_fin(part, level, way, way, sub)

    def finish(part, level, sub=None):
        for way in (0, 1):
            for half in (0, 1):
                fin_copies[part, level, way, half, sub].wait_recv()
        slots = [slot_of(level, part, way, sub) for way in (0, 1)]
        terms = [lambda spot, inner, rows, slot=slot: fins[level][slot + inner] for slot in slots]
        if level == 0:
            terms.append(sibling_term(part))
        add_blocks(part, level, 0, both, terms, sub)

    def gather_pair(part, step, sub, rows=None):
        loads[part, step, sub].wait()
        core_copies[part, step, sub].wait_recv()
        if rows is not None:
            add_blocks(part, 0, step, rows, [sibling_term(part)], sub)

    def second_phase(part, sub):
        finish(part, 0, sub)
        if sub == 2:
            send_chain(part, 1)
        elif sub == 1:
            send_fin(part, 1, 0, 1)
        elif sub == 3:
            send_fin(part, 1, 1, 0)

    for count, sub in enumerate(order):
        for part in range(3):
            gather_pair(part, 2, sub, both)
            send_chain(part, 0, sub)
        if count == 0:
            issue(1)
            loaded = region_loads(full_ref, region, region_sem)
            for copy in loaded:
                copy.start()
        for step, way in ((1, 0), (3, 1)):
            for part in range(3):
                gather_pair(part, step, sub, halves[1 - way])
                send_fin(part, 0, way, 1 - way, sub)
        if count < 2:
            issue(order[count + 2])
        for part in range(3):
            gather_pair(part, 0, sub)
        for part in range(3):
            relay(part, 0, sub)
        if count:
            for part in range(3):
                second_phase(part, order[count - 1])
        if count < 3:
            small.send(count + 1, small.take(count))
        if count == 2:
            for copy in loaded:
                copy.wait()
            matrix = region[...].reshape(16 * PIECE, D)[:FEAT]
            feat_grad_ref[...] = dot_wide(region_ref[...], matrix, LAST)
    summed = small.take(3)
    for col in range(6):
        total_ref[pl.ds(col, 31, stride=6), :] = summed[:31, 128 * col : 128 * col + 128]
    for part in range(3):
        relay(part, 1)
    for part in range(3):
        second_phase(part, 0)
    for part in range(3):
        finish(part, 1)
        for step in (2, 1, 3):
            copy = pltpu.make_async_remote_copy(
                src_ref=block(acc, part, 2, step, both),
                dst_ref=fin_three.at[part, step],
                send_sem=last_send.at[part, step],
                recv_sem=last_recv.at[part, step],
                device_id=moved(here, AXIS_ORDER[part][2], step),
                device_id_type=MESH,
            )
            copy.start()
            last_copies[part, step] = copy
    for part in range(3):
        for step in (1, 3, 2):
            last_copies[part, step].wait_recv()
        add_blocks(
            part,
            2,
            0,
            both,
            [
                lambda spot, inner, rows, step=step: fin_three[part, step, rows, :]
                for step in (1, 2, 3)
            ],
        )

    square = jnp.zeros((8, 128), wide)
    for part in range(3):
        own = acc[part, here[0], here[1], here[2]]
        shares[here[2], part] = own
        value = own.astype(wide)
        value = value * value
        value = value.reshape(PIECE // 8, 8, THIRD)
        square = square + jnp.sum(value[:, :, :128] + value[:, :, 128:], axis=0)
    def share(number, step, rows, way):
        where = shares.at[(here[2] + step) % 4, :, rows]
        return pltpu.make_async_remote_copy(
            src_ref=where,
            dst_ref=where,
            send_sem=share_send.at[number],
            recv_sem=share_recv.at[number],
            device_id=moved(here, 2, way),
            device_id_type=MESH,
        )

    share_copies = [share(0, 0, both, 1), share(1, 0, both, 3)]
    for copy in share_copies:
        copy.start()
    tile_copies = [[], []]

    def tile_out(number, value):
        slots, own = ((tile_a, 2 * here[2] + core), (tile_b, 4 * here[0] + here[1]))[number]
        slots[own] = value
        for step in range(1, (8, 16)[number]):
            copy = pltpu.make_async_remote_copy(
                src_ref=slots.at[own],
                dst_ref=slots.at[own],
                send_sem=tile_send.at[number, step],
                recv_sem=tile_recv.at[number, step],
                device_id=in_plane(here, number, step),
                device_id_type=MESH,
            )
            copy.start()
            tile_copies[number].append(copy)

    def tile_in(number):
        for copy in tile_copies[number]:
            copy.wait_recv()
        slots = (tile_a, tile_b)[number]
        value = slots[0]
        for pos in range(1, (8, 16)[number]):
            value = value + slots[pos]
        return value

    tile_out(0, square)
    share(0, 3, both, 1).wait_recv()
    share_copies.append(share(2, 3, first_half, 1))
    share_copies[2].start()
    share(1, 1, both, 3).wait_recv()
    share_copies.append(share(3, 1, second_half, 3))
    share_copies[3].start()
    first = lax.axis_index("dp") * 5

    def spread_out(grans):
        for gran in grans:
            up = is_up(first + gran)

            def put(gran, dense):
                for piece in range(4):
                    quarter, spot = (4 * gran + piece) // 5, (4 * gran + piece) % 5
                    for part in range(3):
                        value = shares[quarter, part, pl.ds(32 * spot, 32), :].astype(wide)
                        for half in range(2):
                            col = 2 * part + half
                            if dense:
                                rows = pl.ds(6 * GRAN * gran + 6 * 32 * piece + col, 32, stride=6)
                            else:
                                rows = pl.ds(6 * GRAN * gran + 6 * piece + col, 32, stride=24)
                            flat[rows, :] = value[:, 128 * half : 128 * half + 128]

            @pl.when(up)
            def _(gran=gran):
                put(gran, False)

            @pl.when(jnp.logical_not(up))
            def _(gran=gran):
                put(gran, True)

    tile_out(1, tile_in(0))
    share(2, 2, first_half, 1).wait_recv()
    share(3, 2, second_half, 3).wait_recv()
    spread_out((0, 1, 2, 3, 4))
    shard_ref[...] = flat[...].astype(low)
    total = jnp.sum(tile_in(1), axis=0, keepdims=True)
    smalls = total_ref[...]
    total = total + jnp.sum(smalls * smalls, axis=0, keepdims=True)
    square_ref[0, 0] = jnp.sum(total)
    for copy in share_copies:
        copy.wait_send()
    small.end()
    for copy in tile_copies[0] + tile_copies[1]:
        copy.wait_send()
    for copies in (core_copies, chain_copies, fin_copies, last_copies):
        for copy in copies.values():
            copy.wait_send()


def reduce_gradients(grad_rows, small_rows, region_low, full_low):
    low, wide = jnp.bfloat16, jnp.float32
    dma = pltpu.SemaphoreType.DMA
    whole = pl.BlockSpec(memory_space=pltpu.VMEM)
    remote = pl.BlockSpec(memory_space=pl.ANY)
    rows_shape = (3, 4, 4, 2, 4, PIECE, THIRD)
    made = pl.pallas_call(
        reduce_kernel,
        out_shape=(
            jax.ShapeDtypeStruct((3840, 128), low),
            jax.ShapeDtypeStruct((186, 128), wide),
            jax.ShapeDtypeStruct((1, 1), wide),
            jax.ShapeDtypeStruct((128, FEAT), wide),
        ),
        in_specs=[remote, whole, whole, remote],
        out_specs=(whole, whole, pl.BlockSpec(memory_space=pltpu.SMEM), whole),
        scratch_shapes=[
            pltpu.VMEM((3, 4, 4, 4, PIECE, THIRD), low),
            pltpu.VMEM((3, 4, 4, 4, PIECE, THIRD), low),
            pltpu.VMEM((3, 2, 4, 4, HALF, THIRD), low),
            pltpu.VMEM((3, 2, 4, 4, PIECE, THIRD), low),
            pltpu.VMEM((3, 2, 4, HALF, THIRD), low),
            pltpu.VMEM((3, 2, 4, PIECE, THIRD), low),
            pltpu.VMEM((3, 4, PIECE, THIRD), low),
            pltpu.VMEM((4, 3, PIECE, THIRD), low),
            pltpu.VMEM((2, 2, 4, PIECE, D), low),
            pltpu.VMEM((3840, 128), wide),
            pltpu.VMEM((4, 32, D), low),
            pltpu.VMEM((4, 32, D), low),
            pltpu.VMEM((4, 32, D), low),
            pltpu.VMEM((2, 32, D), low),
            pltpu.VMEM((8, 8, 128), wide),
            pltpu.VMEM((16, 8, 128), wide),
            dma((3, 4, 4)),
            dma((3, 4, 4)),
            dma((3, 4, 4)),
            dma((2, 3, 2, 4)),
            dma((2, 3, 2, 4)),
            dma((2, 3, 2, 2, 4)),
            dma((2, 3, 2, 2, 4)),
            dma((3, 4)),
            dma((3, 4)),
            dma((4,)),
            dma((4,)),
            dma((4, 4)),
            dma((4, 4)),
            dma((2, 16)),
            dma((2, 16)),
            dma((3,)),
        ],
        compiler_params=pltpu.CompilerParams(
            collective_id=0, has_side_effects=True, vmem_limit_bytes=62 * 1024 * 1024
        ),
    )(grad_rows.reshape(rows_shape), small_rows, region_low, full_low)
    return made


def local(
    text_in,
    cotangent,
    region_feats,
    boxes,
    region_dest,
    weights_mat,
    moment1_mat,
    moment2_mat,
    weights_small,
    moment1_small,
    moment2_small,
):
    small_in = weights_small.reshape(-1, 128)
    full_low, slots, slot_valid = gather_matrices(
        weights_mat, region_feats, boxes, region_dest, small_in
    )
    hidden_out, text_grad, region_low, small_part, mat_part = both_layers(
        text_in,
        slots,
        slot_valid,
        cotangent,
        small_in,
        region_feats,
        boxes,
        region_dest,
        full_low,
    )
    shard_rows, small_sum, squares, feat_grad = reduce_gradients(
        mat_part, small_part, region_low, full_low
    )
    shard_grad = shard_rows.reshape(-1).astype(jnp.float32)
    small_total = small_sum.reshape(-1)
    grad_norm = jnp.sqrt(squares[0, 0])
    clip_factor = clip_norm / jnp.maximum(grad_norm, clip_norm)
    new_m_mat, new_v_mat, new_w_mat = adam_update(
        weights_mat, moment1_mat, moment2_mat, shard_grad * clip_factor, mat_rate
    )
    new_m_small, new_v_small, new_w_small = adam_update(
        weights_small, moment1_small, moment2_small, small_total * clip_factor, small_rate
    )
    return (
        hidden_out,
        text_grad,
        feat_grad,
        grad_norm,
        shard_grad,
        small_total,
        new_m_mat,
        new_v_mat,
        new_w_mat,
        new_w_mat.astype(jnp.bfloat16),
        new_m_small,
        new_v_small,
        new_w_small,
    )


def solution(mesh):
    return jax.shard_map(
        local,
        mesh=mesh,
        in_specs=(
            P(("dp", "enc"), None, None),
            P(("dp", "enc"), None, None),
            P(("dp", "enc"), None),
            P(None, ("dp", "enc")),
            P(("dp", "enc"), None),
            P("dp"),
            P("dp"),
            P("dp"),
            P(),
            P(),
            P(),
        ),
        out_specs=(
            P(("dp", "enc"), None, None),
            P(("dp", "enc"), None, None),
            P(("dp", "enc"), None),
            P(),
            P("dp"),
            P(),
            P("dp"),
            P("dp"),
            P("dp"),
            P("dp"),
            P(),
            P(),
            P(),
        ),
        check_vma=False,
    )
```

```python
import math

import jax
import jax.numpy as jnp
from jax import lax
from jax.experimental import pallas as pl
from jax.experimental.pallas import tpu as pltpu
from jax.sharding import PartitionSpec as P

MESH = pl.DeviceIdType.MESH

D = 768
HEADS = 12
HEAD_DIM = 64
FF = 3072
FEAT = 2048
LAYERS = 2
CAP_TOK = 128
CAPP = 25
STEP = 10


norm_eps = 1e-05
beta_one = 0.5
beta_two = 0.5
mat_rate = 0.06
small_rate = 0.4
decay_rate = 0.01
adam_eps = 1e-08
clip_norm = 1.0
masked_score = -1e30
highest_exactness = lax.Precision.HIGHEST


def adam_update(params, first_mom, second_mom, gradient, step_rate):
    new_first = beta_one * first_mom + (1.0 - beta_one) * gradient
    new_second = beta_two * second_mom + (1.0 - beta_two) * gradient * gradient
    first_hat = new_first / (1.0 - beta_one**STEP)
    second_hat = new_second / (1.0 - beta_two**STEP)
    new_params = params - step_rate * (
        first_hat / (jnp.sqrt(second_hat) + adam_eps) + decay_rate * params
    )
    return (new_first, new_second, new_params)


ROWS = 512
SEQ_ROWS = 256
LEN = 228
GRAN = 128
CHUNK = 256
GRAN_QKV = (16, 88)
GRAN_OUT = (34, 106)
GRAN_UP = (40, 112)
GRAN_DOWN = (64, 136)
GRANS = 160
LAST = (((1,), (1,)), ((), ()))
FIRST = (((0,), (0,)), ((), ()))
gelu_root = math.sqrt(2.0 / math.pi)
gelu_cube = 0.044715


def is_up(gran):
    return ((gran >= GRAN_UP[0]) & (gran < GRAN_DOWN[0])) | (
        (gran >= GRAN_UP[1]) & (gran < GRAN_DOWN[1])
    )


def dot_wide(left, right, dims=None):
    if dims is None:
        return jnp.dot(left, right, preferred_element_type=jnp.float32)
    return lax.dot_general(left, right, dims, preferred_element_type=jnp.float32)


AXIS_ORDER = ((0, 1, 2), (1, 2, 0), (2, 0, 1))
HALF = 80
PIECE = 160
THIRD = 256


def place():
    dp_pos = lax.axis_index("dp")
    y_pos = lax.axis_index("enc")
    return (dp_pos // 8, (dp_pos // 2) % 4, y_pos, dp_pos % 2)


def device_at(x_pos, z_pos, y_pos, core):
    return (x_pos * 8 + z_pos * 2 + core, y_pos)


def moved(here, axis, step):
    there = list(here)
    if axis == 3:
        there[3] = 1 - here[3]
    else:
        there[axis] = (here[axis] + step) % 4
    return device_at(*there)


def greet(here):
    barrier = pltpu.get_barrier_semaphore()
    for axis, steps in ((0, (1, 2, 3)), (1, (1, 2, 3)), (2, (1, 2, 3)), (3, (1,))):
        for step in steps:
            pl.semaphore_signal(
                barrier, inc=1, device_id=moved(here, axis, step), device_id_type=MESH
            )
    pl.semaphore_wait(barrier, 10)


GATHER_ORDER = ((2, 1, 0), (0, 2, 1), (1, 0, 2))
MESH_DIMS = (0, 1, 3)


def dispatch(dest_row, target):
    earlier = lax.broadcasted_iota(jnp.int32, (128, 128), 0) < lax.broadcasted_iota(
        jnp.int32, (128, 128), 1
    )
    dest_col = jnp.broadcast_to(dest_row, (128, 128)).T
    same = earlier & (dest_col == dest_row)
    rank = jnp.sum(jnp.where(same, 1.0, 0.0), axis=0, keepdims=True).astype(jnp.int32)
    spot = rank + 32 * (dest_row & 1)
    spots = lax.broadcasted_iota(jnp.int32, (64, 128), 0)
    chosen = (spots == spot) & ((dest_row >> 1) == target)
    return jnp.where(chosen, 1.0, 0.0)


def region_loads(full_ref, region, sems):
    return [
        pltpu.make_async_copy(
            full_ref.at[third, 0, pl.ds(0, 2)],
            region.at[:, :, :, :, pl.ds(THIRD * third, THIRD)],
            sems.at[third],
        )
        for third in range(3)
    ]


def gather_kernel(
    flat_in_ref,
    feat_in_ref,
    box_in_ref,
    dest_in_ref,
    small_in_ref,
    full_ref,
    slot_out_ref,
    valid_out_ref,
    flat_ref,
    feat_ref,
    box_ref,
    dest_row_ref,
    small_flat,
    slot_ref,
    valid_ref,
    operand_sems,
    own,
    region,
    rows_out,
    valid_out,
    places,
    own_sem,
    region_sem,
    one_send,
    one_recv,
    two_send,
    two_recv,
    last_one_send,
    last_one_recv,
    last_two_send,
    last_two_recv,
    core_send,
    core_recv,
    slot_send,
    slot_recv,
):
    here = place()
    operands = [
        pltpu.make_async_copy(source, target, operand_sems.at[number])
        for number, (source, target) in enumerate(
            (
                (flat_in_ref, flat_ref),
                (dest_in_ref, dest_row_ref),
                (feat_in_ref, feat_ref),
                (box_in_ref, box_ref),
                (small_in_ref, small_flat),
            )
        )
    ]
    for copy in operands:
        copy.start()
    greet(here)
    operands[0].wait()
    first = lax.axis_index("dp") * 5
    for gran in range(5):
        up = is_up(first + gran)

        def fill(gran, dense):
            for block in range(4):
                row = GRAN * gran + 32 * block
                for col in range(6):
                    if dense:
                        rows = pl.ds(6 * GRAN * gran + 6 * 32 * block + col, 32, stride=6)
                    else:
                        rows = pl.ds(6 * GRAN * gran + 6 * block + col, 32, stride=24)
                    own[
                        col // 2, row // PIECE, pl.ds(row % PIECE, 32), pl.ds(128 * (col % 2), 128)
                    ] = flat_ref[rows, :].astype(jnp.bfloat16)

        @pl.when(up)
        def _(gran=gran):
            fill(gran, False)

        @pl.when(jnp.logical_not(up))
        def _(gran=gran):
            fill(gran, True)

    fills = [
        pltpu.make_async_copy(
            own.at[0], full_ref.at[0, here[0], here[1], here[3]], own_sem.at[0]
        )
    ]
    for part in (1, 2):
        fills.append(
            pltpu.make_async_copy(
                own.at[part, here[2]],
                full_ref.at[part, here[0], here[1], here[3], here[2]],
                own_sem.at[part],
            )
        )
    for copy in fills:
        copy.start()

    first_half, second_half, both = pl.ds(0, HALF), pl.ds(HALF, HALF), pl.ds(0, PIECE)
    halves = (first_half, second_half)
    sent = []

    def spot(part, level, target, rows, core, sub=None):
        index = [None, None, core, None]
        for step, axis in enumerate(GATHER_ORDER[part]):
            if step < level:
                value = slice(None)
            elif step == level:
                value = target
            else:
                value = here[axis]
            index[MESH_DIMS[axis]] = value
        if sub is not None:
            index[MESH_DIMS[GATHER_ORDER[part][1]]] = at_step(part, 1, sub)
        return full_ref.at[(part,) + tuple(index) + (rows, slice(None))]

    def at_step(part, level, step):
        return (here[GATHER_ORDER[part][level]] + step) % 4

    def copy_to(where, device, send_sem, recv_sem, source=None):
        return pltpu.make_async_remote_copy(
            src_ref=where if source is None else source,
            dst_ref=where,
            send_sem=send_sem,
            recv_sem=recv_sem,
            device_id=device,
            device_id_type=MESH,
        )

    def send(where, device, send_sem, recv_sem, source=None):
        copy = copy_to(where, device, send_sem, recv_sem, source)
        copy.start()
        sent.append(copy)

    def neighbour(part, level, way):
        return moved(here, GATHER_ORDER[part][level], (1, 3)[way])

    def begin(part, level, source=None):
        block = spot(part, level, at_step(part, level, 0), both, here[3])
        for way in (0, 1):
            send(
                block,
                neighbour(part, level, way),
                one_send.at[part, level, way],
                one_recv.at[part, level, way],
                source,
            )

    def relay(part, level, way):
        came = at_step(part, level, (3, 1)[way])
        copy_to(
            spot(part, level, came, both, here[3]),
            neighbour(part, level, way),
            one_send.at[part, level, way],
            one_recv.at[part, level, way],
        ).wait_recv()
        send(
            spot(part, level, came, halves[way], here[3]),
            neighbour(part, level, way),
            two_send.at[part, level, way],
            two_recv.at[part, level, way],
        )

    def finish(part, level):
        for way in (0, 1):
            copy_to(
                spot(part, level, at_step(part, level, 2), halves[way], here[3]),
                neighbour(part, level, way),
                two_send.at[part, level, way],
                two_recv.at[part, level, way],
            ).wait_recv()

    sibling = moved(here, 3, 1)

    def begin_last(part, sub, source=None):
        block = spot(part, 2, at_step(part, 2, 0), both, here[3], sub)
        for way in (0, 1):
            send(
                block,
                neighbour(part, 2, way),
                last_one_send.at[part, sub, way],
                last_one_recv.at[part, sub, way],
                source,
            )
        send(block, sibling, core_send.at[part, 16 + sub], core_recv.at[part, 16 + sub], source)

    def relay_last(part, sub):
        for way in (0, 1):
            came = at_step(part, 2, (3, 1)[way])
            block = spot(part, 2, came, both, here[3], sub)
            copy_to(
                block,
                neighbour(part, 2, way),
                last_one_send.at[part, sub, way],
                last_one_recv.at[part, sub, way],
            ).wait_recv()
            send(
                spot(part, 2, came, halves[way], here[3], sub),
                neighbour(part, 2, way),
                last_two_send.at[part, sub, way],
                last_two_recv.at[part, sub, way],
            )
            send(
                block,
                sibling,
                core_send.at[part, 4 * way + sub],
                core_recv.at[part, 4 * way + sub],
            )

    def finish_last(part, sub):
        for way in (0, 1):
            block = spot(part, 2, at_step(part, 2, 2), halves[way], here[3], sub)
            copy_to(
                block,
                neighbour(part, 2, way),
                last_two_send.at[part, sub, way],
                last_two_recv.at[part, sub, way],
            ).wait_recv()
            send(
                block,
                sibling,
                core_send.at[part, 8 + 4 * way + sub],
                core_recv.at[part, 8 + 4 * way + sub],
            )

    def await_sibling(part):
        other = 1 - here[3]

        def wait(where, number):
            copy_to(where, sibling, core_send.at[part, number], core_recv.at[part, number]).wait_recv()

        for sub in range(4):
            wait(spot(part, 2, at_step(part, 2, 0), both, other, sub), 16 + sub)
            for way in (0, 1):
                came = at_step(part, 2, (3, 1)[way])
                wait(spot(part, 2, came, both, other, sub), 4 * way + sub)
                across = spot(part, 2, at_step(part, 2, 2), halves[way], other, sub)
                wait(across, 8 + 4 * way + sub)

    begin(1, 0, own.at[1, here[2]])
    begin(2, 0, own.at[2, here[2]])
    begin(0, 1, own.at[0])
    begin_last(0, 0, own.at[0])

    def slot_copy(kind, step, source, target):
        return pltpu.make_async_remote_copy(
            src_ref=source.at[step],
            dst_ref=target.at[:, here[2]],
            send_sem=slot_send.at[kind, step],
            recv_sem=slot_recv.at[kind, step],
            device_id=moved(here, 2, step),
            device_id_type=MESH,
        )

    for copy in operands[1:]:
        copy.wait()
    for step in (1, 2, 3, 0):
        chosen = dispatch(dest_row_ref[...], (here[2] + step) % 4)
        places[step] = chosen.astype(jnp.bfloat16)
        filled = jnp.broadcast_to(jnp.sum(chosen, axis=1, keepdims=True), (64, 128))
        if step == 0:
            valid_ref[:, here[2]] = filled.reshape(2, 32, 128)
        else:
            valid_out[step] = filled.reshape(2, 32, 128)
            slot_copy(1, step, valid_out, valid_ref).start()
    for copy in fills:
        copy.wait()
    for part in (1, 2):
        relay(part, 0, 0)
        relay(part, 0, 1)
    for part in (1, 2):
        finish(part, 0)
        begin(part, 1)
        begin_last(part, 0)
    for part in range(3):
        for way in (0, 1):
            relay(part, 1, way)
            begin_last(part, (3, 1)[way])
    for part in range(3):
        relay_last(part, 0)
    for part in range(3):
        finish(part, 1)
        begin_last(part, 2)
    for sub in (3, 1, 2):
        for part in range(3):
            relay_last(part, sub)
        before = {3: 0, 1: 3, 2: 1}[sub]
        for part in range(3):
            finish_last(part, before)
    for part in range(3):
        finish_last(part, 2)
    for part in range(3):
        await_sibling(part)

    loads = region_loads(full_ref, region, region_sem)
    for copy in loads:
        copy.start()
    region_small = jnp.concatenate(
        [small_flat[pl.ds(12 + col, 5, stride=6), :] for col in range(6)], axis=1
    )
    emb = region_small[:1] + lax.dot_general(
        box_ref[...],
        region_small[1:],
        FIRST,
        precision=highest_exactness,
        preferred_element_type=jnp.float32,
    )
    for copy in loads:
        copy.wait()
    matrix = region[...].reshape(16 * PIECE, D)[:FEAT]
    emb = emb + dot_wide(feat_ref[...], matrix)
    emb = emb.astype(jnp.bfloat16)
    for step in (2, 1, 3, 0):
        placed = dot_wide(places[step], emb).astype(jnp.bfloat16).reshape(2, 32, D)
        if step == 0:
            slot_ref[:, here[2]] = placed
        else:
            rows_out[step] = placed
            slot_copy(0, step, rows_out, slot_ref).start()
    slot_copies = [slot_copy(0, step, rows_out, slot_ref) for step in (1, 2, 3)]
    slot_copies += [slot_copy(1, step, valid_out, valid_ref) for step in (1, 2, 3)]
    for copy in slot_copies:
        copy.wait_recv()
    results = [
        pltpu.make_async_copy(slot_ref, slot_out_ref, operand_sems.at[5]),
        pltpu.make_async_copy(valid_ref, valid_out_ref, operand_sems.at[6]),
    ]
    for copy in results:
        copy.start()
    for copy in results:
        copy.wait()
    for copy in slot_copies:
        copy.wait_send()
    for copy in sent:
        copy.wait_send()


def gather_matrices(flat_vec, region_feats, boxes, region_dest, small_rows):
    low, wide = jnp.bfloat16, jnp.float32
    dma = pltpu.SemaphoreType.DMA
    return pl.pallas_call(
        gather_kernel,
        out_shape=(
            jax.ShapeDtypeStruct((3, 4, 4, 2, 4, PIECE, THIRD), low),
            jax.ShapeDtypeStruct((2, 4, 32, D), low),
            jax.ShapeDtypeStruct((2, 4, 32, 128), wide),
        ),
        in_specs=[pl.BlockSpec(memory_space=pl.ANY)] * 5,
        out_specs=(pl.BlockSpec(memory_space=pl.ANY),) * 3,
        scratch_shapes=[
            pltpu.VMEM((3840, 128), wide),
            pltpu.VMEM((128, FEAT), low),
            pltpu.VMEM((4, 128), wide),
            pltpu.VMEM((1, 128), jnp.int32),
            pltpu.VMEM((186, 128), wide),
            pltpu.VMEM((2, 4, 32, D), low),
            pltpu.VMEM((2, 4, 32, 128), wide),
            dma((7,)),
            pltpu.VMEM((3, 4, PIECE, THIRD), low),
            pltpu.VMEM((2, 2, 4, PIECE, D), low),
            pltpu.VMEM((4, 2, 32, D), low),
            pltpu.VMEM((4, 2, 32, 128), wide),
            pltpu.VMEM((4, 64, 128), low),
            dma((3,)),
            dma((3,)),
            dma((3, 2, 2)),
            dma((3, 2, 2)),
            dma((3, 2, 2)),
            dma((3, 2, 2)),
            dma((3, 4, 2)),
            dma((3, 4, 2)),
            dma((3, 4, 2)),
            dma((3, 4, 2)),
            dma((3, 20)),
            dma((3, 20)),
            dma((2, 4)),
            dma((2, 4)),
        ],
        compiler_params=pltpu.CompilerParams(
            collective_id=1, has_side_effects=True, vmem_limit_bytes=62 * 1024 * 1024
        ),
    )(
        flat_vec.reshape(3840, 128),
        region_feats,
        boxes,
        region_dest.reshape(1, -1),
        small_rows,
    )


def normal(values):
    centre = values - jnp.mean(values, -1, keepdims=True)
    spread = lax.rsqrt(jnp.mean(centre * centre, -1, keepdims=True) + norm_eps)
    return centre * spread, spread


def layers_kernel(
    text_in_ref,
    slot_in_ref,
    valid_ref,
    cot_ref,
    small_flat,
    feat_ref,
    box_ref,
    dest_row_ref,
    weight_ref,
    hidden_ref,
    text_ref,
    region_ref,
    small_grad_ref,
    grad_ref,
    keep_act,
    keep_slope,
    keep_probs,
    keep_qkv,
    embed,
    row_mask,
    key_mask,
    spreads,
    x_wide,
    f_wide,
    x_low,
    qkv,
    att,
    mid,
    f_low,
    second,
    act,
    slope,
    probs,
    d_low,
    turned,
    w_qkv,
    w_out,
    w_up,
    w_down,
    raw,
    stage_f,
    stage_q,
    stage_r,
    load_sems,
    keep_sems,
    p_sems,
    q_sems,
    r_sems,
    slots_out,
    back,
    back_send,
    back_recv,
    text_sems,
    small_ref,
):
    low, wide = jnp.bfloat16, jnp.float32
    step_rows = 128
    here = place()
    barrier = pltpu.get_barrier_semaphore()
    for step in (1, 2, 3):
        pl.semaphore_signal(
            barrier, inc=1, device_id=moved(here, 2, step), device_id_type=MESH
        )

    for col in range(6):
        small_ref[pl.ds(0, 31), pl.ds(128 * col, 128)] = small_flat[pl.ds(col, 31, stride=6), :]

    def small_row(row):
        return small_ref[pl.ds(row, 1), :]

    def small_part(row, col):
        return small_ref[pl.ds(row, 1), pl.ds(pl.multiple_of(col * CHUNK, CHUNK), CHUNK)]

    def cols(col):
        return pl.ds(pl.multiple_of(col * CHUNK, CHUNK), CHUNK)

    def panel(third):
        return pl.ds(THIRD * third, THIRD)

    def load(which, layer):
        first, count, target, number = {
            "qkv": (GRAN_QKV[layer], 18, raw, 0),
            "out": (GRAN_OUT[layer], 6, w_out, 1),
            "down": (GRAN_DOWN[layer], 24, w_down, 2),
            "up": (GRAN_UP[layer], 24, w_up, 3),
        }[which]
        copies = []
        for third in range(3):
            if which != "up":
                copies.append(
                    pltpu.make_async_copy(
                        weight_ref.at[third, pl.ds(first, count)],
                        target.at[:, :, :, panel(third)],
                        load_sems.at[number, third],
                    )
                )
                continue
            for block in range(4):
                copies.append(
                    pltpu.make_async_copy(
                        weight_ref.at[third, pl.ds(first, count), block],
                        target.at[block, :, :, panel(third)],
                        load_sems.at[number + block, third],
                    )
                )
        return copies

    def begin(which, layer):
        for copy in load(which, layer):
            copy.start()

    def ready(which, layer):
        for copy in load(which, layer):
            copy.wait()

    keeps = {
        "act": (act, keep_act, 0),
        "slope": (slope, keep_slope, 1),
        "probs": (probs, keep_probs, 2),
        "qkv": (w_qkv, keep_qkv, 3),
    }

    def put_away(name):
        here, there, sem = keeps[name]
        return pltpu.make_async_copy(here, there, keep_sems.at[sem])

    def take_back(name):
        here, there, sem = keeps[name]
        return pltpu.make_async_copy(there, here, keep_sems.at[4 + sem])

    def norm_loop(source, layer, number, gain_row, bias_row, store):
        gain, bias = small_row(gain_row), small_row(bias_row)

        def one(step, carry):
            rows = pl.ds(pl.multiple_of(step * step_rows, step_rows), step_rows)
            if layer is None:
                scaled, spread = normal(source[rows, :].astype(wide))
            else:
                scaled, spread = normal(source[layer, rows, :])
                source[layer, rows, :] = scaled
                spreads[number, rows, :] = jnp.broadcast_to(spread, (step_rows, 128))
            store(rows, scaled * gain + bias)
            return carry

        lax.fori_loop(0, ROWS // step_rows, one, 0, unroll=True)

    def norm_back_loop(source, layer, number, gain_row, dy_of, store):
        gain = small_row(gain_row)

        def fold(values):
            return jnp.sum(values.reshape(step_rows // 8, 8, D), axis=0)

        def one(step, carry):
            rows = pl.ds(pl.multiple_of(step * step_rows, step_rows), step_rows)
            if layer is None:
                scaled, spread = normal(source[rows, :].astype(wide))
            else:
                scaled, spread = source[layer, rows, :], spreads[number, rows, :][:, :1]
            grad = dy_of(rows)
            up = grad * gain
            result = spread * (
                up
                - jnp.mean(up, -1, keepdims=True)
                - scaled * jnp.mean(up * scaled, -1, keepdims=True)
            )
            store(rows, result)
            rounded = result.astype(low).astype(wide)
            return (
                carry[0] + fold(grad * scaled),
                carry[1] + fold(grad),
                carry[2] + fold(rounded),
            )

        zero = jnp.zeros((8, D), wide)
        sums = lax.fori_loop(0, ROWS // step_rows, one, (zero, zero, zero), unroll=True)
        return [jnp.sum(value, axis=0, keepdims=True) for value in sums]

    lane = lax.broadcasted_iota(jnp.int32, (SEQ_ROWS, 128), 1)
    halves = (lane < 64, lane >= 64)

    def only(value, half):
        return jnp.where(halves[half], value, jnp.zeros_like(value))

    def stacked(value):
        return jnp.concatenate([only(value, 0), only(value, 1)], axis=0)

    def beside(value):
        return jnp.concatenate([value[:SEQ_ROWS], value[SEQ_ROWS:]], axis=1)

    begin("qkv", 0)

    def slot_spots(shape, slot_axis):
        padded = lax.broadcasted_iota(jnp.int32, shape, 1 - slot_axis)
        slots = lax.broadcasted_iota(jnp.int32, shape, slot_axis)
        place_of = (padded >> 5) * CAPP + (padded & 31)
        chosen = (slots == place_of) & ((padded & 31) < CAPP)
        return jnp.where(chosen, 1.0, 0.0).astype(low)

    for seq in range(2):
        text_rows = pl.ds(seq * SEQ_ROWS, CAP_TOK)
        slot_rows = pl.ds(seq * SEQ_ROWS + CAP_TOK, CAP_TOK)
        embed[text_rows, :] = text_in_ref[seq]
        embed[slot_rows, :] = slot_in_ref[seq]
        row_mask[text_rows, :] = jnp.ones((CAP_TOK, 128), wide)
        row_mask[slot_rows, :] = valid_ref[seq]
        key_mask[seq, :, pl.ds(0, CAP_TOK)] = jnp.ones((8, CAP_TOK), wide)
        key_mask[seq, :, pl.ds(CAP_TOK, CAP_TOK)] = valid_ref[seq].T[:8]

    def first_store(rows, value):
        x_wide[rows, :] = value
        x_low[0, rows, :] = value.astype(low)

    norm_loop(embed, None, None, 0, 1, first_store)

    for layer in range(LAYERS):
        base = 7 + 12 * layer
        ready("qkv", layer)
        if layer == 0:
            for name in ("out", "up", "down"):
                begin(name, 0)
        if layer:
            put_away("qkv").wait()
        for part in range(3):
            for col in range(6):
                stage_f[col] = raw[pl.ds(6 * part, 6), :, :, pl.ds(128 * col, 128)].reshape(
                    D, 128
                ).astype(wide)
            for block in range(3):
                for col in range(6):
                    w_qkv[pl.ds(CHUNK * part, CHUNK), pl.ds(D * block + 128 * col, 128)] = stage_f[
                        col, pl.ds(block, CHUNK, stride=3), :
                    ].astype(low)
        if layer == 0:
            begin("qkv", 1)
            put_away("qkv").start()

        def project(count, carry, layer=layer, base=base):
            block, col = count // 3, count % 3
            value = dot_wide(x_low[layer], w_qkv[:, cols(count)])
            row = jnp.where(block == 2, base + 1, base)
            bias = jnp.where(block == 1, 0.0, small_part(row, col))
            qkv[layer, block, :, cols(col)] = (value + bias).astype(low)
            return carry

        lax.fori_loop(0, 9, project, 0, unroll=9)
        if layer:
            put_away("probs").wait()

        def attend(pair, carry, layer=layer):
            lanes = pl.ds(pl.multiple_of(pair * 128, 128), 128)
            for seq in range(2):
                rows = pl.ds(seq * SEQ_ROWS, SEQ_ROWS)
                scores = dot_wide(
                    stacked(qkv[layer, 0, rows, lanes]), qkv[layer, 1, rows, lanes], LAST
                )
                scores = jnp.where(key_mask[seq, pl.ds(0, 1), :] > 0.5, scores, masked_score)
                grown = jnp.exp2(
                    (scores - jnp.max(scores, -1, keepdims=True)) * (0.125 * math.log2(math.e))
                )
                prob = (grown * (1.0 / jnp.sum(grown, -1, keepdims=True))).astype(low)
                probs[seq, pair] = prob
                total = dot_wide(beside(prob), stacked(qkv[layer, 2, rows, lanes]))
                att[layer, rows, lanes] = total.astype(low)
            return carry

        lax.fori_loop(0, 6, attend, 0, unroll=6)
        ready("out", layer)

        def project_out(col, carry, layer=layer, base=base):
            value = dot_wide(att[layer], w_out[:, :, :, cols(col)].reshape(D, CHUNK))
            mid[layer, :, cols(col)] = x_wide[:, cols(col)] + value + small_part(base + 2, col)
            return carry

        lax.fori_loop(0, 3, project_out, 0, unroll=3)
        if layer == 0:
            begin("out", 1)

        def mid_store(rows, value, layer=layer):
            f_wide[rows, :] = value
            f_low[layer, rows, :] = value.astype(low)

        norm_loop(mid, layer, 2 * layer, base + 3, base + 4, mid_store)
        ready("up", layer)
        if layer:
            put_away("act").wait()
            put_away("slope").wait()

        def widen(count, carry, layer=layer, base=base):
            block, col = count // 3, count % 3
            value = dot_wide(f_low[layer], w_up[block, :, :, cols(col)].reshape(D, CHUNK))
            value = value + small_part(base + 5 + block, col)
            square = value * value
            bent = jnp.tanh(value * (gelu_root + (gelu_root * gelu_cube) * square))
            half = 0.5 + 0.5 * bent
            result = value * half
            act[block, :, cols(col)] = result.astype(low)
            slope[block, :, cols(col)] = (
                half
                + result * (1.0 - half) * (2.0 * gelu_root + (6.0 * gelu_root * gelu_cube) * square)
            ).astype(low)
            return carry

        lax.fori_loop(0, 12, widen, 0, unroll=6)
        if layer == 0:
            begin("up", 1)
        ready("down", layer)

        def narrow(col, carry, layer=layer, base=base):
            value = f_wide[:, cols(col)] + small_part(base + 9, col)
            for block in range(4):
                value = value + dot_wide(
                    act[block], w_down[pl.ds(6 * block, 6), :, :, cols(col)].reshape(D, CHUNK)
                )
            second[layer, :, cols(col)] = value
            return carry

        lax.fori_loop(0, 3, narrow, 0, unroll=3)
        if layer == 0:
            begin("down", 1)
            for name in ("act", "slope", "probs"):
                put_away(name).start()

        def out_store(rows, value, layer=layer):
            if layer + 1 < LAYERS:
                x_wide[rows, :] = value
                x_low[layer + 1, rows, :] = value.astype(low)
            else:
                f_wide[rows, :] = value * row_mask[rows, :][:, :1]

        norm_loop(second, layer, 2 * layer + 1, base + 10, base + 11, out_store)

    take = slot_spots((LEN - CAP_TOK, CAP_TOK), 0)
    spread_out = slot_spots((CAP_TOK, LEN - CAP_TOK), 1)
    for seq in range(2):
        text_rows = pl.ds(seq * SEQ_ROWS, CAP_TOK)
        slot_rows = pl.ds(seq * SEQ_ROWS + CAP_TOK, CAP_TOK)
        hidden_ref[seq, pl.ds(0, CAP_TOK), :] = f_wide[text_rows, :].astype(low)
        hidden_ref[seq, pl.ds(CAP_TOK, LEN - CAP_TOK), :] = dot_wide(
            take, f_wide[slot_rows, :].astype(low)
        ).astype(low)
        x_wide[text_rows, :] = cot_ref[seq, pl.ds(0, CAP_TOK), :].astype(wide)
        x_wide[slot_rows, :] = (
            dot_wide(spread_out, cot_ref[seq, pl.ds(CAP_TOK, LEN - CAP_TOK), :])
            * row_mask[slot_rows, :][:, :1]
        )

    small_grad_ref[...] = jnp.zeros_like(small_grad_ref)
    counts, slots = {"p": 0, "q": 0}, {"p": 9, "q": 4}

    def panels_out(stage, index, target, sems):
        return [
            pltpu.make_async_copy(
                stage.at[index + (panel(third),)], target(third), sems.at[third]
            )
            for third in range(3)
        ]

    def stage_copies(kind, slot, target):
        if kind == "p":
            return panels_out(
                raw, (pl.ds(2 * slot, 2), slice(None), slice(None)), target, p_sems.at[slot]
            )
        return panels_out(stage_q, (slot, slice(None), slice(None)), target, q_sems.at[slot])

    def send(kind, count, value, target):
        slot = count % slots[kind]
        copies = stage_copies(kind, slot, target)

        for copy in copies:
            copy.wait()
        if kind == "p":
            raw[pl.ds(2 * slot, 2)] = value.astype(low).reshape(2, 4, 32, D)
        else:
            stage_q[slot] = value.astype(low).reshape(8, 32, D)
        for copy in copies:
            copy.start()

    back_copies, text_copies = [], []

    def send_slots():
        def embed_back(rows, value):
            x_wide[rows, :] = value

        sums = norm_back_loop(embed, None, None, 0, lambda rows: x_wide[rows, :], embed_back)
        small_grad_ref[pl.ds(0, 1), :] = sums[0]
        small_grad_ref[pl.ds(1, 1), :] = sums[1]
        for seq in range(2):
            text_copies.append(
                pltpu.make_async_copy(
                    x_wide.at[pl.ds(seq * SEQ_ROWS, CAP_TOK)], text_ref.at[seq], text_sems.at[seq]
                )
            )
            text_copies[seq].start()
            slots_out[seq] = (
                x_wide[pl.ds(seq * SEQ_ROWS + CAP_TOK, CAP_TOK), :].astype(low).reshape(4, 32, D)
            )
        pl.semaphore_wait(barrier, 3)
        for step in (2, 1, 3):
            copy = pltpu.make_async_remote_copy(
                src_ref=slots_out.at[:, (here[2] + step) % 4],
                dst_ref=back.at[here[2]],
                send_sem=back_send.at[step],
                recv_sem=back_recv.at[step],
                device_id=moved(here, 2, step),
                device_id_type=MESH,
            )
            copy.start()
            back_copies.append(copy)
        back[here[2]] = slots_out[:, here[2]]

    def all_stages():
        copies = []
        for slot in range(slots["p"]):
            copies += stage_copies(
                "p", slot, lambda third: grad_ref.at[third, pl.ds(GRAN_DOWN[1] + 2 * slot, 2)]
            )
        for slot in range(slots["q"]):
            copies += stage_copies(
                "q",
                slot,
                lambda third: grad_ref.at[third, pl.ds(GRAN_UP[1] + 8 * (slot % 3), 8), slot // 3],
            )
        return copies + panels_out(
            stage_r,
            (slice(None), slice(None), slice(None)),
            lambda third: grad_ref.at[third, pl.ds(GRAN_QKV[1], 6)],
            r_sems,
        )

    for stage in (stage_q, stage_r):
        stage[...] = jnp.zeros_like(stage)
    for copy in all_stages():
        copy.start()

    for layer in reversed(range(LAYERS)):
        base = 7 + 12 * layer
        top = layer == LAYERS - 1

        def d_out(rows):
            return x_wide[rows, :]

        def second_back(rows, value):
            f_wide[rows, :] = value
            d_low[rows, :] = value.astype(low)

        sums = norm_back_loop(second, layer, 2 * layer + 1, base + 10, d_out, second_back)
        for row, value in zip((10, 11, 9), sums):
            small_grad_ref[pl.ds(base + row, 1), :] = value
        if not top:
            ready("down", 0)
            take_back("act").wait()
            take_back("slope").wait()
        p_first = counts["p"]

        def down_back(count, carry, layer=layer, base=base, p_first=p_first):
            block, col = count // 3, count % 3
            grad = dot_wide(act[block, :, cols(col)], d_low[...], FIRST)
            send(
                "p",
                p_first + count,
                grad,
                lambda third: grad_ref.at[third, pl.ds(GRAN_DOWN[layer] + 2 * count, 2)],
            )
            value = dot_wide(d_low[...], w_down[pl.ds(2 * count, 2)].reshape(CHUNK, D), LAST)
            rounded = (value * slope[block, :, cols(col)].astype(wide)).astype(low)
            slope[block, :, cols(col)] = rounded
            small_grad_ref[pl.ds(base + 5 + block, 1), cols(col)] = jnp.sum(
                rounded.astype(wide), axis=0, keepdims=True
            )
            return carry

        lax.fori_loop(0, 12, down_back, 0, unroll=6)
        counts["p"] += 12
        if top:
            begin("down", 0)
            take_back("act").start()
        else:
            ready("up", 0)
        turned[...] = f_low[layer].T
        q_first = counts["q"]

        def up_back(count, carry, layer=layer, q_first=q_first):
            block, part = count // 3, count % 3
            left = turned[pl.ds(pl.multiple_of(part * CHUNK, CHUNK), CHUNK), :]
            grad = dot_wide(left, slope[block])
            send(
                "q",
                q_first + count,
                grad,
                lambda third: grad_ref.at[third, pl.ds(GRAN_UP[layer] + 8 * part, 8), block],
            )
            return carry

        lax.fori_loop(0, 12, up_back, 0, unroll=6)
        counts["q"] += 12

        def first_back(part, carry):
            value = f_wide[:, cols(part)]
            for block in range(4):
                value = value + dot_wide(
                    slope[block], w_up[block, pl.ds(8 * part, 8)].reshape(CHUNK, D), LAST
                )
            f_wide[:, cols(part)] = value
            return carry

        lax.fori_loop(0, 3, first_back, 0, unroll=3)
        if top:
            begin("up", 0)
            take_back("slope").start()

        def mid_back(rows, value):
            x_wide[rows, :] = value
            d_low[rows, :] = value.astype(low)

        sums = norm_back_loop(
            mid, layer, 2 * layer, base + 3, lambda rows: f_wide[rows, :], mid_back
        )
        for row, value in zip((3, 4, 2), sums):
            small_grad_ref[pl.ds(base + row, 1), :] = value
        turned[...] = att[layer].T
        p_first = counts["p"]
        if not top:
            ready("out", 0)

        def out_back(part, carry, layer=layer, p_first=p_first):
            left = turned[pl.ds(pl.multiple_of(part * CHUNK, CHUNK), CHUNK), :]
            grad = dot_wide(left, d_low[...])
            send(
                "p",
                p_first + part,
                grad,
                lambda third: grad_ref.at[third, pl.ds(GRAN_OUT[layer] + 2 * part, 2)],
            )
            value = dot_wide(d_low[...], w_out[pl.ds(2 * part, 2)].reshape(CHUNK, D), LAST)
            att[layer, :, cols(part)] = value.astype(low)
            return carry

        lax.fori_loop(0, 3, out_back, 0, unroll=3)
        counts["p"] += 3
        if top:
            begin("out", 0)
        else:
            take_back("probs").wait()

        def attend_back(pair, carry, layer=layer):
            lanes = pl.ds(pl.multiple_of(pair * 128, 128), 128)
            for seq in range(2):
                rows = pl.ds(seq * SEQ_ROWS, SEQ_ROWS)
                query = stacked(qkv[layer, 0, rows, lanes])
                key_rows = stacked(qkv[layer, 1, rows, lanes])
                value_rows = qkv[layer, 2, rows, lanes]
                grad = stacked(att[layer, rows, lanes])
                prob = probs[seq, pair]
                d_value = dot_wide(prob, grad, FIRST)
                d_prob = dot_wide(grad, value_rows, LAST)
                prob = prob.astype(wide)
                product = d_prob * prob
                d_score = (product - prob * jnp.sum(product, -1, keepdims=True)).astype(low)
                d_query = dot_wide(beside(d_score), key_rows)
                d_key = dot_wide(d_score, query, FIRST)
                qkv[layer, 0, rows, lanes] = (d_query * 0.125).astype(low)
                qkv[layer, 1, rows, lanes] = (d_key * 0.125).astype(low)
                qkv[layer, 2, rows, lanes] = d_value.astype(low)
            return carry

        lax.fori_loop(0, 6, attend_back, 0, unroll=6)
        if top:
            take_back("probs").start()
        if not top:
            take_back("qkv").wait()

        def in_back(part, carry, layer=layer):
            value = x_wide[:, cols(part)]
            for block in range(3):
                value = value + dot_wide(
                    qkv[layer, block],
                    w_qkv[pl.ds(pl.multiple_of(part * CHUNK, CHUNK), CHUNK), pl.ds(D * block, D)],
                    LAST,
                )
            x_wide[:, cols(part)] = value
            return carry

        lax.fori_loop(0, 3, in_back, 0, unroll=3)
        if top:
            take_back("qkv").start()
        else:
            send_slots()
        for block, row in ((0, 0), (2, 1)):

            def column_sum(step, carry, block=block, layer=layer):
                rows = pl.ds(pl.multiple_of(step * 64, 64), 64)
                value = qkv[layer, block, rows, :].astype(wide)
                return carry + jnp.sum(value.reshape(8, 8, D), axis=0)

            value = lax.fori_loop(0, ROWS // 64, column_sum, jnp.zeros((8, D), wide))
            small_grad_ref[pl.ds(base + row, 1), :] = jnp.sum(value, axis=0, keepdims=True)
        turned[...] = x_low[layer].T

        def qkv_back(part, carry, layer=layer):
            left = turned[pl.ds(pl.multiple_of(part * CHUNK, CHUNK), CHUNK), :]
            for block in range(3):
                grad = dot_wide(left, qkv[layer, block])
                for col in range(6):
                    stage_f[col, pl.ds(block, CHUNK, stride=3), :] = grad[
                        :, 128 * col : 128 * col + 128
                    ]
            copies = panels_out(
                stage_r,
                (slice(None), slice(None), slice(None)),
                lambda third: grad_ref.at[third, pl.ds(GRAN_QKV[layer] + 6 * part, 6)],
                r_sems,
            )
            for copy in copies:
                copy.wait()
            for col in range(6):
                stage_r[:, :, :, pl.ds(128 * col, 128)] = (
                    stage_f[col].astype(low).reshape(6, 4, 32, 128)
                )
            for copy in copies:
                copy.start()
            return carry

        lax.fori_loop(0, 3, qkv_back, 0)

    dest_row = dest_row_ref[...]
    dest_col = jnp.broadcast_to(dest_row, (128, 128)).T
    earlier = lax.broadcasted_iota(jnp.int32, (128, 128), 1) < lax.broadcasted_iota(
        jnp.int32, (128, 128), 0
    )
    rank = jnp.sum(
        jnp.where(earlier & (dest_col == dest_row), 1.0, 0.0), axis=1, keepdims=True
    ).astype(jnp.int32)
    spots = lax.broadcasted_iota(jnp.int32, (128, 256), 1)
    chosen = jnp.where(spots == rank + 32 * dest_col[:, :1], 1.0, 0.0).astype(low)
    for copy in back_copies:
        copy.wait_recv()
    d_region = dot_wide(chosen, back[...].reshape(256, D)).astype(low)
    region_ref[...] = d_region
    for part in range(8):
        grad = dot_wide(feat_ref[:, pl.ds(CHUNK * part, CHUNK)], d_region, FIRST)
        send(
            "p",
            counts["p"] + part,
            grad,
            lambda third, part=part: grad_ref.at[third, pl.ds(2 * part, 2)],
        )
    d_wide = d_region.astype(wide)
    small_grad_ref[pl.ds(2, 1), :] = jnp.sum(d_wide, axis=0, keepdims=True)
    small_grad_ref[pl.ds(3, 4), :] = jnp.dot(
        box_ref[...], d_wide, precision=highest_exactness, preferred_element_type=wide
    )
    for copy in back_copies:
        copy.wait_send()
    for copy in text_copies:
        copy.wait()
    for copy in all_stages():
        copy.wait()


def both_layers(
    text_in, slots, valid, cotangent, small_rows, region_feats, boxes, region_dest, weight_rows
):
    low, wide = jnp.bfloat16, jnp.float32
    dma = pltpu.SemaphoreType.DMA
    whole = pl.BlockSpec(memory_space=pltpu.VMEM)
    remote = pl.BlockSpec(memory_space=pl.ANY)
    made = pl.pallas_call(
        layers_kernel,
        out_shape=(
            jax.ShapeDtypeStruct((2, LEN, D), low),
            jax.ShapeDtypeStruct((2, CAP_TOK, D), wide),
            jax.ShapeDtypeStruct((128, D), low),
            jax.ShapeDtypeStruct((32, D), wide),
            jax.ShapeDtypeStruct((3, GRANS, 4, 32, THIRD), low),
            jax.ShapeDtypeStruct((4, ROWS, D), low),
            jax.ShapeDtypeStruct((4, ROWS, D), low),
            jax.ShapeDtypeStruct((2, 6, 2 * SEQ_ROWS, SEQ_ROWS), low),
            jax.ShapeDtypeStruct((D, 3 * D), low),
        ),
        in_specs=[whole] * 8 + [remote],
        out_specs=(whole, remote, whole, whole) + (remote,) * 5,
        scratch_shapes=[
            pltpu.VMEM((ROWS, D), low),
            pltpu.VMEM((ROWS, 128), wide),
            pltpu.VMEM((2, 8, SEQ_ROWS), wide),
            pltpu.VMEM((2 * LAYERS, ROWS, 128), wide),
            pltpu.VMEM((ROWS, D), wide),
            pltpu.VMEM((ROWS, D), wide),
            pltpu.VMEM((LAYERS, ROWS, D), low),
            pltpu.VMEM((LAYERS, 3, ROWS, D), low),
            pltpu.VMEM((LAYERS, ROWS, D), low),
            pltpu.VMEM((LAYERS, ROWS, D), wide),
            pltpu.VMEM((LAYERS, ROWS, D), low),
            pltpu.VMEM((LAYERS, ROWS, D), wide),
            pltpu.VMEM((4, ROWS, D), low),
            pltpu.VMEM((4, ROWS, D), low),
            pltpu.VMEM((2, 6, 2 * SEQ_ROWS, SEQ_ROWS), low),
            pltpu.VMEM((ROWS, D), low),
            pltpu.VMEM((D, ROWS), low),
            pltpu.VMEM((D, 3 * D), low),
            pltpu.VMEM((6, 4, 32, D), low),
            pltpu.VMEM((4, 24, 32, D), low),
            pltpu.VMEM((24, 4, 32, D), low),
            pltpu.VMEM((18, 4, 32, D), low),
            pltpu.VMEM((6, D, 128), wide),
            pltpu.VMEM((4, 8, 32, D), low),
            pltpu.VMEM((6, 4, 32, D), low),
            dma((7, 3)),
            dma((8,)),
            dma((9, 3)),
            dma((4, 3)),
            dma((3,)),
            pltpu.VMEM((2, 4, 32, D), low),
            pltpu.VMEM((4, 2, 32, D), low),
            dma((4,)),
            dma((4,)),
            dma((2,)),
            pltpu.VMEM((32, D), wide),
        ],
        compiler_params=pltpu.CompilerParams(
            collective_id=2, has_side_effects=True, vmem_limit_bytes=62 * 1024 * 1024
        ),
    )(
        text_in,
        slots.reshape(2, CAP_TOK, D),
        valid.reshape(2, CAP_TOK, 128),
        cotangent,
        small_rows,
        region_feats,
        boxes,
        region_dest.reshape(1, -1),
        weight_rows.reshape(3, GRANS, 4, 32, THIRD),
    )
    return made[:5]


def in_plane(here, number, step):
    if number == 0:
        pos = (2 * here[2] + here[3] + step) % 8
        return device_at(here[0], here[1], pos // 2, pos % 2)
    pos = (4 * here[0] + here[1] + step) % 16
    return device_at(pos // 4, pos % 4, here[2], here[3])


def greet_planes(here):
    barrier = pltpu.get_barrier_semaphore()
    for number, count in ((0, 8), (1, 16)):
        for step in range(1, count):
            pl.semaphore_signal(
                barrier, inc=1, device_id=in_plane(here, number, step), device_id_type=MESH
            )
    pl.semaphore_wait(barrier, 22)


class Total:
    def __init__(self, here, slots, send_sems, recv_sems):
        self.here, self.slots, self.sems = here, slots, (send_sems, recv_sems)
        self.copies = {}

    def send(self, level, value=None):
        axis = (2, 1, 0, 3)[level]
        slots, own = self.slots[level], self.here[axis]
        if value is not None:
            slots[own] = value.astype(slots.dtype)
        for step in range(1, 2 if axis == 3 else 4):
            copy = pltpu.make_async_remote_copy(
                src_ref=slots.at[own],
                dst_ref=slots.at[own],
                send_sem=self.sems[0].at[level, step],
                recv_sem=self.sems[1].at[level, step],
                device_id=moved(self.here, axis, step),
                device_id_type=MESH,
            )
            copy.start()
            self.copies[level, step] = copy

    def take(self, level):
        count = 2 if level == 3 else 4
        for step in range(1, count):
            self.copies[level, step].wait_recv()
        value = self.slots[level][0].astype(jnp.float32)
        for pos in range(1, count):
            value = value + self.slots[level][pos].astype(jnp.float32)
        return value

    def end(self):
        for copy in self.copies.values():
            copy.wait_send()


def reduce_kernel(
    grad_ref,
    small_ref,
    region_ref,
    full_ref,
    shard_ref,
    total_ref,
    square_ref,
    feat_grad_ref,
    acc,
    sibling,
    chain_one,
    fin_one,
    chain_two,
    fin_two,
    fin_three,
    shares,
    region,
    flat,
    small_a,
    small_b,
    small_c,
    small_d,
    tile_a,
    tile_b,
    load_sems,
    core_send,
    core_recv,
    chain_send,
    chain_recv,
    fin_send,
    fin_recv,
    last_send,
    last_recv,
    share_send,
    share_recv,
    small_send,
    small_recv,
    tile_send,
    tile_recv,
    region_sem,
):
    low, wide = jnp.bfloat16, jnp.float32
    here = place()
    greet_planes(here)
    core = here[3]

    chains, fins = (chain_one, chain_two), (fin_one, fin_two)
    first_half, second_half, both = pl.ds(0, HALF), pl.ds(HALF, HALF), pl.ds(0, PIECE)
    halves = (first_half, second_half)

    def at_step(part, level, step):
        return (here[AXIS_ORDER[part][level]] + step) % 4

    def fixed(part, level, step, sub=None):
        index = [None] * 3
        for before in range(level):
            index[AXIS_ORDER[part][before]] = here[AXIS_ORDER[part][before]]
        index[AXIS_ORDER[part][level]] = at_step(part, level, step)
        if sub is not None:
            index[AXIS_ORDER[part][level + 1]] = at_step(part, level + 1, sub)
        return index

    def block(buffer, part, level, step, rows, sub=None):
        index = [slice(None) if value is None else value for value in fixed(part, level, step, sub)]
        return buffer.at[(part,) + tuple(index) + (rows, slice(None))]

    def grad_block(part, step, sub, which):
        index = [slice(None) if value is None else value for value in fixed(part, 0, step, sub)]
        index.insert(2, which)
        return grad_ref.at[(part,) + tuple(index) + (slice(None), slice(None))]

    order = (2, 1, 3, 0)
    loads, core_copies = {}, {}
    for sub in order:
        for step in order:
            for part in range(3):
                core_copies[part, step, sub] = pltpu.make_async_remote_copy(
                    src_ref=grad_block(part, step, sub, 1 - core),
                    dst_ref=block(sibling, part, 0, step, both, sub),
                    send_sem=core_send.at[part, step, sub],
                    recv_sem=core_recv.at[part, step, sub],
                    device_id=moved(here, 3, 1),
                    device_id_type=MESH,
                )
                loads[part, step, sub] = pltpu.make_async_copy(
                    grad_block(part, step, sub, core),
                    block(acc, part, 0, step, both, sub),
                    load_sems.at[part, step, sub],
                )

    def issue(sub):
        for step in order:
            for part in range(3):
                core_copies[part, step, sub].start()
                loads[part, step, sub].start()

    small = Total(here, (small_a, small_b, small_c, small_d), small_send, small_recv)
    small.send(0, small_ref[...])
    issue(2)

    def add_blocks(part, level, step, rows, terms, sub=None):
        index = fixed(part, level, step, sub)
        free = [axis for axis in range(3) if index[axis] is None]

        def one(count, carry):
            spot = list(index)
            if free:
                spot[free[0]] = count
            inner = (count,) if free else ()
            where = (part,) + tuple(spot) + (rows, slice(None))
            if len(terms) == 1:
                acc[where] = acc[where] + terms[0](tuple(spot), inner, rows)
                return carry
            value = acc[where].astype(wide)
            for term in terms:
                value = value + term(tuple(spot), inner, rows).astype(wide)
            acc[where] = value.astype(low)
            return carry

        if free:
            lax.fori_loop(0, 4, one, 0)
        else:
            one(0, 0)

    chain_copies, fin_copies, last_copies = {}, {}, {}

    def slot_of(level, part, way, sub):
        return (part, way) if sub is None else (part, way, sub)

    def send_chain(part, level, sub=None):
        for way in (0, 1):
            number = 0 if sub is None else sub
            copy = pltpu.make_async_remote_copy(
                src_ref=block(acc, part, level, 2, halves[way], sub),
                dst_ref=chains[level].at[slot_of(level, part, way, sub)],
                send_sem=chain_send.at[level, part, way, number],
                recv_sem=chain_recv.at[level, part, way, number],
                device_id=moved(here, AXIS_ORDER[part][level], (1, 3)[way]),
                device_id_type=MESH,
            )
            copy.start()
            chain_copies[part, level, way, sub] = copy

    def send_fin(part, level, way, half, sub=None):
        number = 0 if sub is None else sub
        count = 1 if sub is not None else 2 - level
        index = slot_of(level, part, way, sub) + (slice(None),) * count + (halves[half], slice(None))
        copy = pltpu.make_async_remote_copy(
            src_ref=block(acc, part, level, (1, 3)[way], halves[half], sub),
            dst_ref=fins[level].at[index],
            send_sem=fin_send.at[level, part, way, half, number],
            recv_sem=fin_recv.at[level, part, way, half, number],
            device_id=moved(here, AXIS_ORDER[part][level], (1, 3)[way]),
            device_id_type=MESH,
        )
        copy.start()
        fin_copies[part, level, way, half, sub] = copy

    def sibling_term(part):
        return lambda spot, inner, rows: sibling[(part,) + spot + (rows, slice(None))]

    def relay(part, level, sub=None):
        for way in (0, 1):
            chain_copies[part, level, way, sub].wait_recv()
            slot = slot_of(level, part, way, sub)
            terms = [lambda spot, inner, rows, slot=slot: chains[level][slot + inner]]
            if level == 0:
                terms.append(sibling_term(part))
            add_blocks(part, level, (1, 3)[way], halves[way], terms, sub)
            send_fin(part, level, way, way, sub)

    def finish(part, level, sub=None):
        for way in (0, 1):
            for half in (0, 1):
                fin_copies[part, level, way, half, sub].wait_recv()
        slots = [slot_of(level, part, way, sub) for way in (0, 1)]
        terms = [lambda spot, inner, rows, slot=slot: fins[level][slot + inner] for slot in slots]
        if level == 0:
            terms.append(sibling_term(part))
        add_blocks(part, level, 0, both, terms, sub)

    def gather_pair(part, step, sub, rows=None):
        loads[part, step, sub].wait()
        core_copies[part, step, sub].wait_recv()
        if rows is not None:
            add_blocks(part, 0, step, rows, [sibling_term(part)], sub)

    def second_phase(part, sub):
        finish(part, 0, sub)
        if sub == 2:
            send_chain(part, 1)
        elif sub == 1:
            send_fin(part, 1, 0, 1)
        elif sub == 3:
            send_fin(part, 1, 1, 0)

    for count, sub in enumerate(order):
        for part in range(3):
            gather_pair(part, 2, sub, both)
            send_chain(part, 0, sub)
        if count == 0:
            issue(1)
            loaded = region_loads(full_ref, region, region_sem)
            for copy in loaded:
                copy.start()
        for step, way in ((1, 0), (3, 1)):
            for part in range(3):
                gather_pair(part, step, sub, halves[1 - way])
                send_fin(part, 0, way, 1 - way, sub)
        if count < 2:
            issue(order[count + 2])
        for part in range(3):
            gather_pair(part, 0, sub)
        for part in range(3):
            relay(part, 0, sub)
        if count:
            for part in range(3):
                second_phase(part, order[count - 1])
        if count < 3:
            small.send(count + 1, small.take(count))
        if count == 2:
            for copy in loaded:
                copy.wait()
            matrix = region[...].reshape(16 * PIECE, D)[:FEAT]
            feat_grad_ref[...] = dot_wide(region_ref[...], matrix, LAST)
    summed = small.take(3)
    for col in range(6):
        total_ref[pl.ds(col, 31, stride=6), :] = summed[:31, 128 * col : 128 * col + 128]
    for part in range(3):
        relay(part, 1)
    for part in range(3):
        second_phase(part, 0)
    for part in range(3):
        finish(part, 1)
        for step in (2, 1, 3):
            copy = pltpu.make_async_remote_copy(
                src_ref=block(acc, part, 2, step, both),
                dst_ref=fin_three.at[part, step],
                send_sem=last_send.at[part, step],
                recv_sem=last_recv.at[part, step],
                device_id=moved(here, AXIS_ORDER[part][2], step),
                device_id_type=MESH,
            )
            copy.start()
            last_copies[part, step] = copy
    for part in range(3):
        for step in (1, 3, 2):
            last_copies[part, step].wait_recv()
        add_blocks(
            part,
            2,
            0,
            both,
            [
                lambda spot, inner, rows, step=step: fin_three[part, step, rows, :]
                for step in (1, 2, 3)
            ],
        )

    square = jnp.zeros((8, 128), wide)
    for part in range(3):
        own = acc[part, here[0], here[1], here[2]]
        shares[here[2], part] = own
        value = own.astype(wide)
        value = value * value
        value = value.reshape(PIECE // 8, 8, THIRD)
        square = square + jnp.sum(value[:, :, :128] + value[:, :, 128:], axis=0)
    def share(number, step, rows, way):
        where = shares.at[(here[2] + step) % 4, :, rows]
        return pltpu.make_async_remote_copy(
            src_ref=where,
            dst_ref=where,
            send_sem=share_send.at[number],
            recv_sem=share_recv.at[number],
            device_id=moved(here, 2, way),
            device_id_type=MESH,
        )

    share_copies = [share(0, 0, both, 1), share(1, 0, both, 3)]
    for copy in share_copies:
        copy.start()
    tile_copies = [[], []]

    def tile_out(number, value):
        slots, own = ((tile_a, 2 * here[2] + core), (tile_b, 4 * here[0] + here[1]))[number]
        slots[own] = value
        for step in range(1, (8, 16)[number]):
            copy = pltpu.make_async_remote_copy(
                src_ref=slots.at[own],
                dst_ref=slots.at[own],
                send_sem=tile_send.at[number, step],
                recv_sem=tile_recv.at[number, step],
                device_id=in_plane(here, number, step),
                device_id_type=MESH,
            )
            copy.start()
            tile_copies[number].append(copy)

    def tile_in(number):
        for copy in tile_copies[number]:
            copy.wait_recv()
        slots = (tile_a, tile_b)[number]
        value = slots[0]
        for pos in range(1, (8, 16)[number]):
            value = value + slots[pos]
        return value

    tile_out(0, square)
    share(0, 3, both, 1).wait_recv()
    share_copies.append(share(2, 3, first_half, 1))
    share_copies[2].start()
    share(1, 1, both, 3).wait_recv()
    share_copies.append(share(3, 1, second_half, 3))
    share_copies[3].start()
    first = lax.axis_index("dp") * 5

    def spread_out(grans):
        for gran in grans:
            up = is_up(first + gran)

            def put(gran, dense):
                for piece in range(4):
                    quarter, spot = (4 * gran + piece) // 5, (4 * gran + piece) % 5
                    for part in range(3):
                        value = shares[quarter, part, pl.ds(32 * spot, 32), :].astype(wide)
                        for half in range(2):
                            col = 2 * part + half
                            if dense:
                                rows = pl.ds(6 * GRAN * gran + 6 * 32 * piece + col, 32, stride=6)
                            else:
                                rows = pl.ds(6 * GRAN * gran + 6 * piece + col, 32, stride=24)
                            flat[rows, :] = value[:, 128 * half : 128 * half + 128]

            @pl.when(up)
            def _(gran=gran):
                put(gran, False)

            @pl.when(jnp.logical_not(up))
            def _(gran=gran):
                put(gran, True)

    tile_out(1, tile_in(0))
    share(2, 2, first_half, 1).wait_recv()
    share(3, 2, second_half, 3).wait_recv()
    spread_out((0, 1, 2, 3, 4))
    shard_ref[...] = flat[...].astype(low)
    total = jnp.sum(tile_in(1), axis=0, keepdims=True)
    smalls = total_ref[...]
    total = total + jnp.sum(smalls * smalls, axis=0, keepdims=True)
    square_ref[0, 0] = jnp.sum(total)
    for copy in share_copies:
        copy.wait_send()
    small.end()
    for copy in tile_copies[0] + tile_copies[1]:
        copy.wait_send()
    for copies in (core_copies, chain_copies, fin_copies, last_copies):
        for copy in copies.values():
            copy.wait_send()


def reduce_gradients(grad_rows, small_rows, region_low, full_low):
    low, wide = jnp.bfloat16, jnp.float32
    dma = pltpu.SemaphoreType.DMA
    whole = pl.BlockSpec(memory_space=pltpu.VMEM)
    remote = pl.BlockSpec(memory_space=pl.ANY)
    rows_shape = (3, 4, 4, 2, 4, PIECE, THIRD)
    made = pl.pallas_call(
        reduce_kernel,
        out_shape=(
            jax.ShapeDtypeStruct((3840, 128), low),
            jax.ShapeDtypeStruct((186, 128), wide),
            jax.ShapeDtypeStruct((1, 1), wide),
            jax.ShapeDtypeStruct((128, FEAT), wide),
        ),
        in_specs=[remote, whole, whole, remote],
        out_specs=(whole, whole, pl.BlockSpec(memory_space=pltpu.SMEM), whole),
        scratch_shapes=[
            pltpu.VMEM((3, 4, 4, 4, PIECE, THIRD), low),
            pltpu.VMEM((3, 4, 4, 4, PIECE, THIRD), low),
            pltpu.VMEM((3, 2, 4, 4, HALF, THIRD), low),
            pltpu.VMEM((3, 2, 4, 4, PIECE, THIRD), low),
            pltpu.VMEM((3, 2, 4, HALF, THIRD), low),
            pltpu.VMEM((3, 2, 4, PIECE, THIRD), low),
            pltpu.VMEM((3, 4, PIECE, THIRD), low),
            pltpu.VMEM((4, 3, PIECE, THIRD), low),
            pltpu.VMEM((2, 2, 4, PIECE, D), low),
            pltpu.VMEM((3840, 128), wide),
            pltpu.VMEM((4, 32, D), low),
            pltpu.VMEM((4, 32, D), low),
            pltpu.VMEM((4, 32, D), low),
            pltpu.VMEM((2, 32, D), low),
            pltpu.VMEM((8, 8, 128), wide),
            pltpu.VMEM((16, 8, 128), wide),
            dma((3, 4, 4)),
            dma((3, 4, 4)),
            dma((3, 4, 4)),
            dma((2, 3, 2, 4)),
            dma((2, 3, 2, 4)),
            dma((2, 3, 2, 2, 4)),
            dma((2, 3, 2, 2, 4)),
            dma((3, 4)),
            dma((3, 4)),
            dma((4,)),
            dma((4,)),
            dma((4, 4)),
            dma((4, 4)),
            dma((2, 16)),
            dma((2, 16)),
            dma((3,)),
        ],
        compiler_params=pltpu.CompilerParams(
            collective_id=0, has_side_effects=True, vmem_limit_bytes=62 * 1024 * 1024
        ),
    )(grad_rows.reshape(rows_shape), small_rows, region_low, full_low)
    return made


def local(
    text_in,
    cotangent,
    region_feats,
    boxes,
    region_dest,
    weights_mat,
    moment1_mat,
    moment2_mat,
    weights_small,
    moment1_small,
    moment2_small,
):
    small_in = weights_small.reshape(-1, 128)
    full_low, slots, slot_valid = gather_matrices(
        weights_mat, region_feats, boxes, region_dest, small_in
    )
    hidden_out, text_grad, region_low, small_part, mat_part = both_layers(
        text_in,
        slots,
        slot_valid,
        cotangent,
        small_in,
        region_feats,
        boxes,
        region_dest,
        full_low,
    )
    shard_rows, small_sum, squares, feat_grad = reduce_gradients(
        mat_part, small_part, region_low, full_low
    )
    shard_grad = shard_rows.reshape(-1).astype(jnp.float32)
    small_total = small_sum.reshape(-1)
    grad_norm = jnp.sqrt(squares[0, 0])
    clip_factor = clip_norm / jnp.maximum(grad_norm, clip_norm)
    new_m_mat, new_v_mat, new_w_mat = adam_update(
        weights_mat, moment1_mat, moment2_mat, shard_grad * clip_factor, mat_rate
    )
    new_m_small, new_v_small, new_w_small = adam_update(
        weights_small, moment1_small, moment2_small, small_total * clip_factor, small_rate
    )
    return (
        hidden_out,
        text_grad,
        feat_grad,
        grad_norm,
        shard_grad,
        small_total,
        new_m_mat,
        new_v_mat,
        new_w_mat,
        new_w_mat.astype(jnp.bfloat16),
        new_m_small,
        new_v_small,
        new_w_small,
    )


def solution(mesh):
    return jax.shard_map(
        local,
        mesh=mesh,
        in_specs=(
            P(("dp", "enc"), None, None),
            P(("dp", "enc"), None, None),
            P(("dp", "enc"), None),
            P(None, ("dp", "enc")),
            P(("dp", "enc"), None),
            P("dp"),
            P("dp"),
            P("dp"),
            P(),
            P(),
            P(),
        ),
        out_specs=(
            P(("dp", "enc"), None, None),
            P(("dp", "enc"), None, None),
            P(("dp", "enc"), None),
            P(),
            P("dp"),
            P(),
            P("dp"),
            P("dp"),
            P("dp"),
            P("dp"),
            P(),
            P(),
            P(),
        ),
        check_vma=False,
    )
```
